32 devices in a mesh: site: 4 (over y, core), blk: 8 (over z, x).
Axes of the slice: x: 2, y: 2, z: 4, core: 2. Of those that a mesh axis runs over, the one named last changes fastest.
Arguments:
- corner: bfloat16 [4, 48, 128, 128], P('site', 'blk')
- bcorner: bfloat16 [2, 4, 48, 128, 128], P(None, 'site', 'blk'), may hold values from -6 to 6
- edge: bfloat16 [4, 48, 128, 2304], P('site', 'blk'), may hold values from -0.5 to 0.5
- bedge: bfloat16 [4, 48, 128, 2304], P('site', 'blk'), may hold values from -0.5 to 0.5
- proj: bfloat16 [4, 48, 2304, 128], P('site', 'blk'), may hold values from -0.125 to 0.125
- joining: int32 [4, 48], P('site'), may hold values from 0 to 47, as said below
- momentum: float32 [1], replicated, may hold values from 0.5 to 2.5
Outputs:
- new_corner: bfloat16 [4, 48, 128, 128], P('site', 'blk')
- new_bcorner: bfloat16 [2, 4, 48, 128, 128], P(None, 'site', 'blk')
- momentum_sum: float32 [2, 48, 128, 128], P(None, 'blk', 'site')
The draws below stay inside these ranges and needn't reach their ends.
Inputs may be any that keep to these rules, and one draw needn't show every extreme that they name: Each row of joining is a permutation of the 48 slots. The 6 new slots of one blk device take their blocks from the slots of at most 3 blk devices, exactly 2 from each of them.
All inputs are finite; a program needn't handle non-finite values. Where the reference program divides by a largest or mean magnitude, that divisor is 1e-20 or more.
Results may differ from the reference program's by a relative error of at most 0.024.
Values may be sent and summed in bfloat16 or wider, within the bound.
No kernel may reach another device: no remote copies, remote signals or barrier semaphores. Data moves between devices by JAX's collectives and lax.ppermute only.
A program may use at most 128 MiB of HBM per device.

```python
import jax
import jax.numpy as jnp
from jax import lax

M = 128
K = 2304
CAP = 2
NB_DEV = 6
SITES = 4
SLOTS = 48


def draw_corner(key, part):
    key_base, key_rows, key_cols = jax.random.split(jax.random.fold_in(key, 11), 3)
    base = jax.random.normal(key_base, (SITES, SLOTS, M, M), jnp.float32)
    rows = jnp.exp((jax.random.uniform(key_rows, (SITES, SLOTS, M, 1), jnp.float32) - 0.5) * jnp.log(10.0))
    cols = jnp.exp((jax.random.uniform(key_cols, (SITES, SLOTS, 1, M), jnp.float32) - 0.5) * jnp.log(10.0))
    slot_scale = 1.0 + 2.0 * jnp.arange(SLOTS, dtype=jnp.float32) / max(SLOTS - 1, 1)
    return (base * rows * cols * slot_scale[None, :, None, None]).astype(jnp.bfloat16)


def joining_site(key):
    groups = NB_DEV // CAP
    blocks = SLOTS // NB_DEV
    key_off, key_src, key_dst = jax.random.split(key, 3)
    offsets = jax.random.permutation(key_off, blocks)[:groups]
    shuffle_src = jax.vmap(lambda subkey: jax.random.permutation(subkey, NB_DEV))(jax.random.split(key_src, blocks))
    shuffle_dst = jax.vmap(lambda subkey: jax.random.permutation(subkey, NB_DEV))(jax.random.split(key_dst, blocks))
    targets = jnp.arange(blocks, dtype=jnp.int32)[:, None]
    positions = jnp.arange(NB_DEV, dtype=jnp.int32)[None, :]
    group_of = positions // CAP
    within = positions % CAP
    source_device = (targets + offsets[group_of]) % blocks
    source_slot = shuffle_src[source_device, group_of * CAP + within]
    sources = source_device * NB_DEV + source_slot
    shuffled = jnp.take_along_axis(sources, shuffle_dst, axis=1)
    return shuffled.reshape(SLOTS).astype(jnp.int32)


def draw_joining(key, part):
    keys = jax.random.split(jax.random.fold_in(key, 23), SITES)
    return jax.vmap(joining_site)(keys)


def level_of(stream_key, extent, cuts, low, top_value):
    factor_of = 1.0
    for dim, shards_of in cuts:
        steps = jax.random.uniform(jax.random.fold_in(jax.random.fold_in(stream_key, 6), dim), (shards_of,), jnp.float32, low / len(cuts), top_value / len(cuts))
        factor_of = factor_of * jnp.repeat(jnp.exp(steps), extent[dim] // shards_of).reshape((-1,) + (1,) * (len(extent) - 1 - dim))
    return factor_of


def normal_values(own_key, extent, spread, limit, pieces=(), kind=jnp.bfloat16):
    factor_of = level_of(own_key, extent, pieces, -0.22, 0.18) if pieces else 1.0
    array = jax.random.normal(own_key, extent, jnp.float32) * spread * factor_of
    return jnp.minimum(jnp.maximum(array, -limit), limit).astype(kind)


def setup_inputs(seed: int = 0) -> dict:
    seeds = jax.random.split(jax.random.key(seed), 8)
    return {
        "corner": draw_corner(jax.random.fold_in(seeds[7], 71), 0),
        "bcorner": normal_values(seeds[1], (2, SITES, SLOTS, M, M), 1.0, 6.0, ((1, 4), (2, 8))),
        "edge": normal_values(seeds[2], (SITES, SLOTS, M, K), M ** -0.5, 0.5, ((0, 4), (1, 8))),
        "bedge": normal_values(seeds[3], (SITES, SLOTS, M, K), M ** -0.5, 0.5, ((0, 4), (1, 8))),
        "proj": normal_values(seeds[4], (SITES, SLOTS, K, M), K ** -0.5, 0.125, ((0, 4), (1, 8))),
        "joining": draw_joining(jax.random.fold_in(seeds[7], 71), 0),
        "momentum": jnp.clip(jax.random.uniform(seeds[6], (1,), jnp.float32, 0.5, 2.5), 0.5, 2.5),
    }


epsilon = 1e-6


def product(left, right):
    return jnp.einsum("jmn,jnk->jmk", left.astype(jnp.float32), right.astype(jnp.float32), precision=lax.Precision.HIGHEST)


def reference(corner, bcorner, edge, bedge, proj, joining, momentum):
    left_corner = jnp.roll(corner, 1, axis=0)
    left_bcorner = jnp.moveaxis(jnp.roll(bcorner, 1, axis=1), 0, 1)
    sites = jnp.arange(SITES, dtype=jnp.int32)

    def one_site(items):
        corner_here, bcorner_here, column, bcolumn, project, sources, index = items
        enlarged = product(corner_here, column).astype(jnp.bfloat16)
        real_term = product(bcorner_here[0], column)
        imag_term = product(bcorner_here[1], column)
        inserted = product(corner_here, bcolumn)
        angle = momentum[0] * index.astype(jnp.float32)
        cosine = jnp.cos(angle)
        sine = jnp.sin(angle)
        excited_re = (cosine * real_term - sine * imag_term + inserted).astype(jnp.bfloat16)
        excited_im = (sine * real_term + cosine * imag_term).astype(jnp.bfloat16)
        projected = jnp.stack([product(enlarged, project).astype(jnp.bfloat16),
                               product(excited_re, project).astype(jnp.bfloat16),
                               product(excited_im, project).astype(jnp.bfloat16)], axis=1)
        peak = jnp.max(jnp.abs(projected[:, 0].astype(jnp.float32)))
        routed = projected[sources]
        scaled = routed.astype(jnp.float32) / (peak + epsilon)
        new_corner = scaled[:, 0].astype(jnp.bfloat16)
        new_b = jnp.stack([scaled[:, 1], scaled[:, 2]], axis=0).astype(jnp.bfloat16)
        return new_corner, new_b

    corners, bparts = lax.map(one_site, (left_corner, left_bcorner, edge, bedge, proj, joining, sites))
    new_bcorner = jnp.moveaxis(bparts, 0, 1)
    momentum_sum = jnp.sum(new_bcorner.astype(jnp.float32), axis=1)
    return corners, new_bcorner, momentum_sum
```

```python
import jax
import jax.numpy as jnp
from jax import lax
from jax.experimental import pallas as pl
from jax.experimental.pallas import tpu as pltpu
from jax.sharding import PartitionSpec as P

epsilon = 1e-06


def shifted(block, axis, distance):
    devices = range(lax.axis_size(axis))
    route = [((i - distance) % len(devices), i) for i in devices]
    return lax.ppermute(block, axis, route)


def edge_proj_kernel(edge_ref, bedge_ref, proj_ref, w_ref, v_ref):
    project = proj_ref[0, 0]
    w_ref[0] = jnp.dot(edge_ref[0, 0], project, preferred_element_type=jnp.float32).astype(w_ref.dtype)
    v_ref[0] = jnp.dot(bedge_ref[0, 0], project, preferred_element_type=jnp.float32).astype(v_ref.dtype)


def edge_proj(edge, bedge, proj):
    _, slots, m, k = edge.shape
    block = jax.ShapeDtypeStruct((slots, m, m), jnp.bfloat16)
    return pl.pallas_call(
        edge_proj_kernel,
        grid=(slots,),
        out_shape=(block, block),
        in_specs=[
            pl.BlockSpec((1, 1, m, k), lambda i: (0, i, 0, 0)),
            pl.BlockSpec((1, 1, m, k), lambda i: (0, i, 0, 0)),
            pl.BlockSpec((1, 1, k, m), lambda i: (0, i, 0, 0)),
        ],
        out_specs=[pl.BlockSpec((1, m, m), lambda i: (i, 0, 0))] * 2,
        cost_estimate=pl.CostEstimate(
            flops=4 * slots * m * k * m, bytes_accessed=6 * slots * m * k, transcendentals=0
        ),
        compiler_params=pltpu.CompilerParams(vmem_limit_bytes=24 << 20),
        name="edge_proj",
    )(edge, bedge, proj)


def product(left, right):
    return jnp.einsum("jmn,jnk->jmk", left, right, preferred_element_type=jnp.float32)


def per_device(corner, bcorner, edge, bedge, proj, joining, momentum):
    _, per_dev, m, _ = corner.shape
    blks = lax.axis_size("blk")
    sites = lax.axis_size("site")
    rows = m // blks
    my_site = lax.axis_index("site")
    left_corner, left_bcorner = shifted((corner, bcorner), "site", 1)
    w, v = edge_proj(edge, bedge, proj)
    angle = momentum[0] * my_site.astype(jnp.float32)
    cosine = jnp.cos(angle)
    sine = jnp.sin(angle)
    ground = product(left_corner[0], w).astype(jnp.bfloat16)
    real_term = product(left_bcorner[0, 0], w)
    imag_term = product(left_bcorner[1, 0], w)
    inserted = product(left_corner[0], v)
    re = (cosine * real_term - sine * imag_term + inserted).astype(jnp.bfloat16)
    im = (sine * real_term + cosine * imag_term).astype(jnp.bfloat16)
    local_peak = jnp.max(jnp.abs(ground))
    blocks = jnp.stack([ground, re, im], axis=1).reshape(per_dev, 3, blks, rows, m)
    blocks = jnp.moveaxis(blocks, 2, 0).reshape(blks, per_dev * 3 * rows, m)
    payload = jnp.concatenate([blocks, jnp.full((blks, 16, m), local_peak, jnp.bfloat16)], axis=1)
    arrived = lax.all_to_all(payload, "blk", 0, 0, tiled=True)
    peak = jnp.max(arrived[:, -16:].astype(jnp.float32))
    pieces = arrived[:, :-16].reshape(blks * per_dev, 3, rows, m)
    routed = pieces[joining[0]].astype(jnp.float32) / (peak + epsilon)
    scaled = routed.astype(jnp.bfloat16).reshape(blks, per_dev, 3, rows, m)
    final = lax.all_to_all(scaled, "blk", 0, 0, tiled=True)
    new = jnp.transpose(final, (2, 1, 0, 3, 4)).reshape(3, per_dev, m, m)
    terms = lax.all_to_all(final[:, :, 1:], "site", 0, 0, tiled=True)
    summed = jnp.sum(terms.reshape(sites, blks // sites, per_dev, 2, rows, m).astype(jnp.float32), axis=0)
    summed = jnp.transpose(summed, (2, 1, 0, 3, 4)).reshape(2, per_dev, m // sites, m)
    return (new[0][None], new[1:][:, None], summed)


def solution(mesh):
    in_specs = (
        P("site", "blk", None, None),
        P(None, "site", "blk", None, None),
        P("site", "blk", None, None),
        P("site", "blk", None, None),
        P("site", "blk", None, None),
        P("site", None),
        P(),
    )
    out_specs = (
        P("site", "blk", None, None),
        P(None, "site", "blk", None, None),
        P(None, "blk", "site", None),
    )
    return jax.shard_map(
        per_device, mesh=mesh, in_specs=in_specs, out_specs=out_specs, check_vma=False
    )
```

```python
import functools

import jax
import jax.numpy as jnp
from jax import lax
from jax.experimental import pallas as pl
from jax.experimental.pallas import tpu as pltpu
from jax.sharding import PartitionSpec as P

epsilon = 1e-06
TILE = 16
VMEM = pl.BlockSpec(memory_space=pltpu.VMEM)
SMEM = pl.BlockSpec(memory_space=pltpu.SMEM)


def shifted(block, axis, distance):
    n = lax.axis_size(axis)
    return lax.ppermute(block, axis, [((i - distance) % n, i) for i in range(n)])


def exchanged(parts, axis):
    return [part if k == 0 else shifted(part, axis, k) for k, part in enumerate(parts)]


def edge_proj_kernel(edge_ref, bedge_ref, proj_ref, w_ref, v_ref):
    project = proj_ref[0, 0]
    w_ref[0] = jnp.dot(edge_ref[0, 0], project, preferred_element_type=jnp.float32).astype(w_ref.dtype)
    v_ref[0] = jnp.dot(bedge_ref[0, 0], project, preferred_element_type=jnp.float32).astype(v_ref.dtype)


def edge_proj(edge, bedge, proj):
    _, slots, m, k = edge.shape
    block = jax.ShapeDtypeStruct((slots, m, m), jnp.bfloat16)
    return pl.pallas_call(
        edge_proj_kernel,
        grid=(slots,),
        out_shape=(block, block),
        in_specs=[
            pl.BlockSpec((1, 1, m, k), lambda i: (0, i, 0, 0)),
            pl.BlockSpec((1, 1, m, k), lambda i: (0, i, 0, 0)),
            pl.BlockSpec((1, 1, k, m), lambda i: (0, i, 0, 0)),
        ],
        out_specs=[pl.BlockSpec((1, m, m), lambda i: (i, 0, 0))] * 2,
        cost_estimate=pl.CostEstimate(
            flops=4 * slots * m * k * m, bytes_accessed=6 * slots * m * k, transcendentals=0
        ),
        compiler_params=pltpu.CompilerParams(vmem_limit_bytes=60 << 20),
        name="edge_proj",
    )(edge, bedge, proj)


def small_call(kernel, out_shape, in_specs, scratch, name):
    return pl.pallas_call(
        kernel,
        out_shape=out_shape,
        in_specs=in_specs,
        out_specs=jax.tree.map(lambda _: VMEM, out_shape),
        scratch_shapes=scratch,
        cost_estimate=pl.CostEstimate(flops=1 << 28, bytes_accessed=1 << 20, transcendentals=0),
        compiler_params=pltpu.CompilerParams(vmem_limit_bytes=24 << 20),
        name=name,
    )


def blocks_of(place, turn, corner, bcorner, w, v):
    cosine, sine = turn
    dot = functools.partial(jnp.dot, preferred_element_type=jnp.float32)
    ground = dot(corner, w).astype(jnp.bfloat16)
    real_term = dot(bcorner[0], w)
    imag_term = dot(bcorner[1], w)
    re = cosine * real_term - sine * imag_term + dot(corner, v)
    im = sine * real_term + cosine * imag_term
    return ground, re.astype(jnp.bfloat16), im.astype(jnp.bfloat16)


def project_kernel(n, here, turn, corner, bcorner, w, v, *refs):
    b_out, g_out, stage = refs[:n], refs[n : 2 * n], refs[2 * n]
    slots, m, _ = w.shape
    rows = m // n
    top = jnp.zeros((m, m), jnp.float32)
    for i in range(slots):
        blocks = blocks_of(here, (turn[0], turn[1]), corner[0, i], (bcorner[0, 0, i], bcorner[1, 0, i]), w[i], v[i])
        for kind in range(3):
            stage[3 * i + kind] = blocks[kind]
        top = jnp.maximum(top, jnp.abs(blocks[0].astype(jnp.float32)))
    peak = jnp.full((TILE, m), jnp.max(top), jnp.float32).astype(jnp.bfloat16)
    for k in range(n):
        first = pl.multiple_of(lax.rem(here[0] + k, n) * rows, rows)
        for i in range(slots):
            g_out[k][i * rows : (i + 1) * rows] = stage[3 * i, pl.ds(first, rows)]
            for c in range(2):
                at = (2 * i + c) * rows
                b_out[k][at : at + rows] = stage[3 * i + 1 + c, pl.ds(first, rows)]
        b_out[k][2 * slots * rows :] = peak


def project(here, turn, corner, bcorner, w, v, n):
    slots, m, _ = w.shape
    rows = m // n
    b_piece = jax.ShapeDtypeStruct((2 * slots * rows + TILE, m), jnp.bfloat16)
    g_piece = jax.ShapeDtypeStruct((slots * rows, m), jnp.bfloat16)
    out = small_call(
        functools.partial(project_kernel, n),
        [b_piece] * n + [g_piece] * n,
        [SMEM, SMEM] + [VMEM] * 4,
        [pltpu.VMEM((3 * slots, m, m), jnp.bfloat16)],
        "project",
    )(here, turn, corner, bcorner, w, v)
    return out[:n], out[n:]


def route_kernel(n, slots, has_peak, here, joining, *refs):
    if has_peak:
        pieces, out, peak_out, held = refs[:n], refs[n : 2 * n], refs[2 * n], refs[2 * n + 1]
    else:
        peak_in, pieces, out, held = refs[0], refs[1 : n + 1], refs[n + 1 : 2 * n + 1], refs[2 * n + 1]
    size = out[0].shape[0] // slots
    for k in range(n):
        d = lax.rem(here[0] + n - k, n)
        for i in range(slots):
            held[d * slots + i] = pieces[k][i * size : (i + 1) * size]
    if has_peak:
        top = pieces[0][slots * size :].astype(jnp.float32)
        for k in range(1, n):
            top = jnp.maximum(top, pieces[k][slots * size :].astype(jnp.float32))
        peak_out[...] = top
    else:
        top = peak_in[...]
    divisor = jnp.concatenate([top] * (size // TILE), axis=0) + epsilon
    for k in range(n):
        t = lax.rem(here[0] + k, n)
        for i in range(slots):
            q = joining[0, t * slots + i]
            out[k][i * size : (i + 1) * size] = (held[q].astype(jnp.float32) / divisor).astype(jnp.bfloat16)


def route(here, joining, pieces, slots, peak=None):
    n = len(pieces)
    has_peak = peak is None
    m = pieces[0].shape[1]
    size = (pieces[0].shape[0] - TILE * has_peak) // slots
    out_shape = [jax.ShapeDtypeStruct((slots * size, m), jnp.bfloat16)] * n
    if has_peak:
        out_shape = out_shape + [jax.ShapeDtypeStruct((TILE, m), jnp.float32)]
    ins = ([] if has_peak else [peak]) + list(pieces)
    return small_call(
        functools.partial(route_kernel, n, slots, has_peak),
        out_shape,
        [SMEM, SMEM] + [VMEM] * len(ins),
        [pltpu.VMEM((n * slots, size, m), jnp.bfloat16)],
        "route",
    )(here, joining, *ins)


def join_b_kernel(n, sites, here, *refs):
    pieces, new, shares = refs[:n], refs[n], refs[n + 1 :]
    _, _, slots, m, _ = new.shape
    rows, wide = m // n, m // sites
    for k in range(n):
        first = pl.multiple_of(lax.rem(here[0] + n - k, n) * rows, rows)
        for i in range(slots):
            for c in range(2):
                at = (2 * i + c) * rows
                new[c, 0, i, pl.ds(first, rows)] = pieces[k][at : at + rows]
    for k in range(sites):
        first = pl.multiple_of(lax.rem(here[1] + k, sites) * wide, wide)
        for i in range(slots):
            for c in range(2):
                shares[k][c, i] = new[c, 0, i, pl.ds(first, wide)]


def join_b(here, pieces, slots, sites):
    n, m = len(pieces), pieces[0].shape[1]
    share = jax.ShapeDtypeStruct((2, slots, m // sites, m), jnp.bfloat16)
    return small_call(
        functools.partial(join_b_kernel, n, sites),
        [jax.ShapeDtypeStruct((2, 1, slots, m, m), jnp.bfloat16)] + [share] * sites,
        [SMEM] + [VMEM] * n,
        [],
        "join_b",
    )(here, *pieces)


def join_g_kernel(n, here, *refs):
    pieces, new = refs[:n], refs[n]
    _, slots, m, _ = new.shape
    rows = m // n
    for k in range(n):
        first = pl.multiple_of(lax.rem(here[0] + n - k, n) * rows, rows)
        for i in range(slots):
            new[0, i, pl.ds(first, rows)] = pieces[k][i * rows : (i + 1) * rows]


def join_g(here, pieces, slots):
    n, m = len(pieces), pieces[0].shape[1]
    return small_call(
        functools.partial(join_g_kernel, n),
        [jax.ShapeDtypeStruct((1, slots, m, m), jnp.bfloat16)],
        [SMEM] + [VMEM] * n,
        [],
        "join_g",
    )(here, *pieces)[0]


def routed_by_tiles(here, turn, corner, bcorner, w, v, joining, n, sites):
    slots = w.shape[0]
    b_parts, g_parts = project(here, turn, corner, bcorner, w, v, n)
    b_parts = exchanged(b_parts, "blk")
    g_parts = exchanged(g_parts, "blk")
    *b_parts, peak = route(here, joining, b_parts, slots)
    b_parts = exchanged(b_parts, "blk")
    g_parts = exchanged(route(here, joining, g_parts, slots, peak), "blk")
    new_b, *shares = join_b(here, b_parts, slots, sites)
    shares = exchanged(shares, "site")
    new_corner = join_g(here, g_parts, slots)
    return new_corner, new_b, shares


def routed_by_rows(here, turn, corner, bcorner, w, v, joining, n, sites):
    slots, m, _ = w.shape
    rows = m // n
    ground, re, im = jax.vmap(lambda c, b, x, y: blocks_of(here, (turn[0], turn[1]), c, b, x, y))(
        corner[0], jnp.moveaxis(bcorner[:, 0], 0, 1), w, v
    )
    peak = lax.pmax(jnp.max(jnp.abs(ground)).astype(jnp.float32), "blk")
    blocks = jnp.moveaxis(jnp.stack([ground, re, im], axis=1).reshape(slots, 3, n, rows, m), 2, 0)
    pieces = lax.all_to_all(blocks, "blk", 0, 0, tiled=True).reshape(n * slots, 3, rows, m)
    scaled = (pieces[joining[0]].astype(jnp.float32) / (peak + epsilon)).astype(jnp.bfloat16)
    final = lax.all_to_all(scaled.reshape(n, slots, 3, rows, m), "blk", 0, 0, tiled=True)
    new = jnp.transpose(final, (2, 1, 0, 3, 4)).reshape(3, slots, m, m)
    shares = jnp.moveaxis(new[1:].reshape(2, slots, sites, m // sites, m), 2, 0)
    shares = lax.all_to_all(shares, "site", 0, 0, tiled=True)
    return new[0][None], new[1:][:, None], [shares[i] for i in range(sites)]


def per_device(corner, bcorner, edge, bedge, proj, joining, momentum):
    m = corner.shape[2]
    n, sites = lax.axis_size("blk"), lax.axis_size("site")
    my_site = lax.axis_index("site")
    here = jnp.stack([lax.axis_index("blk"), my_site]).astype(jnp.int32)
    angle = momentum[0] * my_site.astype(jnp.float32)
    turn = jnp.stack([jnp.cos(angle), jnp.sin(angle)])
    left_corner = shifted(corner, "site", 1)
    left_bcorner = shifted(bcorner, "site", 1)
    w, v = edge_proj(edge, bedge, proj)
    routed = routed_by_tiles if m % (n * TILE) == 0 else routed_by_rows
    new_corner, new_b, shares = routed(here, turn, left_corner, left_bcorner, w, v, joining, n, sites)
    summed = shares[0].astype(jnp.float32)
    for share in shares[1:]:
        summed = summed + share.astype(jnp.float32)
    return (new_corner, new_b, summed)


def solution(mesh):
    in_specs = (
        P("site", "blk", None, None),
        P(None, "site", "blk", None, None),
        P("site", "blk", None, None),
        P("site", "blk", None, None),
        P("site", "blk", None, None),
        P("site", None),
        P(),
    )
    out_specs = (
        P("site", "blk", None, None),
        P(None, "site", "blk", None, None),
        P(None, "blk", "site", None),
    )
    return jax.shard_map(
        per_device, mesh=mesh, in_specs=in_specs, out_specs=out_specs, check_vma=False
    )
```

```python
import functools

import jax
import jax.numpy as jnp
from jax import lax
from jax.experimental import pallas as pl
from jax.experimental.pallas import tpu as pltpu
from jax.sharding import PartitionSpec as P

epsilon = 1e-06
CAP = 2
TILE = 16
VMEM = pl.BlockSpec(memory_space=pltpu.VMEM)
SMEM = pl.BlockSpec(memory_space=pltpu.SMEM)
HBM = pl.BlockSpec(memory_space=pltpu.HBM)


def swapped(part, axis, k):
    n = lax.axis_size(axis)
    return part if k == 0 else lax.ppermute(part, axis, [(i, i ^ k) for i in range(n)])


def all_swapped(parts, axis):
    order = sorted(range(len(parts)), reverse=True)
    out = {k: swapped(parts[k], axis, k) for k in order}
    return [out[k] for k in range(len(parts))]


def edge_proj_kernel(edge, bedge, proj, w_ref, v_ref, edge_buf, bedge_buf, proj_buf, sems):
    slots = w_ref.shape[0]
    pairs = ((proj, proj_buf), (edge, edge_buf), (bedge, bedge_buf))
    copies = [
        [pltpu.make_async_copy(src.at[0, i], buf.at[i], sems.at[3 * i + a]) for a, (src, buf) in enumerate(pairs)]
        for i in range(slots)
    ]
    for group in copies:
        for copy in group:
            copy.start()
    dot = functools.partial(jnp.dot, preferred_element_type=jnp.float32)
    for i, (first, second, third) in enumerate(copies):
        first.wait()
        second.wait()
        w_ref[i] = dot(edge_buf[i], proj_buf[i]).astype(w_ref.dtype)
        third.wait()
        v_ref[i] = dot(bedge_buf[i], proj_buf[i]).astype(v_ref.dtype)


def edge_proj(edge, bedge, proj):
    _, slots, m, k = edge.shape
    block = jax.ShapeDtypeStruct((slots, m, m), jnp.bfloat16)
    return pl.pallas_call(
        edge_proj_kernel,
        out_shape=(block, block),
        in_specs=[HBM] * 3,
        out_specs=[VMEM] * 2,
        scratch_shapes=[
            pltpu.VMEM((slots, m, k), jnp.bfloat16),
            pltpu.VMEM((slots, m, k), jnp.bfloat16),
            pltpu.VMEM((slots, k, m), jnp.bfloat16),
            pltpu.SemaphoreType.DMA((3 * slots,)),
        ],
        cost_estimate=pl.CostEstimate(
            flops=4 * slots * m * k * m, bytes_accessed=6 * slots * m * k, transcendentals=0
        ),
        compiler_params=pltpu.CompilerParams(vmem_limit_bytes=20 << 20),
        name="edge_proj",
    )(edge, bedge, proj)


def small_call(kernel, out_shape, in_specs, scratch, name):
    return pl.pallas_call(
        kernel,
        out_shape=out_shape,
        in_specs=in_specs,
        out_specs=jax.tree.map(lambda _: VMEM, out_shape),
        scratch_shapes=scratch,
        cost_estimate=pl.CostEstimate(flops=1 << 28, bytes_accessed=1 << 20, transcendentals=0),
        compiler_params=pltpu.CompilerParams(vmem_limit_bytes=24 << 20),
        name=name,
    )


def project_kernel(n, here, turn, joining, corner, bcorner, w, v, *refs):
    b_out, g_out, stage, picks = refs[:n], refs[n : 2 * n], refs[2 * n], refs[2 * n + 1]
    slots, m, _ = w.shape
    me, cosine, sine = here[0], turn[0], turn[1]
    dot = functools.partial(jnp.dot, preferred_element_type=jnp.float32)
    top = jnp.zeros((m, m), jnp.float32)
    for i in range(slots):
        ground = dot(corner[0, i], w[i]).astype(jnp.bfloat16)
        real_term = dot(bcorner[0, 0, i], w[i])
        imag_term = dot(bcorner[1, 0, i], w[i])
        re = cosine * real_term - sine * imag_term + dot(corner[0, i], v[i])
        im = sine * real_term + cosine * imag_term
        stage[3 * i] = ground
        stage[3 * i + 1] = re.astype(jnp.bfloat16)
        stage[3 * i + 2] = im.astype(jnp.bfloat16)
        top = jnp.maximum(top, jnp.abs(ground.astype(jnp.float32)))
    peak = jnp.full((TILE, m), jnp.max(top), jnp.float32).astype(jnp.bfloat16)
    for p in range(CAP * n):
        picks[p] = 0
    for t in range(n):
        count = jnp.int32(0)
        for i in range(slots):
            mine = joining[0, t * slots + i] - me * slots
            inside = jnp.logical_and(mine >= 0, mine < slots)
            picks[jnp.where(inside, CAP * t + count, CAP * n)] = mine
            count = count + inside.astype(jnp.int32)
    for k in range(n):
        t = jnp.bitwise_xor(me, k)
        for j in range(CAP):
            slot = picks[CAP * t + j]
            g_out[k][j * m : (j + 1) * m] = stage[3 * slot]
            for c in range(2):
                at = (2 * j + c) * m
                b_out[k][at : at + m] = stage[3 * slot + 1 + c]
        b_out[k][2 * CAP * m :] = peak


def project(here, turn, joining, corner, bcorner, w, v, n):
    slots, m, _ = w.shape
    b_piece = jax.ShapeDtypeStruct((2 * CAP * m + TILE, m), jnp.bfloat16)
    g_piece = jax.ShapeDtypeStruct((CAP * m, m), jnp.bfloat16)
    out = small_call(
        functools.partial(project_kernel, n),
        [b_piece] * n + [g_piece] * n,
        [SMEM] * 3 + [VMEM] * 4,
        [pltpu.VMEM((3 * slots, m, m), jnp.bfloat16), pltpu.SMEM((CAP * n + 1,), jnp.int32)],
        "project",
    )(here, turn, joining, corner, bcorner, w, v)
    return out[:n], out[n:]


def find_places(n, slots, me, joining, places):
    for p in range(CAP * n):
        places[p] = -1
    owners = []
    for i in range(slots):
        owner = lax.div(joining[0, me * slots + i], slots)
        rank = sum([(other == owner).astype(jnp.int32) for other in owners], jnp.int32(0))
        places[CAP * owner + rank] = i
        owners.append(owner)


def join_b_kernel(n, shared, here, joining, *refs):
    pieces, new, peak, shares, places = refs[:n], refs[n], refs[n + 1], refs[n + 2 : -1], refs[-1]
    _, _, slots, m, _ = new.shape
    find_places(n, slots, here[0], joining, places)
    top = pieces[0][2 * CAP * m :].astype(jnp.float32)
    for k in range(1, n):
        top = jnp.maximum(top, pieces[k][2 * CAP * m :].astype(jnp.float32))
    peak[...] = top
    divisor = jnp.concatenate([top] * (m // TILE), axis=0) + epsilon
    for k in range(n):
        d = jnp.bitwise_xor(here[0], k)
        for j in range(CAP):
            place = places[CAP * d + j]

            @pl.when(place >= 0)
            def _():
                for c in range(2):
                    at = (2 * j + c) * m
                    new[c, 0, place] = (pieces[k][at : at + m].astype(jnp.float32) / divisor).astype(jnp.bfloat16)

    for k in range(shared):
        wide = m // shared
        first = pl.multiple_of(jnp.bitwise_xor(here[1], k) * wide, wide)
        for i in range(slots):
            for c in range(2):
                shares[k][c, i] = new[c, 0, i, pl.ds(first, wide)]


def join_b(here, joining, pieces, slots, m, shared):
    n = len(pieces)
    share = [jax.ShapeDtypeStruct((2, slots, m // shared, m), jnp.bfloat16)] * shared if shared else []
    return small_call(
        functools.partial(join_b_kernel, n, shared),
        [jax.ShapeDtypeStruct((2, 1, slots, m, m), jnp.bfloat16), jax.ShapeDtypeStruct((TILE, m), jnp.float32)] + share,
        [SMEM] * 2 + [VMEM] * n,
        [pltpu.SMEM((CAP * n,), jnp.int32)],
        "join_b",
    )(here, joining, *pieces)


def join_g_kernel(n, here, joining, peak, *refs):
    pieces, new, places = refs[:n], refs[n], refs[n + 1]
    _, slots, m, _ = new.shape
    find_places(n, slots, here[0], joining, places)
    divisor = jnp.concatenate([peak[...]] * (m // TILE), axis=0) + epsilon
    for k in range(n):
        d = jnp.bitwise_xor(here[0], k)
        for j in range(CAP):
            place = places[CAP * d + j]

            @pl.when(place >= 0)
            def _():
                piece = pieces[k][j * m : (j + 1) * m].astype(jnp.float32)
                new[0, place] = (piece / divisor).astype(jnp.bfloat16)


def join_g(here, joining, peak, pieces, slots, m):
    n = len(pieces)
    return small_call(
        functools.partial(join_g_kernel, n),
        [jax.ShapeDtypeStruct((1, slots, m, m), jnp.bfloat16)],
        [SMEM] * 2 + [VMEM] * (n + 1),
        [pltpu.SMEM((CAP * n,), jnp.int32)],
        "join_g",
    )(here, joining, peak, *pieces)[0]


def per_device(corner, bcorner, edge, bedge, proj, joining, momentum):
    _, slots, m, _ = corner.shape
    n, sites = lax.axis_size("blk"), lax.axis_size("site")
    my_site = lax.axis_index("site")
    here = jnp.stack([lax.axis_index("blk"), my_site]).astype(jnp.int32)
    angle = momentum[0] * my_site.astype(jnp.float32)
    turn = jnp.stack([jnp.cos(angle), jnp.sin(angle)])
    onward = [(i, (i + 1) % sites) for i in range(sites)]
    left_corner = lax.ppermute(corner, "site", onward)
    left_bcorner = lax.ppermute(bcorner, "site", onward)
    w, v = edge_proj(edge, bedge, proj)
    b_parts, g_parts = project(here, turn, joining, left_corner, left_bcorner, w, v, n)
    b_parts = all_swapped(b_parts, "blk")
    g_parts = all_swapped(g_parts, "blk")
    shared = sites if m % (sites * TILE) == 0 else 0
    new_b, peak, *shares = join_b(here, joining, b_parts, slots, m, shared)
    if shared:
        shares = all_swapped(shares, "site")
    else:
        shares = jnp.moveaxis(new_b.reshape(2, slots, sites, m // sites, m), 2, 0)
        shares = lax.all_to_all(shares, "site", 0, 0, tiled=True)
    new_corner = join_g(here, joining, peak, g_parts, slots, m)
    summed = shares[0].astype(jnp.float32)
    for k in range(1, sites):
        summed = summed + shares[k].astype(jnp.float32)
    return (new_corner, new_b, summed)


def solution(mesh):
    in_specs = (
        P("site", "blk", None, None),
        P(None, "site", "blk", None, None),
        P("site", "blk", None, None),
        P("site", "blk", None, None),
        P("site", "blk", None, None),
        P("site", None),
        P(),
    )
    out_specs = (
        P("site", "blk", None, None),
        P(None, "site", "blk", None, None),
        P(None, "blk", "site", None),
    )
    return jax.shard_map(
        per_device, mesh=mesh, in_specs=in_specs, out_specs=out_specs, check_vma=False
    )
```

```python
import functools

import jax
import jax.numpy as jnp
from jax import lax
from jax.experimental import pallas as pl
from jax.experimental.pallas import tpu as pltpu
from jax.sharding import PartitionSpec as P

epsilon = 1e-06
TILE = 16
VMEM = pl.BlockSpec(memory_space=pltpu.VMEM)
SMEM = pl.BlockSpec(memory_space=pltpu.SMEM)
HBM = pl.BlockSpec(memory_space=pltpu.HBM)


def all_swapped(parts, axis):
    n = len(parts)
    out = {k: lax.ppermute(parts[k], axis, [(i, i ^ k) for i in range(n)]) for k in range(n - 1, 0, -1)}
    return [parts[0]] + [out[k] for k in range(1, n)]


def edge_proj_kernel(edge, bedge, proj, wv_ref, edge_buf, bedge_buf, proj_buf, sems):
    slots = proj.shape[1]
    pairs = ((proj, proj_buf), (edge, edge_buf), (bedge, bedge_buf))
    copies = [
        [pltpu.make_async_copy(src.at[0, i], buf.at[i], sems.at[3 * i + a]) for a, (src, buf) in enumerate(pairs)]
        for i in range(slots)
    ]
    for group in copies:
        for copy in group:
            copy.start()
    dot = functools.partial(jnp.dot, preferred_element_type=jnp.float32)
    for i, (first, second, third) in enumerate(copies):
        first.wait()
        second.wait()
        wv_ref[2 * i] = dot(edge_buf[i], proj_buf[i]).astype(wv_ref.dtype)
        third.wait()
        wv_ref[2 * i + 1] = dot(bedge_buf[i], proj_buf[i]).astype(wv_ref.dtype)


def edge_proj(edge, bedge, proj):
    _, slots, m, k = edge.shape
    return pl.pallas_call(
        edge_proj_kernel,
        out_shape=jax.ShapeDtypeStruct((2 * slots, m, m), jnp.bfloat16),
        in_specs=[HBM] * 3,
        out_specs=VMEM,
        scratch_shapes=[
            pltpu.VMEM((slots, m, k), jnp.bfloat16),
            pltpu.VMEM((slots, m, k), jnp.bfloat16),
            pltpu.VMEM((slots, k, m), jnp.bfloat16),
            pltpu.SemaphoreType.DMA((3 * slots,)),
        ],
        cost_estimate=pl.CostEstimate(
            flops=4 * slots * m * k * m, bytes_accessed=6 * slots * m * k, transcendentals=0
        ),
        compiler_params=pltpu.CompilerParams(vmem_limit_bytes=60 << 20),
        name="edge_proj",
    )(edge, bedge, proj)


def small_call(kernel, out_shape, in_specs, scratch, name):
    return pl.pallas_call(
        kernel,
        out_shape=out_shape,
        in_specs=in_specs,
        out_specs=jax.tree.map(lambda _: VMEM, out_shape),
        scratch_shapes=scratch,
        cost_estimate=pl.CostEstimate(flops=1 << 28, bytes_accessed=1 << 20, transcendentals=0),
        compiler_params=pltpu.CompilerParams(vmem_limit_bytes=24 << 20),
        name=name,
    )


def blocks_of(turn, corner, bcorner, w, v):
    cosine, sine = turn
    dot = functools.partial(jnp.dot, preferred_element_type=jnp.float32)
    ground = dot(corner, w).astype(jnp.bfloat16)
    real_term = dot(bcorner[0], w)
    imag_term = dot(bcorner[1], w)
    re = cosine * real_term - sine * imag_term + dot(corner, v)
    im = sine * real_term + cosine * imag_term
    return ground, re.astype(jnp.bfloat16), im.astype(jnp.bfloat16)


def project_kernel(turn, corner, bcorner, wv, b_out, g_out):
    n = b_out.shape[0]
    slots, m = corner.shape[1], corner.shape[2]
    rows = m // n
    top = jnp.zeros((m, m), jnp.float32)
    for i in range(slots):
        here = (bcorner[0, 0, i], bcorner[1, 0, i])
        blocks = blocks_of((turn[0], turn[1]), corner[0, i], here, wv[2 * i], wv[2 * i + 1])
        top = jnp.maximum(top, jnp.abs(blocks[0].astype(jnp.float32)))
        for j in range(n):
            g_out[j, i * rows : (i + 1) * rows] = blocks[0][j * rows : (j + 1) * rows]
            for c in range(2):
                at = (2 * i + c) * rows
                b_out[j, at : at + rows] = blocks[1 + c][j * rows : (j + 1) * rows]
    peak = jnp.full((TILE, m), jnp.max(top), jnp.float32).astype(jnp.bfloat16)
    for j in range(n):
        b_out[j, 2 * slots * rows :] = peak


def project(turn, corner, bcorner, wv, n):
    _, slots, m, _ = corner.shape
    rows = m // n
    return small_call(
        project_kernel,
        [
            jax.ShapeDtypeStruct((n, 2 * slots * rows + TILE, m), jnp.bfloat16),
            jax.ShapeDtypeStruct((n, slots * rows, m), jnp.bfloat16),
        ],
        [SMEM] + [VMEM] * 3,
        [],
        "project",
    )(turn, corner, bcorner, wv)


def routed_to(out, pieces, joining, divisor):
    n, deep, _ = out.shape
    size = divisor.shape[0]
    slots = deep // size
    for t in range(n):
        for i in range(slots):
            q = joining[0, t * slots + i]
            d = lax.div(q, slots)
            first = pl.multiple_of((q - d * slots) * size, size)
            piece = pieces[d, pl.ds(first, size)].astype(jnp.float32)
            out[t, i * size : (i + 1) * size] = (piece / divisor).astype(out.dtype)


def route_b_kernel(joining, pieces, out, peak):
    n, deep, _ = out.shape
    top = pieces[0, deep:].astype(jnp.float32)
    for d in range(1, n):
        top = jnp.maximum(top, pieces[d, deep:].astype(jnp.float32))
    peak[...] = top
    routed_to(out, pieces, joining, jnp.concatenate([top, top], axis=0) + epsilon)


def route_g_kernel(joining, peak, pieces, out):
    routed_to(out, pieces, joining, peak[...] + epsilon)


def join_b_kernel(shared, here, pieces, new, *shares):
    n = pieces.shape[0]
    _, _, slots, m, _ = new.shape
    rows, wide = m // n, m // shared
    for j in range(n):
        for i in range(slots):
            for c in range(2):
                at = (2 * i + c) * rows
                new[c, 0, i, j * rows : (j + 1) * rows] = pieces[j, at : at + rows]
    for k in range(shared):
        first = pl.multiple_of(jnp.bitwise_xor(here[0], k) * wide, wide)
        for i in range(slots):
            for c in range(2):
                shares[k][c, i] = new[c, 0, i, pl.ds(first, wide)]


def join_g_kernel(pieces, new):
    n = pieces.shape[0]
    _, slots, m, _ = new.shape
    rows = m // n
    for j in range(n):
        for i in range(slots):
            new[0, i, j * rows : (j + 1) * rows] = pieces[j, i * rows : (i + 1) * rows]


def transposed(pieces):
    return lax.all_to_all(pieces, "blk", 0, 0, tiled=True)


def routed_by_tiles(turn, corner, bcorner, wv, joining, n, sites):
    _, slots, m, _ = corner.shape
    rows = m // n
    shape = lambda *dims, kind=jnp.bfloat16: jax.ShapeDtypeStruct(dims, kind)
    here = jnp.reshape(lax.axis_index("site"), (1,)).astype(jnp.int32)
    b_parts, g_parts = project(turn, corner, bcorner, wv, n)
    b_parts = transposed(b_parts)
    g_parts = transposed(g_parts)
    b_out = [shape(n, 2 * slots * rows, m), shape(TILE, m, kind=jnp.float32)]
    b_parts, peak = small_call(route_b_kernel, b_out, [SMEM, VMEM], [], "route_b")(joining, b_parts)
    b_parts = transposed(b_parts)
    g_out = [shape(n, slots * rows, m)]
    g_parts = small_call(route_g_kernel, g_out, [SMEM, VMEM, VMEM], [], "route_g")(joining, peak, g_parts)[0]
    g_parts = transposed(g_parts)
    new_out = [shape(2, 1, slots, m, m)] + [shape(2, slots, m // sites, m)] * sites
    join_b = small_call(functools.partial(join_b_kernel, sites), new_out, [SMEM, VMEM], [], "join_b")
    new_b, *shares = join_b(here, b_parts)
    shares = all_swapped(shares, "site")
    new_corner = small_call(join_g_kernel, [shape(1, slots, m, m)], [VMEM], [], "join_g")(g_parts)[0]
    return new_corner, new_b, shares


def routed_by_rows(turn, corner, bcorner, wv, joining, n, sites):
    _, slots, m, _ = corner.shape
    rows = m // n
    wv = wv.reshape(slots, 2, m, m)
    ground, re, im = jax.vmap(lambda c, b, x: blocks_of((turn[0], turn[1]), c, b, x[0], x[1]))(
        corner[0], jnp.moveaxis(bcorner[:, 0], 0, 1), wv
    )
    peak = lax.pmax(jnp.max(jnp.abs(ground)).astype(jnp.float32), "blk")
    blocks = jnp.moveaxis(jnp.stack([ground, re, im], axis=1).reshape(slots, 3, n, rows, m), 2, 0)
    pieces = transposed(blocks).reshape(n * slots, 3, rows, m)
    scaled = (pieces[joining[0]].astype(jnp.float32) / (peak + epsilon)).astype(jnp.bfloat16)
    final = transposed(scaled.reshape(n, slots, 3, rows, m))
    new = jnp.transpose(final, (2, 1, 0, 3, 4)).reshape(3, slots, m, m)
    shares = jnp.moveaxis(new[1:].reshape(2, slots, sites, m // sites, m), 2, 0)
    shares = lax.all_to_all(shares, "site", 0, 0, tiled=True)
    return new[0][None], new[1:][:, None], [shares[i] for i in range(sites)]


def per_device(corner, bcorner, edge, bedge, proj, joining, momentum):
    m = corner.shape[2]
    n, sites = lax.axis_size("blk"), lax.axis_size("site")
    angle = momentum[0] * lax.axis_index("site").astype(jnp.float32)
    turn = jnp.stack([jnp.cos(angle), jnp.sin(angle)])
    onward = [(i, (i + 1) % sites) for i in range(sites)]
    left_corner = lax.ppermute(corner, "site", onward)
    left_bcorner = lax.ppermute(bcorner, "site", onward)
    wv = edge_proj(edge, bedge, proj)
    routed = routed_by_tiles if m % (n * TILE) == 0 and m % (sites * TILE) == 0 else routed_by_rows
    new_corner, new_b, shares = routed(turn, left_corner, left_bcorner, wv, joining, n, sites)
    summed = shares[0].astype(jnp.float32)
    for share in shares[1:]:
        summed = summed + share.astype(jnp.float32)
    return (new_corner, new_b, summed)


def solution(mesh):
    in_specs = (
        P("site", "blk", None, None),
        P(None, "site", "blk", None, None),
        P("site", "blk", None, None),
        P("site", "blk", None, None),
        P("site", "blk", None, None),
        P("site", None),
        P(),
    )
    out_specs = (
        P("site", "blk", None, None),
        P(None, "site", "blk", None, None),
        P(None, "blk", "site", None),
    )
    return jax.shard_map(
        per_device, mesh=mesh, in_specs=in_specs, out_specs=out_specs, check_vma=False
    )
```

```python
import functools

import jax
import jax.numpy as jnp
from jax import lax
from jax.experimental import pallas as pl
from jax.experimental.pallas import tpu as pltpu
from jax.sharding import PartitionSpec as P

epsilon = 1e-06
SUB = 8
VMEM = pl.BlockSpec(memory_space=pltpu.VMEM)
SMEM = pl.BlockSpec(memory_space=pltpu.SMEM)
HBM = pl.BlockSpec(memory_space=pltpu.HBM)


def edge_proj_kernel(edge, bedge, proj, wv_ref, edge_buf, bedge_buf, proj_buf, sems):
    slots = proj.shape[1]
    pairs = ((proj, proj_buf), (edge, edge_buf), (bedge, bedge_buf))
    copies = [
        [pltpu.make_async_copy(src.at[0, i], buf.at[i], sems.at[3 * i + a]) for a, (src, buf) in enumerate(pairs)]
        for i in range(slots)
    ]
    for group in copies:
        for copy in group:
            copy.start()
    dot = functools.partial(jnp.dot, preferred_element_type=jnp.float32)
    for i, (first, second, third) in enumerate(copies):
        first.wait()
        second.wait()
        wv_ref[2 * i] = dot(edge_buf[i], proj_buf[i]).astype(wv_ref.dtype)
        third.wait()
        wv_ref[2 * i + 1] = dot(bedge_buf[i], proj_buf[i]).astype(wv_ref.dtype)


def edge_proj(edge, bedge, proj):
    _, slots, m, k = edge.shape
    return pl.pallas_call(
        edge_proj_kernel,
        out_shape=jax.ShapeDtypeStruct((2 * slots, m, m), jnp.bfloat16),
        in_specs=[HBM] * 3,
        out_specs=VMEM,
        scratch_shapes=[
            pltpu.VMEM((slots, m, k), jnp.bfloat16),
            pltpu.VMEM((slots, m, k), jnp.bfloat16),
            pltpu.VMEM((slots, k, m), jnp.bfloat16),
            pltpu.SemaphoreType.DMA((3 * slots,)),
        ],
        cost_estimate=pl.CostEstimate(
            flops=4 * slots * m * k * m, bytes_accessed=6 * slots * m * k, transcendentals=0
        ),
        compiler_params=pltpu.CompilerParams(vmem_limit_bytes=60 << 20),
        name="edge_proj",
    )(edge, bedge, proj)


def small_call(kernel, out_shape, in_specs, scratch, name):
    return pl.pallas_call(
        kernel,
        out_shape=out_shape,
        in_specs=in_specs,
        out_specs=jax.tree.map(lambda _: VMEM, out_shape),
        scratch_shapes=scratch,
        cost_estimate=pl.CostEstimate(flops=1 << 28, bytes_accessed=1 << 20, transcendentals=0),
        compiler_params=pltpu.CompilerParams(vmem_limit_bytes=24 << 20),
        name=name,
    )


def blocks_of(turn, corner, bcorner, w, v):
    cosine, sine = turn
    dot = functools.partial(jnp.dot, preferred_element_type=jnp.float32)
    ground = dot(corner, w)
    real_term = dot(bcorner[0], w)
    imag_term = dot(bcorner[1], w)
    re = cosine * real_term - sine * imag_term + dot(corner, v)
    im = sine * real_term + cosine * imag_term
    return ground, re, im


def spread_kernel(sites, turn, corner, bcorner, wv, out, stage):
    slots, m = corner.shape[1], corner.shape[2]
    per_site, tiles = out.shape[0] // sites, 3 * slots * sites
    top = jnp.zeros((m, m), jnp.float32)
    for i in range(slots):
        here = (bcorner[0, 0, i], bcorner[1, 0, i])
        ground, re, im = blocks_of((turn[0], turn[1]), corner[0, i], here, wv[2 * i], wv[2 * i + 1])
        top = jnp.maximum(top, jnp.abs(ground))
        for s in range(sites):
            for r in range(sites):
                rows = slice((r * sites + s) * SUB, (r * sites + s + 1) * SUB)
                places = (
                    (2 * i * sites + r, re),
                    ((2 * i + 1) * sites + r, im),
                    ((2 * slots + i) * sites + r, ground),
                )
                for place, block in places:
                    at = (s * tiles + place) * SUB
                    stage[at : at + SUB] = block[rows]
    peak = jnp.full((SUB, m), jnp.max(top), jnp.float32)
    for s in range(sites):
        for j in range(per_site):
            piece = stage[pl.ds(s * tiles * SUB + j, tiles, stride=SUB)]
            out[s * per_site + j] = jnp.concatenate([piece, peak], axis=0).astype(out.dtype)


def route_kernel(sites, slots, joining, pieces, out, held, sums):
    n = pieces.shape[0] // sites
    deep, m = pieces.shape[1], pieces.shape[2]
    for p in range(sites * n):
        held[p * deep : (p + 1) * deep] = pieces[p].astype(jnp.float32)
    low = lax.broadcasted_iota(jnp.int32, (SUB, m), 0) < SUB // 2
    divisors = []
    for s in range(sites):
        last = [held[(s * n + d + 1) * deep - SUB : (s * n + d + 1) * deep] for d in range(n)]
        divisors.append(functools.reduce(jnp.maximum, last) + epsilon)
    for t in range(n):
        total = [jnp.zeros((SUB, m), jnp.float32)] * slots
        routed = []
        for s in range(sites):
            b_tiles, g_tiles = [], []
            for i in range(slots):
                q = joining[s, t * slots + i]
                d = lax.div(q, slots)
                slot = q - d * slots
                base = (s * n + d) * deep
                tile = held[pl.ds(pl.multiple_of(base + slot * SUB, SUB), SUB)]
                tile = (tile / divisors[s]).astype(jnp.bfloat16).astype(jnp.float32)
                b_tiles.append(tile)
                total[i] = total[i] + tile
                pair = lax.shift_right_logical(slot, 1)
                tile = held[pl.ds(pl.multiple_of(base + (slots + pair) * SUB, SUB), SUB)]
                other_half = jnp.bitwise_and(slot, 1) != i % 2
                g_tiles.append(jnp.where(other_half, pltpu.roll(tile, SUB // 2, 0), tile))
            for i in range(0, slots, 2):
                b_tiles.append(jnp.where(low, g_tiles[i], g_tiles[i + 1]) / divisors[s])
            routed.append(b_tiles)
        for i in range(slots):
            at = (t * slots + i) * SUB
            sums[at : at + SUB] = total[i]
        for s in range(sites):
            share = sums[pl.ds(t * slots * SUB + s, 2 * slots, stride=sites)]
            filler = jnp.zeros((out.shape[1] - len(routed[s]) * SUB - 2 * slots, m), jnp.float32)
            out[s * n + t] = jnp.concatenate(routed[s] + [share, filler], axis=0).astype(out.dtype)


def join_kernel(sites, pieces, new_corner, new_b, summed, stage):
    n = pieces.shape[0] // sites
    deep = pieces.shape[1]
    slots = new_corner.shape[1]
    for s in range(sites):
        for j in range(n):
            stage[pl.ds(s * deep * SUB + j, deep, stride=SUB)] = pieces[s * n + j].astype(jnp.float32)

    def tile(s, place):
        at = (s * deep + place) * SUB
        return stage[at : at + SUB]

    for i in range(slots):
        for r in range(sites):
            for s in range(0, sites, 2):
                rows = slice((r * sites + s) * SUB, (r * sites + s + 2) * SUB)

                def both(place):
                    return jnp.concatenate([tile(s, place), tile(s + 1, place)], axis=0).astype(jnp.bfloat16)

                new_b[0, 0, i, rows] = both(2 * i * sites + r)
                new_b[1, 0, i, rows] = both((2 * i + 1) * sites + r)
                new_corner[0, i, rows] = both((2 * slots + i) * sites + r)
        for s in range(sites):
            for c in range(2):
                summed[c, i, s * SUB : (s + 1) * SUB] = tile(s, 3 * slots * sites + 2 * i + c)


def routed_by_sublanes(turn, corner, bcorner, wv, joining, n, sites):
    _, slots, m, _ = corner.shape
    shape = lambda *dims, kind=jnp.bfloat16: jax.ShapeDtypeStruct(dims, kind)
    scratch = lambda rows: pltpu.VMEM((rows, m), jnp.float32)
    every = ("site", "blk")
    tiles = 3 * slots * sites
    joining = lax.all_gather(joining, "site", axis=0, tiled=True)
    deep = tiles + SUB
    pieces = small_call(
        functools.partial(spread_kernel, sites),
        [shape(sites * n, deep, m)],
        [SMEM] + [VMEM] * 3,
        [scratch((sites * tiles + 1) * SUB)],
        "spread",
    )(turn, corner, bcorner, wv)[0]
    pieces = lax.all_to_all(pieces, every, 0, 0, tiled=True)
    wide = tiles + 2 * slots + (-(tiles + 2 * slots)) % SUB
    pieces = small_call(
        functools.partial(route_kernel, sites, slots),
        [shape(sites * n, wide, m)],
        [SMEM, VMEM],
        [scratch(sites * n * deep), scratch((n * slots + 1) * SUB)],
        "route",
    )(joining, pieces)[0]
    pieces = lax.all_to_all(pieces, every, 0, 0, tiled=True)
    return small_call(
        functools.partial(join_kernel, sites),
        [shape(1, slots, m, m), shape(2, 1, slots, m, m), shape(2, slots, m // sites, m, kind=jnp.float32)],
        [VMEM],
        [scratch((sites * wide + 1) * SUB)],
        "join",
    )(pieces)


def transposed(pieces):
    return lax.all_to_all(pieces, "blk", 0, 0, tiled=True)


def routed_by_rows(turn, corner, bcorner, wv, joining, n, sites):
    _, slots, m, _ = corner.shape
    rows = m // n
    wv = wv.reshape(slots, 2, m, m)
    ground, re, im = jax.vmap(lambda c, b, x: blocks_of((turn[0], turn[1]), c, b, x[0], x[1]))(
        corner[0], jnp.moveaxis(bcorner[:, 0], 0, 1), wv
    )
    blocks = jnp.stack([ground, re, im], axis=1).astype(jnp.bfloat16)
    peak = lax.pmax(jnp.max(jnp.abs(blocks[:, 0])).astype(jnp.float32), "blk")
    blocks = jnp.moveaxis(blocks.reshape(slots, 3, n, rows, m), 2, 0)
    pieces = transposed(blocks).reshape(n * slots, 3, rows, m)
    scaled = (pieces[joining[0]].astype(jnp.float32) / (peak + epsilon)).astype(jnp.bfloat16)
    final = transposed(scaled.reshape(n, slots, 3, rows, m))
    new = jnp.transpose(final, (2, 1, 0, 3, 4)).reshape(3, slots, m, m)
    shares = jnp.moveaxis(new[1:].reshape(2, slots, sites, m // sites, m), 2, 0)
    shares = lax.all_to_all(shares, "site", 0, 0, tiled=True)
    return new[0][None], new[1:][:, None], jnp.sum(shares.astype(jnp.float32), axis=0)


def per_device(corner, bcorner, edge, bedge, proj, joining, momentum):
    m = corner.shape[2]
    n, sites = lax.axis_size("blk"), lax.axis_size("site")
    angle = momentum[0] * lax.axis_index("site").astype(jnp.float32)
    turn = jnp.stack([jnp.cos(angle), jnp.sin(angle)])
    onward = [(i, (i + 1) % sites) for i in range(sites)]
    left_corner = lax.ppermute(corner, "site", onward)
    left_bcorner = lax.ppermute(bcorner, "site", onward)
    wv = edge_proj(edge, bedge, proj)
    fits = n == SUB and m == sites * sites * SUB and sites == SUB // 2
    routed = routed_by_sublanes if fits else routed_by_rows
    return routed(turn, left_corner, left_bcorner, wv, joining, n, sites)


def solution(mesh):
    in_specs = (
        P("site", "blk", None, None),
        P(None, "site", "blk", None, None),
        P("site", "blk", None, None),
        P("site", "blk", None, None),
        P("site", "blk", None, None),
        P("site", None),
        P(),
    )
    out_specs = (
        P("site", "blk", None, None),
        P(None, "site", "blk", None, None),
        P(None, "blk", "site", None),
    )
    return jax.shard_map(
        per_device, mesh=mesh, in_specs=in_specs, out_specs=out_specs, check_vma=False
    )
```

```python
import functools

import jax
import jax.numpy as jnp
from jax import lax
from jax.experimental import pallas as pl
from jax.experimental.pallas import tpu as pltpu
from jax.sharding import PartitionSpec as P

epsilon = 1e-06
TILE = 16
VMEM = pl.BlockSpec(memory_space=pltpu.VMEM)
SMEM = pl.BlockSpec(memory_space=pltpu.SMEM)
HBM = pl.BlockSpec(memory_space=pltpu.HBM)


def all_swapped(parts, axis):
    n = len(parts)
    out = {k: lax.ppermute(parts[k], axis, [(i, i ^ k) for i in range(n)]) for k in range(n - 1, 0, -1)}
    return [parts[0]] + [out[k] for k in range(1, n)]


def edge_proj_kernel(edge, bedge, proj, wv_ref, edge_buf, bedge_buf, proj_buf, sems):
    slots = proj.shape[1]
    pairs = ((proj, proj_buf), (edge, edge_buf), (bedge, bedge_buf))
    copies = [
        [pltpu.make_async_copy(src.at[0, i], buf.at[i], sems.at[3 * i + a]) for a, (src, buf) in enumerate(pairs)]
        for i in range(slots)
    ]
    for group in copies:
        for copy in group:
            copy.start()
    dot = functools.partial(jnp.dot, preferred_element_type=jnp.float32)
    for i, (first, second, third) in enumerate(copies):
        first.wait()
        second.wait()
        wv_ref[2 * i] = dot(edge_buf[i], proj_buf[i]).astype(wv_ref.dtype)
        third.wait()
        wv_ref[2 * i + 1] = dot(bedge_buf[i], proj_buf[i]).astype(wv_ref.dtype)


def edge_proj(edge, bedge, proj):
    _, slots, m, k = edge.shape
    return pl.pallas_call(
        edge_proj_kernel,
        out_shape=jax.ShapeDtypeStruct((2 * slots, m, m), jnp.bfloat16),
        in_specs=[HBM] * 3,
        out_specs=VMEM,
        scratch_shapes=[
            pltpu.VMEM((slots, m, k), jnp.bfloat16),
            pltpu.VMEM((slots, m, k), jnp.bfloat16),
            pltpu.VMEM((slots, k, m), jnp.bfloat16),
            pltpu.SemaphoreType.DMA((3 * slots,)),
        ],
        cost_estimate=pl.CostEstimate(
            flops=4 * slots * m * k * m, bytes_accessed=6 * slots * m * k, transcendentals=0
        ),
        compiler_params=pltpu.CompilerParams(vmem_limit_bytes=60 << 20),
        name="edge_proj",
    )(edge, bedge, proj)


def small_call(kernel, out_shape, in_specs, scratch, name):
    return pl.pallas_call(
        kernel,
        out_shape=out_shape,
        in_specs=in_specs,
        out_specs=jax.tree.map(lambda _: VMEM, out_shape),
        scratch_shapes=scratch,
        cost_estimate=pl.CostEstimate(flops=1 << 28, bytes_accessed=1 << 20, transcendentals=0),
        compiler_params=pltpu.CompilerParams(vmem_limit_bytes=24 << 20),
        name=name,
    )


def blocks_of(turn, corner, bcorner, w, v):
    cosine, sine = turn
    dot = functools.partial(jnp.dot, preferred_element_type=jnp.float32)
    ground = dot(corner, w).astype(jnp.bfloat16)
    real_term = dot(bcorner[0], w)
    imag_term = dot(bcorner[1], w)
    re = cosine * real_term - sine * imag_term + dot(corner, v)
    im = sine * real_term + cosine * imag_term
    return ground, re.astype(jnp.bfloat16), im.astype(jnp.bfloat16)


def spread_kernel(n, here, turn, corner, bcorner, wv, *refs):
    out, stage = refs[:n], refs[n]
    slots, m = corner.shape[1], corner.shape[2]
    rows = m // n
    top = jnp.zeros((m, m), jnp.float32)
    for i in range(slots):
        b_here = (bcorner[0, 0, i], bcorner[1, 0, i])
        blocks = blocks_of((turn[0], turn[1]), corner[0, i], b_here, wv[2 * i], wv[2 * i + 1])
        top = jnp.maximum(top, jnp.abs(blocks[0].astype(jnp.float32)))
        for kind in range(3):
            stage[3 * i + kind] = blocks[kind]
    peak = jnp.full((TILE, m), jnp.max(top), jnp.float32).astype(jnp.bfloat16)
    for k in range(n):
        first = pl.multiple_of(jnp.bitwise_xor(here[0], k) * rows, rows)
        for b in range(3 * slots):
            out[k][b * rows : (b + 1) * rows] = stage[b, pl.ds(first, rows)]
        out[k][3 * slots * rows :] = peak


def route_kernel(n, slots, here, joining, *refs):
    pieces, out, held = refs[:n], refs[n : 2 * n], refs[2 * n]
    size = held.shape[1]
    for k in range(n):
        d = jnp.bitwise_xor(here[0], k)
        for i in range(slots):
            held[d * slots + i] = pieces[k][i * size : (i + 1) * size]
    top = functools.reduce(jnp.maximum, [piece[slots * size :].astype(jnp.float32) for piece in pieces])
    divisor = jnp.concatenate([top] * (size // TILE), axis=0) + epsilon
    for k in range(n):
        t = jnp.bitwise_xor(here[0], k)
        for i in range(slots):
            q = joining[0, t * slots + i]
            out[k][i * size : (i + 1) * size] = (held[q].astype(jnp.float32) / divisor).astype(jnp.bfloat16)


def share_kernel(n, sites, here, *refs):
    pieces, shares, stage = refs[:n], refs[n : n + sites], refs[n + sites]
    _, slots, wide, m = shares[0].shape
    rows = m // n
    for k in range(n):
        first = pl.multiple_of(jnp.bitwise_xor(here[0], k) * rows, rows)
        for i in range(slots):
            for c in range(2):
                at = (3 * i + 1 + c) * rows
                stage[c, i, pl.ds(first, rows)] = pieces[k][at : at + rows]
    for k in range(sites):
        first = pl.multiple_of(jnp.bitwise_xor(here[1], k) * wide, wide)
        for i in range(slots):
            for c in range(2):
                shares[k][c, i] = stage[c, i, pl.ds(first, wide)]


def join_kernel(n, here, *refs):
    pieces, new_corner, new_b = refs[:n], refs[n], refs[n + 1]
    _, slots, m, _ = new_corner.shape
    rows = m // n
    for k in range(n):
        first = pl.multiple_of(jnp.bitwise_xor(here[0], k) * rows, rows)
        for i in range(slots):
            at = 3 * i * rows
            new_corner[0, i, pl.ds(first, rows)] = pieces[k][at : at + rows]
            for c in range(2):
                at = (3 * i + 1 + c) * rows
                new_b[c, 0, i, pl.ds(first, rows)] = pieces[k][at : at + rows]


def routed_by_tiles(turn, corner, bcorner, wv, joining, n, sites):
    _, slots, m, _ = corner.shape
    rows = m // n
    shape = lambda *dims: jax.ShapeDtypeStruct(dims, jnp.bfloat16)
    scratch = lambda *dims: [pltpu.VMEM(dims, jnp.bfloat16)]
    bind = functools.partial
    here = jnp.stack([lax.axis_index("blk"), lax.axis_index("site")]).astype(jnp.int32)
    pieces = [shape(3 * slots * rows + TILE, m)] * n
    kept = scratch(3 * slots, m, m)
    parts = small_call(bind(spread_kernel, n), pieces, [SMEM] * 2 + [VMEM] * 3, kept, "spread")(
        here, turn, corner, bcorner, wv
    )
    parts = all_swapped(parts, "blk")
    pieces = [shape(3 * slots * rows, m)] * n
    kept = scratch(n * slots, 3 * rows, m)
    parts = small_call(bind(route_kernel, n, slots), pieces, [SMEM] * 2 + [VMEM] * n, kept, "route")(
        here, joining, *parts
    )
    parts = all_swapped(parts, "blk")
    ins = [SMEM] + [VMEM] * n
    pieces = [shape(2, slots, m // sites, m)] * sites
    shares = small_call(bind(share_kernel, n, sites), pieces, ins, scratch(2, slots, m, m), "share")(here, *parts)
    shares = all_swapped(shares, "site")
    pieces = [shape(1, slots, m, m), shape(2, 1, slots, m, m)]
    new_corner, new_b = small_call(bind(join_kernel, n), pieces, ins, [], "join")(here, *parts)
    return new_corner, new_b, shares


def transposed(pieces):
    return lax.all_to_all(pieces, "blk", 0, 0, tiled=True)


def routed_by_rows(turn, corner, bcorner, wv, joining, n, sites):
    _, slots, m, _ = corner.shape
    rows = m // n
    wv = wv.reshape(slots, 2, m, m)
    ground, re, im = jax.vmap(lambda c, b, x: blocks_of((turn[0], turn[1]), c, b, x[0], x[1]))(
        corner[0], jnp.moveaxis(bcorner[:, 0], 0, 1), wv
    )
    peak = lax.pmax(jnp.max(jnp.abs(ground)).astype(jnp.float32), "blk")
    blocks = jnp.moveaxis(jnp.stack([ground, re, im], axis=1).reshape(slots, 3, n, rows, m), 2, 0)
    pieces = transposed(blocks).reshape(n * slots, 3, rows, m)
    scaled = (pieces[joining[0]].astype(jnp.float32) / (peak + epsilon)).astype(jnp.bfloat16)
    final = transposed(scaled.reshape(n, slots, 3, rows, m))
    new = jnp.transpose(final, (2, 1, 0, 3, 4)).reshape(3, slots, m, m)
    shares = jnp.moveaxis(new[1:].reshape(2, slots, sites, m // sites, m), 2, 0)
    shares = lax.all_to_all(shares, "site", 0, 0, tiled=True)
    return new[0][None], new[1:][:, None], [shares[i] for i in range(sites)]


def per_device(corner, bcorner, edge, bedge, proj, joining, momentum):
    m = corner.shape[2]
    n, sites = lax.axis_size("blk"), lax.axis_size("site")
    angle = momentum[0] * lax.axis_index("site").astype(jnp.float32)
    turn = jnp.stack([jnp.cos(angle), jnp.sin(angle)])
    onward = [(i, (i + 1) % sites) for i in range(sites)]
    left_corner = lax.ppermute(corner, "site", onward)
    left_bcorner = lax.ppermute(bcorner, "site", onward)
    wv = edge_proj(edge, bedge, proj)
    routed = routed_by_tiles if m % (n * TILE) == 0 and m % (sites * TILE) == 0 else routed_by_rows
    new_corner, new_b, shares = routed(turn, left_corner, left_bcorner, wv, joining, n, sites)
    summed = shares[0].astype(jnp.float32)
    for share in shares[1:]:
        summed = summed + share.astype(jnp.float32)
    return (new_corner, new_b, summed)


def solution(mesh):
    in_specs = (
        P("site", "blk", None, None),
        P(None, "site", "blk", None, None),
        P("site", "blk", None, None),
        P("site", "blk", None, None),
        P("site", "blk", None, None),
        P("site", None),
        P(),
    )
    out_specs = (
        P("site", "blk", None, None),
        P(None, "site", "blk", None, None),
        P(None, "blk", "site", None),
    )
    return jax.shard_map(
        per_device, mesh=mesh, in_specs=in_specs, out_specs=out_specs, check_vma=False
    )
```

```python
import functools

import jax
import jax.numpy as jnp
from jax import lax
from jax.experimental import pallas as pl
from jax.experimental.pallas import tpu as pltpu
from jax.sharding import PartitionSpec as P

epsilon = 1e-06
TILE = 16
VMEM = pl.BlockSpec(memory_space=pltpu.VMEM)
SMEM = pl.BlockSpec(memory_space=pltpu.SMEM)
HBM = pl.BlockSpec(memory_space=pltpu.HBM)


def far_first(n):
    far, near = range(n // 2, n), range(n // 2 - 1, 0, -1)
    return (0, *sorted(far, key=lambda k: (k & 1, -k)), *near)


def all_swapped(parts, steps, axis):
    n = len(parts)
    return [lax.ppermute(part, axis, [(i, i ^ k) for i in range(n)]) if k else part for part, k in zip(parts, steps)]


def edge_proj_kernel(edge, bedge, proj, wv_ref, edge_buf, bedge_buf, proj_buf, sems):
    slots = proj.shape[1]
    pairs = ((proj, proj_buf), (edge, edge_buf), (bedge, bedge_buf))
    copies = [
        [pltpu.make_async_copy(src.at[0, i], buf.at[i], sems.at[3 * i + a]) for a, (src, buf) in enumerate(pairs)]
        for i in range(slots)
    ]
    for group in copies:
        for copy in group:
            copy.start()
    dot = functools.partial(jnp.dot, preferred_element_type=jnp.float32)
    for i, (first, second, third) in enumerate(copies):
        first.wait()
        second.wait()
        wv_ref[2 * i] = dot(edge_buf[i], proj_buf[i]).astype(wv_ref.dtype)
        third.wait()
        wv_ref[2 * i + 1] = dot(bedge_buf[i], proj_buf[i]).astype(wv_ref.dtype)


def edge_proj(edge, bedge, proj):
    _, slots, m, k = edge.shape
    return pl.pallas_call(
        edge_proj_kernel,
        out_shape=jax.ShapeDtypeStruct((2 * slots, m, m), jnp.bfloat16),
        in_specs=[HBM] * 3,
        out_specs=VMEM,
        scratch_shapes=[
            pltpu.VMEM((slots, m, k), jnp.bfloat16),
            pltpu.VMEM((slots, m, k), jnp.bfloat16),
            pltpu.VMEM((slots, k, m), jnp.bfloat16),
            pltpu.SemaphoreType.DMA((3 * slots,)),
        ],
        cost_estimate=pl.CostEstimate(
            flops=4 * slots * m * k * m, bytes_accessed=6 * slots * m * k, transcendentals=0
        ),
        compiler_params=pltpu.CompilerParams(vmem_limit_bytes=60 << 20),
        name="edge_proj",
    )(edge, bedge, proj)


def small_call(kernel, out_shape, in_specs, scratch, name):
    return pl.pallas_call(
        kernel,
        out_shape=out_shape,
        in_specs=in_specs,
        out_specs=jax.tree.map(lambda _: VMEM, out_shape),
        scratch_shapes=scratch,
        cost_estimate=pl.CostEstimate(flops=1 << 28, bytes_accessed=1 << 20, transcendentals=0),
        compiler_params=pltpu.CompilerParams(vmem_limit_bytes=24 << 20),
        name=name,
    )


def blocks_of(turn, corner, bcorner, w, v):
    cosine, sine = turn
    dot = functools.partial(jnp.dot, preferred_element_type=jnp.float32)
    ground = dot(corner, w).astype(jnp.bfloat16)
    real_term = dot(bcorner[0], w)
    imag_term = dot(bcorner[1], w)
    re = cosine * real_term - sine * imag_term + dot(corner, v)
    im = sine * real_term + cosine * imag_term
    return ground, re.astype(jnp.bfloat16), im.astype(jnp.bfloat16)


def spread_kernel(steps, here, turn, corner, bcorner, wv, *refs):
    n = len(steps)
    out, stage = refs[:n], refs[n]
    slots, m = corner.shape[1], corner.shape[2]
    rows = m // n
    top = jnp.zeros((m, m), jnp.float32)
    for i in range(slots):
        b_here = (bcorner[0, 0, i], bcorner[1, 0, i])
        blocks = blocks_of((turn[0], turn[1]), corner[0, i], b_here, wv[2 * i], wv[2 * i + 1])
        top = jnp.maximum(top, jnp.abs(blocks[0].astype(jnp.float32)))
        for kind in range(3):
            stage[3 * i + kind] = blocks[kind]
    peak = jnp.full((TILE, m), jnp.max(top), jnp.float32).astype(jnp.bfloat16)
    for p, k in enumerate(steps):
        first = pl.multiple_of(jnp.bitwise_xor(here[0], k) * rows, rows)
        for b in range(3 * slots):
            out[p][b * rows : (b + 1) * rows] = stage[b, pl.ds(first, rows)]
        out[p][3 * slots * rows :] = peak


def route_kernel(steps, slots, here, joining, *refs):
    n = len(steps)
    pieces, out, held = refs[:n], refs[n : 2 * n], refs[2 * n]
    size = held.shape[1]
    for p, k in enumerate(steps):
        d = jnp.bitwise_xor(here[0], k)
        for i in range(slots):
            held[d * slots + i] = pieces[p][i * size : (i + 1) * size]
    top = functools.reduce(jnp.maximum, [piece[slots * size :].astype(jnp.float32) for piece in pieces])
    divisor = jnp.concatenate([top] * (size // TILE), axis=0) + epsilon
    for p, k in enumerate(steps):
        t = jnp.bitwise_xor(here[0], k)
        for i in range(slots):
            q = joining[0, t * slots + i]
            out[p][i * size : (i + 1) * size] = (held[q].astype(jnp.float32) / divisor).astype(jnp.bfloat16)


def share_kernel(steps, site_steps, here, *refs):
    n, sites = len(steps), len(site_steps)
    pieces, shares, stage = refs[:n], refs[n : n + sites], refs[n + sites]
    _, slots, wide, m = shares[0].shape
    rows = m // n
    for p, k in enumerate(steps):
        first = pl.multiple_of(jnp.bitwise_xor(here[0], k) * rows, rows)
        for i in range(slots):
            for c in range(2):
                at = (3 * i + 1 + c) * rows
                stage[c, i, pl.ds(first, rows)] = pieces[p][at : at + rows]
    for p, k in enumerate(site_steps):
        first = pl.multiple_of(jnp.bitwise_xor(here[1], k) * wide, wide)
        for i in range(slots):
            for c in range(2):
                shares[p][c, i] = stage[c, i, pl.ds(first, wide)]


def join_kernel(steps, here, *refs):
    n = len(steps)
    pieces, new_corner, new_b = refs[:n], refs[n], refs[n + 1]
    _, slots, m, _ = new_corner.shape
    rows = m // n
    for p, k in enumerate(steps):
        first = pl.multiple_of(jnp.bitwise_xor(here[0], k) * rows, rows)
        for i in range(slots):
            at = 3 * i * rows
            new_corner[0, i, pl.ds(first, rows)] = pieces[p][at : at + rows]
            for c in range(2):
                at = (3 * i + 1 + c) * rows
                new_b[c, 0, i, pl.ds(first, rows)] = pieces[p][at : at + rows]


def routed_by_tiles(turn, corner, bcorner, wv, joining, n, sites):
    _, slots, m, _ = corner.shape
    rows = m // n
    shape = lambda *dims: jax.ShapeDtypeStruct(dims, jnp.bfloat16)
    scratch = lambda *dims: [pltpu.VMEM(dims, jnp.bfloat16)]
    bind = functools.partial
    steps, site_steps = far_first(n), far_first(sites)
    here = jnp.stack([lax.axis_index("blk"), lax.axis_index("site")]).astype(jnp.int32)
    pieces = [shape(3 * slots * rows + TILE, m)] * n
    kept = scratch(3 * slots, m, m)
    parts = small_call(bind(spread_kernel, steps), pieces, [SMEM] * 2 + [VMEM] * 3, kept, "spread")(
        here, turn, corner, bcorner, wv
    )
    parts = all_swapped(parts, steps, "blk")
    pieces = [shape(3 * slots * rows, m)] * n
    kept = scratch(n * slots, 3 * rows, m)
    parts = small_call(bind(route_kernel, steps, slots), pieces, [SMEM] * 2 + [VMEM] * n, kept, "route")(
        here, joining, *parts
    )
    parts = all_swapped(parts, steps, "blk")
    ins = [SMEM] + [VMEM] * n
    pieces = [shape(2, slots, m // sites, m)] * sites
    shares = small_call(bind(share_kernel, steps, site_steps), pieces, ins, scratch(2, slots, m, m), "share")(here, *parts)
    shares = all_swapped(shares, site_steps, "site")
    pieces = [shape(1, slots, m, m), shape(2, 1, slots, m, m)]
    new_corner, new_b = small_call(bind(join_kernel, steps), pieces, ins, [], "join")(here, *parts)
    return new_corner, new_b, shares


def transposed(pieces):
    return lax.all_to_all(pieces, "blk", 0, 0, tiled=True)


def routed_by_rows(turn, corner, bcorner, wv, joining, n, sites):
    _, slots, m, _ = corner.shape
    rows = m // n
    wv = wv.reshape(slots, 2, m, m)
    ground, re, im = jax.vmap(lambda c, b, x: blocks_of((turn[0], turn[1]), c, b, x[0], x[1]))(
        corner[0], jnp.moveaxis(bcorner[:, 0], 0, 1), wv
    )
    peak = lax.pmax(jnp.max(jnp.abs(ground)).astype(jnp.float32), "blk")
    blocks = jnp.moveaxis(jnp.stack([ground, re, im], axis=1).reshape(slots, 3, n, rows, m), 2, 0)
    pieces = transposed(blocks).reshape(n * slots, 3, rows, m)
    scaled = (pieces[joining[0]].astype(jnp.float32) / (peak + epsilon)).astype(jnp.bfloat16)
    final = transposed(scaled.reshape(n, slots, 3, rows, m))
    new = jnp.transpose(final, (2, 1, 0, 3, 4)).reshape(3, slots, m, m)
    shares = jnp.moveaxis(new[1:].reshape(2, slots, sites, m // sites, m), 2, 0)
    shares = lax.all_to_all(shares, "site", 0, 0, tiled=True)
    return new[0][None], new[1:][:, None], [shares[i] for i in range(sites)]


def per_device(corner, bcorner, edge, bedge, proj, joining, momentum):
    m = corner.shape[2]
    n, sites = lax.axis_size("blk"), lax.axis_size("site")
    angle = momentum[0] * lax.axis_index("site").astype(jnp.float32)
    turn = jnp.stack([jnp.cos(angle), jnp.sin(angle)])
    onward = [(i, (i + 1) % sites) for i in range(sites)]
    left_corner = lax.ppermute(corner, "site", onward)
    left_bcorner = lax.ppermute(bcorner, "site", onward)
    wv = edge_proj(edge, bedge, proj)
    routed = routed_by_tiles if m % (n * TILE) == 0 and m % (sites * TILE) == 0 else routed_by_rows
    new_corner, new_b, shares = routed(turn, left_corner, left_bcorner, wv, joining, n, sites)
    summed = shares[0].astype(jnp.float32)
    for share in shares[1:]:
        summed = summed + share.astype(jnp.float32)
    return (new_corner, new_b, summed)


def solution(mesh):
    in_specs = (
        P("site", "blk", None, None),
        P(None, "site", "blk", None, None),
        P("site", "blk", None, None),
        P("site", "blk", None, None),
        P("site", "blk", None, None),
        P("site", None),
        P(),
    )
    out_specs = (
        P("site", "blk", None, None),
        P(None, "site", "blk", None, None),
        P(None, "blk", "site", None),
    )
    return jax.shard_map(
        per_device, mesh=mesh, in_specs=in_specs, out_specs=out_specs, check_vma=False
    )
```

```python
import functools

import jax
import jax.numpy as jnp
from jax import lax
from jax.experimental import pallas as pl
from jax.experimental.pallas import tpu as pltpu
from jax.sharding import PartitionSpec as P

epsilon = 1e-06
TILE = 16
AHEAD = 2
VMEM = pl.BlockSpec(memory_space=pltpu.VMEM)
SMEM = pl.BlockSpec(memory_space=pltpu.SMEM)
HBM = pl.BlockSpec(memory_space=pltpu.HBM)


def far_first(n):
    far, near = range(n // 2, n), range(n // 2 - 1, 0, -1)
    return (0, *sorted(far, key=lambda k: (k & 1, -k)), *near)


def all_swapped(parts, steps, axis):
    n = len(parts)
    return [lax.ppermute(part, axis, [(i, i ^ k) for i in range(n)]) if k else part for part, k in zip(parts, steps)]


def edge_proj_kernel(edge, bedge, proj, wv_ref, edge_buf, bedge_buf, proj_buf, sems):
    slots = proj.shape[1]
    pairs = ((proj, proj_buf), (edge, edge_buf), (bedge, bedge_buf))
    copies = [
        [pltpu.make_async_copy(src.at[0, i], buf.at[i], sems.at[3 * i + a]) for a, (src, buf) in enumerate(pairs)]
        for i in range(slots)
    ]
    for group in copies[:AHEAD]:
        for copy in group:
            copy.start()
    dot = functools.partial(jnp.dot, preferred_element_type=jnp.float32)
    for i, (first, second, third) in enumerate(copies):
        for group in copies[i + AHEAD : i + AHEAD + 1]:
            for copy in group:
                copy.start()
        first.wait()
        second.wait()
        wv_ref[2 * i] = dot(edge_buf[i], proj_buf[i]).astype(wv_ref.dtype)
        third.wait()
        wv_ref[2 * i + 1] = dot(bedge_buf[i], proj_buf[i]).astype(wv_ref.dtype)


def edge_proj(edge, bedge, proj):
    _, slots, m, k = edge.shape
    return pl.pallas_call(
        edge_proj_kernel,
        out_shape=jax.ShapeDtypeStruct((2 * slots, m, m), jnp.bfloat16),
        in_specs=[HBM] * 3,
        out_specs=VMEM,
        scratch_shapes=[
            pltpu.VMEM((slots, m, k), jnp.bfloat16),
            pltpu.VMEM((slots, m, k), jnp.bfloat16),
            pltpu.VMEM((slots, k, m), jnp.bfloat16),
            pltpu.SemaphoreType.DMA((3 * slots,)),
        ],
        cost_estimate=pl.CostEstimate(
            flops=4 * slots * m * k * m, bytes_accessed=6 * slots * m * k, transcendentals=0
        ),
        compiler_params=pltpu.CompilerParams(vmem_limit_bytes=52 << 20),
        name="edge_proj",
    )(edge, bedge, proj)


def small_call(kernel, out_shape, in_specs, scratch, name):
    return pl.pallas_call(
        kernel,
        out_shape=out_shape,
        in_specs=in_specs,
        out_specs=jax.tree.map(lambda _: VMEM, out_shape),
        scratch_shapes=scratch,
        cost_estimate=pl.CostEstimate(flops=1 << 28, bytes_accessed=1 << 20, transcendentals=0),
        compiler_params=pltpu.CompilerParams(vmem_limit_bytes=24 << 20),
        name=name,
    )


def blocks_of(turn, corner, bcorner, w, v):
    cosine, sine = turn
    dot = functools.partial(jnp.dot, preferred_element_type=jnp.float32)
    ground = dot(corner, w).astype(jnp.bfloat16)
    real_term = dot(bcorner[0], w)
    imag_term = dot(bcorner[1], w)
    re = cosine * real_term - sine * imag_term + dot(corner, v)
    im = sine * real_term + cosine * imag_term
    return ground, re.astype(jnp.bfloat16), im.astype(jnp.bfloat16)


def spread_kernel(steps, here, turn, corner, bcorner, wv, *refs):
    n = len(steps)
    out, stage = refs[:n], refs[n]
    slots, m = corner.shape[1], corner.shape[2]
    rows = m // n
    top = jnp.zeros((m, m), jnp.float32)
    for i in range(slots):
        b_here = (bcorner[0, 0, i], bcorner[1, 0, i])
        blocks = blocks_of((turn[0], turn[1]), corner[0, i], b_here, wv[2 * i], wv[2 * i + 1])
        top = jnp.maximum(top, jnp.abs(blocks[0].astype(jnp.float32)))
        for kind in range(3):
            stage[3 * i + kind] = blocks[kind]
    peak = jnp.full((TILE, m), jnp.max(top), jnp.float32).astype(jnp.bfloat16)
    for p, k in enumerate(steps):
        first = pl.multiple_of(jnp.bitwise_xor(here[0], k) * rows, rows)
        for b in range(3 * slots):
            out[p][b * rows : (b + 1) * rows] = stage[b, pl.ds(first, rows)]
        out[p][3 * slots * rows :] = peak


def route_kernel(steps, slots, here, joining, *refs):
    n = len(steps)
    pieces, out, held = refs[:n], refs[n : 2 * n], refs[2 * n]
    size = held.shape[1]
    for p, k in enumerate(steps):
        d = jnp.bitwise_xor(here[0], k)
        for i in range(slots):
            held[d * slots + i] = pieces[p][i * size : (i + 1) * size]
    top = functools.reduce(jnp.maximum, [piece[slots * size :].astype(jnp.float32) for piece in pieces])
    divisor = jnp.concatenate([top] * (size // TILE), axis=0) + epsilon
    for p, k in enumerate(steps):
        t = jnp.bitwise_xor(here[0], k)
        for i in range(slots):
            q = joining[0, t * slots + i]
            out[p][i * size : (i + 1) * size] = (held[q].astype(jnp.float32) / divisor).astype(jnp.bfloat16)


def share_kernel(steps, site_steps, here, *refs):
    n, sites = len(steps), len(site_steps)
    pieces, shares, stage = refs[:n], refs[n : n + sites], refs[n + sites]
    _, slots, wide, m = shares[0].shape
    rows = m // n
    for p, k in enumerate(steps):
        first = pl.multiple_of(jnp.bitwise_xor(here[0], k) * rows, rows)
        for i in range(slots):
            for c in range(2):
                at = (3 * i + 1 + c) * rows
                stage[c, i, pl.ds(first, rows)] = pieces[p][at : at + rows]
    for p, k in enumerate(site_steps):
        first = pl.multiple_of(jnp.bitwise_xor(here[1], k) * wide, wide)
        for i in range(slots):
            for c in range(2):
                shares[p][c, i] = stage[c, i, pl.ds(first, wide)]


def join_kernel(steps, here, *refs):
    n = len(steps)
    pieces, new_corner, new_b = refs[:n], refs[n], refs[n + 1]
    _, slots, m, _ = new_corner.shape
    rows = m // n
    for p, k in enumerate(steps):
        first = pl.multiple_of(jnp.bitwise_xor(here[0], k) * rows, rows)
        for i in range(slots):
            at = 3 * i * rows
            new_corner[0, i, pl.ds(first, rows)] = pieces[p][at : at + rows]
            for c in range(2):
                at = (3 * i + 1 + c) * rows
                new_b[c, 0, i, pl.ds(first, rows)] = pieces[p][at : at + rows]


def routed_by_tiles(turn, corner, bcorner, wv, joining, n, sites):
    _, slots, m, _ = corner.shape
    rows = m // n
    shape = lambda *dims: jax.ShapeDtypeStruct(dims, jnp.bfloat16)
    scratch = lambda *dims: [pltpu.VMEM(dims, jnp.bfloat16)]
    bind = functools.partial
    steps, site_steps = far_first(n), far_first(sites)
    here = jnp.stack([lax.axis_index("blk"), lax.axis_index("site")]).astype(jnp.int32)
    pieces = [shape(3 * slots * rows + TILE, m)] * n
    kept = scratch(3 * slots, m, m)
    parts = small_call(bind(spread_kernel, steps), pieces, [SMEM] * 2 + [VMEM] * 3, kept, "spread")(
        here, turn, corner, bcorner, wv
    )
    parts = all_swapped(parts, steps, "blk")
    pieces = [shape(3 * slots * rows, m)] * n
    kept = scratch(n * slots, 3 * rows, m)
    parts = small_call(bind(route_kernel, steps, slots), pieces, [SMEM] * 2 + [VMEM] * n, kept, "route")(
        here, joining, *parts
    )
    parts = all_swapped(parts, steps, "blk")
    ins = [SMEM] + [VMEM] * n
    pieces = [shape(2, slots, m // sites, m)] * sites
    shares = small_call(bind(share_kernel, steps, site_steps), pieces, ins, scratch(2, slots, m, m), "share")(here, *parts)
    shares = all_swapped(shares, site_steps, "site")
    pieces = [shape(1, slots, m, m), shape(2, 1, slots, m, m)]
    new_corner, new_b = small_call(bind(join_kernel, steps), pieces, ins, [], "join")(here, *parts)
    return new_corner, new_b, shares


def transposed(pieces):
    return lax.all_to_all(pieces, "blk", 0, 0, tiled=True)


def routed_by_rows(turn, corner, bcorner, wv, joining, n, sites):
    _, slots, m, _ = corner.shape
    rows = m // n
    wv = wv.reshape(slots, 2, m, m)
    ground, re, im = jax.vmap(lambda c, b, x: blocks_of((turn[0], turn[1]), c, b, x[0], x[1]))(
        corner[0], jnp.moveaxis(bcorner[:, 0], 0, 1), wv
    )
    peak = lax.pmax(jnp.max(jnp.abs(ground)).astype(jnp.float32), "blk")
    blocks = jnp.moveaxis(jnp.stack([ground, re, im], axis=1).reshape(slots, 3, n, rows, m), 2, 0)
    pieces = transposed(blocks).reshape(n * slots, 3, rows, m)
    scaled = (pieces[joining[0]].astype(jnp.float32) / (peak + epsilon)).astype(jnp.bfloat16)
    final = transposed(scaled.reshape(n, slots, 3, rows, m))
    new = jnp.transpose(final, (2, 1, 0, 3, 4)).reshape(3, slots, m, m)
    shares = jnp.moveaxis(new[1:].reshape(2, slots, sites, m // sites, m), 2, 0)
    shares = lax.all_to_all(shares, "site", 0, 0, tiled=True)
    return new[0][None], new[1:][:, None], [shares[i] for i in range(sites)]


def per_device(corner, bcorner, edge, bedge, proj, joining, momentum):
    m = corner.shape[2]
    n, sites = lax.axis_size("blk"), lax.axis_size("site")
    angle = momentum[0] * lax.axis_index("site").astype(jnp.float32)
    turn = jnp.stack([jnp.cos(angle), jnp.sin(angle)])
    onward = [(i, (i + 1) % sites) for i in range(sites)]
    left_corner = lax.ppermute(corner, "site", onward)
    left_bcorner = lax.ppermute(bcorner, "site", onward)
    wv = edge_proj(edge, bedge, proj)
    routed = routed_by_tiles if m % (n * TILE) == 0 and m % (sites * TILE) == 0 else routed_by_rows
    new_corner, new_b, shares = routed(turn, left_corner, left_bcorner, wv, joining, n, sites)
    summed = shares[0].astype(jnp.float32)
    for share in shares[1:]:
        summed = summed + share.astype(jnp.float32)
    return (new_corner, new_b, summed)


def solution(mesh):
    in_specs = (
        P("site", "blk", None, None),
        P(None, "site", "blk", None, None),
        P("site", "blk", None, None),
        P("site", "blk", None, None),
        P("site", "blk", None, None),
        P("site", None),
        P(),
    )
    out_specs = (
        P("site", "blk", None, None),
        P(None, "site", "blk", None, None),
        P(None, "blk", "site", None),
    )
    return jax.shard_map(
        per_device, mesh=mesh, in_specs=in_specs, out_specs=out_specs, check_vma=False
    )
```

```python
import functools

import jax
import jax.numpy as jnp
from jax import lax
from jax.experimental import pallas as pl
from jax.experimental.pallas import tpu as pltpu
from jax.sharding import PartitionSpec as P

epsilon = 1e-06
TILE = 16
AHEAD = 2
VMEM = pl.BlockSpec(memory_space=pltpu.VMEM)
SMEM = pl.BlockSpec(memory_space=pltpu.SMEM)
HBM = pl.BlockSpec(memory_space=pltpu.HBM)


def far_first(n):
    far, near = range(n // 2, n), range(n // 2 - 1, 0, -1)
    return (0, *sorted(far, key=lambda k: (k & 1, -k)), *near)


def all_swapped(parts, steps, axis):
    n = len(parts)
    return [lax.ppermute(part, axis, [(i, i ^ k) for i in range(n)]) if k else part for part, k in zip(parts, steps)]


def edge_proj_kernel(edge, bedge, proj, wv_ref, edge_buf, bedge_buf, proj_buf, sems):
    slots = proj.shape[1]
    pairs = ((proj, proj_buf), (edge, edge_buf), (bedge, bedge_buf))
    copies = [
        [pltpu.make_async_copy(src.at[0, i], buf.at[i], sems.at[3 * i + a]) for a, (src, buf) in enumerate(pairs)]
        for i in range(slots)
    ]
    for group in copies[:AHEAD]:
        for copy in group:
            copy.start()
    dot = functools.partial(jnp.dot, preferred_element_type=jnp.float32)
    for i, (first, second, third) in enumerate(copies):
        for group in copies[i + AHEAD : i + AHEAD + 1]:
            for copy in group:
                copy.start()
        first.wait()
        second.wait()
        wv_ref[2 * i] = dot(edge_buf[i], proj_buf[i]).astype(wv_ref.dtype)
        third.wait()
        wv_ref[2 * i + 1] = dot(bedge_buf[i], proj_buf[i]).astype(wv_ref.dtype)


def edge_proj(edge, bedge, proj):
    _, slots, m, k = edge.shape
    return pl.pallas_call(
        edge_proj_kernel,
        out_shape=jax.ShapeDtypeStruct((2 * slots, m, m), jnp.bfloat16),
        in_specs=[HBM] * 3,
        out_specs=VMEM,
        scratch_shapes=[
            pltpu.VMEM((slots, m, k), jnp.bfloat16),
            pltpu.VMEM((slots, m, k), jnp.bfloat16),
            pltpu.VMEM((slots, k, m), jnp.bfloat16),
            pltpu.SemaphoreType.DMA((3 * slots,)),
        ],
        cost_estimate=pl.CostEstimate(
            flops=4 * slots * m * k * m, bytes_accessed=6 * slots * m * k, transcendentals=0
        ),
        compiler_params=pltpu.CompilerParams(vmem_limit_bytes=52 << 20),
        name="edge_proj",
    )(edge, bedge, proj)


def small_call(kernel, out_shape, in_specs, scratch, name):
    return pl.pallas_call(
        kernel,
        out_shape=out_shape,
        in_specs=in_specs,
        out_specs=jax.tree.map(lambda _: VMEM, out_shape),
        scratch_shapes=scratch,
        cost_estimate=pl.CostEstimate(flops=1 << 28, bytes_accessed=1 << 20, transcendentals=0),
        compiler_params=pltpu.CompilerParams(vmem_limit_bytes=24 << 20),
        name=name,
    )


def blocks_of(turn, corner, bcorner, w, v):
    cosine, sine = turn
    dot = functools.partial(jnp.dot, preferred_element_type=jnp.float32)
    ground = dot(corner, w).astype(jnp.bfloat16)
    real_term = dot(bcorner[0], w)
    imag_term = dot(bcorner[1], w)
    re = cosine * real_term - sine * imag_term + dot(corner, v)
    im = sine * real_term + cosine * imag_term
    return ground, re.astype(jnp.bfloat16), im.astype(jnp.bfloat16)


def spread_kernel(steps, here, turn, corner, bcorner, wv, *refs):
    n = len(steps)
    out, stage = refs[:n], refs[n]
    slots, m = corner.shape[1], corner.shape[2]
    rows = m // n
    top = jnp.zeros((m, m), jnp.float32)
    for i in range(slots):
        b_here = (bcorner[0, 0, i], bcorner[1, 0, i])
        blocks = blocks_of((turn[0], turn[1]), corner[0, i], b_here, wv[2 * i], wv[2 * i + 1])
        top = jnp.maximum(top, jnp.abs(blocks[0].astype(jnp.float32)))
        for kind in range(3):
            stage[3 * i + kind] = blocks[kind]
    peak = jnp.full((TILE, m), jnp.max(top), jnp.float32).astype(jnp.bfloat16)
    for p, k in enumerate(steps):
        first = pl.multiple_of(jnp.bitwise_xor(here[0], k) * rows, rows)
        for b in range(3 * slots):
            out[p][b * rows : (b + 1) * rows] = stage[b, pl.ds(first, rows)]
        out[p][3 * slots * rows :] = peak


def route_kernel(steps, slots, here, joining, *refs):
    n = len(steps)
    pieces, out, held = refs[:n], refs[n : 2 * n], refs[2 * n]
    size = held.shape[1]
    for p, k in enumerate(steps):
        d = jnp.bitwise_xor(here[0], k)
        for i in range(slots):
            held[d * slots + i] = pieces[p][i * size : (i + 1) * size]
    top = functools.reduce(jnp.maximum, [piece[slots * size :].astype(jnp.float32) for piece in pieces])
    divisor = jnp.concatenate([top] * (size // TILE), axis=0) + epsilon
    for p, k in enumerate(steps):
        t = jnp.bitwise_xor(here[0], k)
        for i in range(slots):
            q = joining[0, t * slots + i]
            out[p][i * size : (i + 1) * size] = (held[q].astype(jnp.float32) / divisor).astype(jnp.bfloat16)


def share_kernel(steps, here, *refs):
    n = len(steps)
    pieces, kept, away, stage = refs[:n], refs[n], refs[n + 1], refs[n + 2]
    _, _, slots, wide, m = kept.shape
    rows = m // n
    for p, k in enumerate(steps):
        first = pl.multiple_of(jnp.bitwise_xor(here[0], k) * rows, rows)
        for i in range(slots):
            for c in range(2):
                at = (3 * i + 1 + c) * rows
                stage[c, i, pl.ds(first, rows)] = pieces[p][at : at + rows]
    for out, place, k in ((away, 0, 1), (away, 1, 3), (kept, 0, 0), (kept, 1, 2)):
        first = pl.multiple_of(jnp.bitwise_xor(here[1], k) * wide, wide)
        for i in range(slots):
            for c in range(2):
                out[place, c, i] = stage[c, i, pl.ds(first, wide)]


def join_kernel(steps, here, *refs):
    n = len(steps)
    pieces, new_corner, new_b = refs[:n], refs[n], refs[n + 1]
    _, slots, m, _ = new_corner.shape
    rows = m // n
    for p, k in enumerate(steps):
        first = pl.multiple_of(jnp.bitwise_xor(here[0], k) * rows, rows)
        for i in range(slots):
            at = 3 * i * rows
            new_corner[0, i, pl.ds(first, rows)] = pieces[p][at : at + rows]
            for c in range(2):
                at = (3 * i + 1 + c) * rows
                new_b[c, 0, i, pl.ds(first, rows)] = pieces[p][at : at + rows]


def routed_by_tiles(turn, corner, bcorner, wv, joining, n, sites):
    _, slots, m, _ = corner.shape
    rows = m // n
    shape = lambda *dims: jax.ShapeDtypeStruct(dims, jnp.bfloat16)
    scratch = lambda *dims: [pltpu.VMEM(dims, jnp.bfloat16)]
    bind = functools.partial
    steps = far_first(n)
    here = jnp.stack([lax.axis_index("blk"), lax.axis_index("site")]).astype(jnp.int32)
    pieces = [shape(3 * slots * rows + TILE, m)] * n
    kept = scratch(3 * slots, m, m)
    parts = small_call(bind(spread_kernel, steps), pieces, [SMEM] * 2 + [VMEM] * 3, kept, "spread")(
        here, turn, corner, bcorner, wv
    )
    parts = all_swapped(parts, steps, "blk")
    pieces = [shape(3 * slots * rows, m)] * n
    kept = scratch(n * slots, 3 * rows, m)
    parts = small_call(bind(route_kernel, steps, slots), pieces, [SMEM] * 2 + [VMEM] * n, kept, "route")(
        here, joining, *parts
    )
    parts = all_swapped(parts, steps, "blk")
    ins = [SMEM] + [VMEM] * n
    pieces = [shape(2, 2, slots, m // sites, m)] * 2
    kept, away = small_call(bind(share_kernel, steps), pieces, ins, scratch(2, slots, m, m), "share")(here, *parts)
    came = lax.ppermute(away, "site", [(i, i ^ 1) for i in range(sites)])
    partial = kept.astype(jnp.float32) + came.astype(jnp.float32)
    came = lax.ppermute(partial[1].astype(jnp.bfloat16), "site", [(i, i ^ 2) for i in range(sites)])
    pieces = [shape(1, slots, m, m), shape(2, 1, slots, m, m)]
    new_corner, new_b = small_call(bind(join_kernel, steps), pieces, ins, [], "join")(here, *parts)
    return new_corner, new_b, partial[0] + came.astype(jnp.float32)


def transposed(pieces):
    return lax.all_to_all(pieces, "blk", 0, 0, tiled=True)


def routed_by_rows(turn, corner, bcorner, wv, joining, n, sites):
    _, slots, m, _ = corner.shape
    rows = m // n
    wv = wv.reshape(slots, 2, m, m)
    ground, re, im = jax.vmap(lambda c, b, x: blocks_of((turn[0], turn[1]), c, b, x[0], x[1]))(
        corner[0], jnp.moveaxis(bcorner[:, 0], 0, 1), wv
    )
    peak = lax.pmax(jnp.max(jnp.abs(ground)).astype(jnp.float32), "blk")
    blocks = jnp.moveaxis(jnp.stack([ground, re, im], axis=1).reshape(slots, 3, n, rows, m), 2, 0)
    pieces = transposed(blocks).reshape(n * slots, 3, rows, m)
    scaled = (pieces[joining[0]].astype(jnp.float32) / (peak + epsilon)).astype(jnp.bfloat16)
    final = transposed(scaled.reshape(n, slots, 3, rows, m))
    new = jnp.transpose(final, (2, 1, 0, 3, 4)).reshape(3, slots, m, m)
    shares = jnp.moveaxis(new[1:].reshape(2, slots, sites, m // sites, m), 2, 0)
    shares = lax.all_to_all(shares, "site", 0, 0, tiled=True)
    return new[0][None], new[1:][:, None], jnp.sum(shares.astype(jnp.float32), axis=0)


def per_device(corner, bcorner, edge, bedge, proj, joining, momentum):
    m = corner.shape[2]
    n, sites = lax.axis_size("blk"), lax.axis_size("site")
    angle = momentum[0] * lax.axis_index("site").astype(jnp.float32)
    turn = jnp.stack([jnp.cos(angle), jnp.sin(angle)])
    onward = [(i, (i + 1) % sites) for i in range(sites)]
    left_bcorner = lax.ppermute(bcorner, "site", onward)
    left_corner = lax.ppermute(corner, "site", [(i, i ^ 1) for i in range(sites)])
    left_corner = lax.ppermute(left_corner, "site", [(i, i if i % 2 else (i + 2) % sites) for i in range(sites)])
    wv = edge_proj(edge, bedge, proj)
    routed = routed_by_tiles if m % (n * TILE) == 0 and sites == 4 else routed_by_rows
    return routed(turn, left_corner, left_bcorner, wv, joining, n, sites)


def solution(mesh):
    in_specs = (
        P("site", "blk", None, None),
        P(None, "site", "blk", None, None),
        P("site", "blk", None, None),
        P("site", "blk", None, None),
        P("site", "blk", None, None),
        P("site", None),
        P(),
    )
    out_specs = (
        P("site", "blk", None, None),
        P(None, "site", "blk", None, None),
        P(None, "blk", "site", None),
    )
    return jax.shard_map(
        per_device, mesh=mesh, in_specs=in_specs, out_specs=out_specs, check_vma=False
    )
```

```python
import functools

import jax
import jax.numpy as jnp
from jax import lax
from jax.experimental import pallas as pl
from jax.experimental.pallas import tpu as pltpu
from jax.sharding import PartitionSpec as P

epsilon = 1e-06
TILE = 16
AHEAD = 2
VMEM = pl.BlockSpec(memory_space=pltpu.VMEM)
SMEM = pl.BlockSpec(memory_space=pltpu.SMEM)
HBM = pl.BlockSpec(memory_space=pltpu.HBM)


def start_order(n):
    far = sorted(range(n // 2, n), key=lambda k: (k & 1, -k))
    return (0, far[0], 1, *far[1:], *range(2, n // 2))


def all_swapped(parts, steps, axis):
    n = len(parts)
    return [lax.ppermute(part, axis, [(i, i ^ k) for i in range(n)]) if k else part for part, k in zip(parts, steps)]


def edge_proj_kernel(edge, bedge, proj, wv_ref, edge_buf, bedge_buf, proj_buf, sems):
    slots = proj.shape[1]
    pairs = ((proj, proj_buf), (edge, edge_buf), (bedge, bedge_buf))
    copies = [
        [pltpu.make_async_copy(src.at[0, i], buf.at[i], sems.at[3 * i + a]) for a, (src, buf) in enumerate(pairs)]
        for i in range(slots)
    ]
    for group in copies[:AHEAD]:
        for copy in group:
            copy.start()
    dot = functools.partial(jnp.dot, preferred_element_type=jnp.float32)
    for i, (first, second, third) in enumerate(copies):
        for group in copies[i + AHEAD : i + AHEAD + 1]:
            for copy in group:
                copy.start()
        first.wait()
        second.wait()
        wv_ref[2 * i] = dot(edge_buf[i], proj_buf[i]).astype(wv_ref.dtype)
        third.wait()
        wv_ref[2 * i + 1] = dot(bedge_buf[i], proj_buf[i]).astype(wv_ref.dtype)


def edge_proj(edge, bedge, proj):
    _, slots, m, k = edge.shape
    return pl.pallas_call(
        edge_proj_kernel,
        out_shape=jax.ShapeDtypeStruct((2 * slots, m, m), jnp.bfloat16),
        in_specs=[HBM] * 3,
        out_specs=VMEM,
        scratch_shapes=[
            pltpu.VMEM((slots, m, k), jnp.bfloat16),
            pltpu.VMEM((slots, m, k), jnp.bfloat16),
            pltpu.VMEM((slots, k, m), jnp.bfloat16),
            pltpu.SemaphoreType.DMA((3 * slots,)),
        ],
        cost_estimate=pl.CostEstimate(
            flops=4 * slots * m * k * m, bytes_accessed=6 * slots * m * k, transcendentals=0
        ),
        compiler_params=pltpu.CompilerParams(vmem_limit_bytes=52 << 20),
        name="edge_proj",
    )(edge, bedge, proj)


def small_call(kernel, out_shape, in_specs, scratch, name):
    return pl.pallas_call(
        kernel,
        out_shape=out_shape,
        in_specs=in_specs,
        out_specs=jax.tree.map(lambda _: VMEM, out_shape),
        scratch_shapes=scratch,
        cost_estimate=pl.CostEstimate(flops=1 << 28, bytes_accessed=1 << 20, transcendentals=0),
        compiler_params=pltpu.CompilerParams(vmem_limit_bytes=24 << 20),
        name=name,
    )


def blocks_of(turn, corner, bcorner, w, v):
    cosine, sine = turn
    dot = functools.partial(jnp.dot, preferred_element_type=jnp.float32)
    ground = dot(corner, w).astype(jnp.bfloat16)
    real_term = dot(bcorner[0], w)
    imag_term = dot(bcorner[1], w)
    re = cosine * real_term - sine * imag_term + dot(corner, v)
    im = sine * real_term + cosine * imag_term
    return ground, re.astype(jnp.bfloat16), im.astype(jnp.bfloat16)


def spread_kernel(steps, here, turn, corner, bcorner, wv, *refs):
    n = len(steps)
    out, stage = refs[:n], refs[n]
    slots, m = corner.shape[1], corner.shape[2]
    rows = m // n
    top = jnp.zeros((m, m), jnp.float32)
    for i in range(slots):
        b_here = (bcorner[0, 0, i], bcorner[1, 0, i])
        blocks = blocks_of((turn[0], turn[1]), corner[0, i], b_here, wv[2 * i], wv[2 * i + 1])
        top = jnp.maximum(top, jnp.abs(blocks[0].astype(jnp.float32)))
        for kind in range(3):
            stage[3 * i + kind] = blocks[kind]
    peak = jnp.full((TILE, m), jnp.max(top), jnp.float32).astype(jnp.bfloat16)
    for p, k in enumerate(steps):
        first = pl.multiple_of(jnp.bitwise_xor(here[0], k) * rows, rows)
        for b in range(3 * slots):
            out[p][b * rows : (b + 1) * rows] = stage[b, pl.ds(first, rows)]
        out[p][3 * slots * rows :] = peak


def route_kernel(steps, slots, here, joining, *refs):
    n = len(steps)
    pieces, out, held = refs[:n], refs[n : 2 * n], refs[2 * n]
    size = held.shape[1]
    for p, k in enumerate(steps):
        d = jnp.bitwise_xor(here[0], k)
        for i in range(slots):
            held[d * slots + i] = pieces[p][i * size : (i + 1) * size]
    top = functools.reduce(jnp.maximum, [piece[slots * size :].astype(jnp.float32) for piece in pieces])
    divisor = jnp.concatenate([top] * (size // TILE), axis=0) + epsilon
    for p, k in enumerate(steps):
        t = jnp.bitwise_xor(here[0], k)
        for i in range(slots):
            q = joining[0, t * slots + i]
            out[p][i * size : (i + 1) * size] = (held[q].astype(jnp.float32) / divisor).astype(jnp.bfloat16)


def share_kernel(steps, here, *refs):
    n = len(steps)
    pieces, kept, away, stage = refs[:n], refs[n], refs[n + 1], refs[n + 2]
    _, _, slots, wide, m = kept.shape
    rows = m // n
    for p, k in enumerate(steps):
        first = pl.multiple_of(jnp.bitwise_xor(here[0], k) * rows, rows)
        for i in range(slots):
            for c in range(2):
                at = (3 * i + 1 + c) * rows
                stage[c, i, pl.ds(first, rows)] = pieces[p][at : at + rows]
    for out, place, k in ((away, 0, 1), (away, 1, 3), (kept, 0, 0), (kept, 1, 2)):
        first = pl.multiple_of(jnp.bitwise_xor(here[1], k) * wide, wide)
        for i in range(slots):
            for c in range(2):
                out[place, c, i] = stage[c, i, pl.ds(first, wide)]


def join_kernel(steps, here, *refs):
    n = len(steps)
    pieces, new_corner, new_b = refs[:n], refs[n], refs[n + 1]
    _, slots, m, _ = new_corner.shape
    rows = m // n
    for p, k in enumerate(steps):
        first = pl.multiple_of(jnp.bitwise_xor(here[0], k) * rows, rows)
        for i in range(slots):
            at = 3 * i * rows
            new_corner[0, i, pl.ds(first, rows)] = pieces[p][at : at + rows]
            for c in range(2):
                at = (3 * i + 1 + c) * rows
                new_b[c, 0, i, pl.ds(first, rows)] = pieces[p][at : at + rows]


def routed_by_tiles(turn, corner, bcorner, wv, joining, n, sites):
    _, slots, m, _ = corner.shape
    rows = m // n
    shape = lambda *dims: jax.ShapeDtypeStruct(dims, jnp.bfloat16)
    scratch = lambda *dims: [pltpu.VMEM(dims, jnp.bfloat16)]
    bind = functools.partial
    steps = start_order(n)
    here = jnp.stack([lax.axis_index("blk"), lax.axis_index("site")]).astype(jnp.int32)
    pieces = [shape(3 * slots * rows + TILE, m)] * n
    kept = scratch(3 * slots, m, m)
    parts = small_call(bind(spread_kernel, steps), pieces, [SMEM] * 2 + [VMEM] * 3, kept, "spread")(
        here, turn, corner, bcorner, wv
    )
    parts = all_swapped(parts, steps, "blk")
    pieces = [shape(3 * slots * rows, m)] * n
    kept = scratch(n * slots, 3 * rows, m)
    parts = small_call(bind(route_kernel, steps, slots), pieces, [SMEM] * 2 + [VMEM] * n, kept, "route")(
        here, joining, *parts
    )
    parts = all_swapped(parts, steps, "blk")
    ins = [SMEM] + [VMEM] * n
    pieces = [shape(2, 2, slots, m // sites, m)] * 2
    kept, away = small_call(bind(share_kernel, steps), pieces, ins, scratch(2, slots, m, m), "share")(here, *parts)
    came = lax.ppermute(away, "site", [(i, i ^ 1) for i in range(sites)])
    partial = kept.astype(jnp.float32) + came.astype(jnp.float32)
    came = lax.ppermute(partial[1].astype(jnp.bfloat16), "site", [(i, i ^ 2) for i in range(sites)])
    pieces = [shape(1, slots, m, m), shape(2, 1, slots, m, m)]
    new_corner, new_b = small_call(bind(join_kernel, steps), pieces, ins, [], "join")(here, *parts)
    return new_corner, new_b, partial[0] + came.astype(jnp.float32)


def transposed(pieces):
    return lax.all_to_all(pieces, "blk", 0, 0, tiled=True)


def routed_by_rows(turn, corner, bcorner, wv, joining, n, sites):
    _, slots, m, _ = corner.shape
    rows = m // n
    wv = wv.reshape(slots, 2, m, m)
    ground, re, im = jax.vmap(lambda c, b, x: blocks_of((turn[0], turn[1]), c, b, x[0], x[1]))(
        corner[0], jnp.moveaxis(bcorner[:, 0], 0, 1), wv
    )
    peak = lax.pmax(jnp.max(jnp.abs(ground)).astype(jnp.float32), "blk")
    blocks = jnp.moveaxis(jnp.stack([ground, re, im], axis=1).reshape(slots, 3, n, rows, m), 2, 0)
    pieces = transposed(blocks).reshape(n * slots, 3, rows, m)
    scaled = (pieces[joining[0]].astype(jnp.float32) / (peak + epsilon)).astype(jnp.bfloat16)
    final = transposed(scaled.reshape(n, slots, 3, rows, m))
    new = jnp.transpose(final, (2, 1, 0, 3, 4)).reshape(3, slots, m, m)
    shares = jnp.moveaxis(new[1:].reshape(2, slots, sites, m // sites, m), 2, 0)
    shares = lax.all_to_all(shares, "site", 0, 0, tiled=True)
    return new[0][None], new[1:][:, None], jnp.sum(shares.astype(jnp.float32), axis=0)


def per_device(corner, bcorner, edge, bedge, proj, joining, momentum):
    m = corner.shape[2]
    n, sites = lax.axis_size("blk"), lax.axis_size("site")
    angle = momentum[0] * lax.axis_index("site").astype(jnp.float32)
    turn = jnp.stack([jnp.cos(angle), jnp.sin(angle)])
    onward = [(i, (i + 1) % sites) for i in range(sites)]
    left_bcorner = lax.ppermute(bcorner, "site", onward)
    left_corner = lax.ppermute(corner, "site", [(i, i ^ 1) for i in range(sites)])
    left_corner = lax.ppermute(left_corner, "site", [(i, i if i % 2 else (i + 2) % sites) for i in range(sites)])
    wv = edge_proj(edge, bedge, proj)
    routed = routed_by_tiles if m % (n * TILE) == 0 and sites == 4 else routed_by_rows
    return routed(turn, left_corner, left_bcorner, wv, joining, n, sites)


def solution(mesh):
    in_specs = (
        P("site", "blk", None, None),
        P(None, "site", "blk", None, None),
        P("site", "blk", None, None),
        P("site", "blk", None, None),
        P("site", "blk", None, None),
        P("site", None),
        P(),
    )
    out_specs = (
        P("site", "blk", None, None),
        P(None, "site", "blk", None, None),
        P(None, "blk", "site", None),
    )
    return jax.shard_map(
        per_device, mesh=mesh, in_specs=in_specs, out_specs=out_specs, check_vma=False
    )
```

```python
import functools

import jax
import jax.numpy as jnp
from jax import lax
from jax.experimental import pallas as pl
from jax.experimental.pallas import tpu as pltpu
from jax.sharding import PartitionSpec as P

epsilon = 1e-06
TILE = 16
FIRST = (6, 4)
AHEAD = 2
VMEM = pl.BlockSpec(memory_space=pltpu.VMEM)
SMEM = pl.BlockSpec(memory_space=pltpu.SMEM)
HBM = pl.BlockSpec(memory_space=pltpu.HBM)


def start_order(n):
    far = sorted(range(n // 2, n), key=lambda k: (k & 1, -k))
    return (0, far[0], 1, *far[1:], *range(2, n // 2))


def piece_start(j, m, n, sites):
    return pl.multiple_of(lax.rem(j, sites) * (m // sites) + lax.div(j, sites) * (m // n), m // n)


def all_swapped(parts, steps, axis):
    n = len(parts)
    return [lax.ppermute(part, axis, [(i, i ^ k) for i in range(n)]) if k else part for part, k in zip(parts, steps)]


def edge_proj_kernel(edge, bedge, proj, wv_ref, edge_buf, bedge_buf, proj_buf, sems):
    slots = proj.shape[1]
    pairs = ((proj, proj_buf), (edge, edge_buf), (bedge, bedge_buf))
    copies = [
        [pltpu.make_async_copy(src.at[0, i], buf.at[i], sems.at[3 * i + a]) for a, (src, buf) in enumerate(pairs)]
        for i in range(slots)
    ]
    for group in copies[:AHEAD]:
        for copy in group:
            copy.start()
    dot = functools.partial(jnp.dot, preferred_element_type=jnp.float32)
    for i, (first, second, third) in enumerate(copies):
        for group in copies[i + AHEAD : i + AHEAD + 1]:
            for copy in group:
                copy.start()
        first.wait()
        second.wait()
        wv_ref[2 * i] = dot(edge_buf[i], proj_buf[i]).astype(wv_ref.dtype)
        third.wait()
        wv_ref[2 * i + 1] = dot(bedge_buf[i], proj_buf[i]).astype(wv_ref.dtype)


def edge_proj(edge, bedge, proj):
    _, slots, m, k = edge.shape
    return pl.pallas_call(
        edge_proj_kernel,
        out_shape=jax.ShapeDtypeStruct((2 * slots, m, m), jnp.bfloat16),
        in_specs=[HBM] * 3,
        out_specs=VMEM,
        scratch_shapes=[
            pltpu.VMEM((slots, m, k), jnp.bfloat16),
            pltpu.VMEM((slots, m, k), jnp.bfloat16),
            pltpu.VMEM((slots, k, m), jnp.bfloat16),
            pltpu.SemaphoreType.DMA((3 * slots,)),
        ],
        cost_estimate=pl.CostEstimate(
            flops=4 * slots * m * k * m, bytes_accessed=6 * slots * m * k, transcendentals=0
        ),
        compiler_params=pltpu.CompilerParams(vmem_limit_bytes=52 << 20),
        name="edge_proj",
    )(edge, bedge, proj)


def small_call(kernel, out_shape, in_specs, scratch, name):
    return pl.pallas_call(
        kernel,
        out_shape=out_shape,
        in_specs=in_specs,
        out_specs=jax.tree.map(lambda _: VMEM, out_shape),
        scratch_shapes=scratch,
        cost_estimate=pl.CostEstimate(flops=1 << 28, bytes_accessed=1 << 20, transcendentals=0),
        compiler_params=pltpu.CompilerParams(vmem_limit_bytes=24 << 20),
        name=name,
    )


def blocks_of(turn, corner, bcorner, w, v):
    cosine, sine = turn
    dot = functools.partial(jnp.dot, preferred_element_type=jnp.float32)
    ground = dot(corner, w).astype(jnp.bfloat16)
    real_term = dot(bcorner[0], w)
    imag_term = dot(bcorner[1], w)
    re = cosine * real_term - sine * imag_term + dot(corner, v)
    im = sine * real_term + cosine * imag_term
    return ground, re.astype(jnp.bfloat16), im.astype(jnp.bfloat16)


def spread_kernel(steps, sites, here, turn, corner, bcorner, wv, *refs):
    n = len(steps)
    out, stage = refs[:n], refs[n]
    slots, m = corner.shape[1], corner.shape[2]
    rows = m // n
    top = jnp.zeros((m, m), jnp.float32)
    for i in range(slots):
        b_here = (bcorner[0, 0, i], bcorner[1, 0, i])
        blocks = blocks_of((turn[0], turn[1]), corner[0, i], b_here, wv[2 * i], wv[2 * i + 1])
        top = jnp.maximum(top, jnp.abs(blocks[0].astype(jnp.float32)))
        for kind in range(3):
            stage[3 * i + kind] = blocks[kind]
    peak = jnp.full((TILE, m), jnp.max(top), jnp.float32).astype(jnp.bfloat16)
    for p, k in enumerate(steps):
        first = piece_start(jnp.bitwise_xor(here[0], k), m, n, sites)
        for b in range(3 * slots):
            out[p][b * rows : (b + 1) * rows] = stage[b, pl.ds(first, rows)]
        out[p][3 * slots * rows :] = peak


def route_kernel(steps, slots, here, joining, *refs):
    n = len(steps)
    pieces, out, held = refs[:n], refs[n : 2 * n], refs[2 * n]
    size = held.shape[1]
    for p, k in enumerate(steps):
        d = jnp.bitwise_xor(here[0], k)
        for i in range(slots):
            held[d * slots + i] = pieces[p][i * size : (i + 1) * size]
    top = functools.reduce(jnp.maximum, [piece[slots * size :].astype(jnp.float32) for piece in pieces])
    divisor = jnp.concatenate([top] * (size // TILE), axis=0) + epsilon
    for p, k in enumerate(steps):
        t = jnp.bitwise_xor(here[0], k)
        for i in range(slots):
            q = joining[0, t * slots + i]
            out[p][i * size : (i + 1) * size] = (held[q].astype(jnp.float32) / divisor).astype(jnp.bfloat16)


def share_kernel(steps, sites, here, *refs):
    pieces, out, stage = refs[:sites], refs[-1 - sites : -1], refs[-1]
    _, slots, rows, _ = out[0].shape
    for p, k in enumerate(steps):
        r = lax.rem(jnp.bitwise_xor(here[0], k), sites)
        for i in range(slots):
            for c in range(2):
                at = (3 * i + 1 + c) * rows
                stage[r, c, i] = pieces[p][at : at + rows]
    for k in range(sites):
        out[k][...] = stage[jnp.bitwise_xor(here[1], k)]


def sum_kernel(sites, here, *refs):
    near, far, summed = refs[:sites], refs[sites : 2 * sites], refs[2 * sites]
    _, slots, rows, _ = near[0].shape
    half = lax.div(here[0], sites)
    for shares, place in ((near, half), (far, 1 - half)):
        first = pl.multiple_of(place * rows, rows)
        for i in range(slots):
            for c in range(2):
                summed[c, i, pl.ds(first, rows)] = sum([share[c, i].astype(jnp.float32) for share in shares[1:]],
                                                       shares[0][c, i].astype(jnp.float32))


def join_kernel(steps, sites, here, *refs):
    n = len(steps)
    pieces, new_corner, new_b = refs[:n], refs[n], refs[n + 1]
    _, slots, m, _ = new_corner.shape
    rows = m // n
    for p, k in enumerate(steps):
        first = piece_start(jnp.bitwise_xor(here[0], k), m, n, sites)
        for i in range(slots):
            at = 3 * i * rows
            new_corner[0, i, pl.ds(first, rows)] = pieces[p][at : at + rows]
            for c in range(2):
                at = (3 * i + 1 + c) * rows
                new_b[c, 0, i, pl.ds(first, rows)] = pieces[p][at : at + rows]


def routed_by_tiles(turn, corner, bcorner, wv, joining, n, sites):
    _, slots, m, _ = corner.shape
    rows = m // n
    shape = lambda *dims: jax.ShapeDtypeStruct(dims, jnp.bfloat16)
    scratch = lambda *dims: [pltpu.VMEM(dims, jnp.bfloat16)]
    bind = functools.partial
    steps = start_order(n)
    here = jnp.stack([lax.axis_index("blk"), lax.axis_index("site")]).astype(jnp.int32)
    pieces = [shape(3 * slots * rows + TILE, m)] * n
    kept = scratch(3 * slots, m, m)
    parts = small_call(bind(spread_kernel, steps, sites), pieces, [SMEM] * 2 + [VMEM] * 3, kept, "spread")(
        here, turn, corner, bcorner, wv
    )
    parts = all_swapped(parts, steps, "blk")
    pieces = [shape(3 * slots * rows, m)] * n
    kept = scratch(n * slots, 3 * rows, m)
    parts = small_call(bind(route_kernel, steps, slots), pieces, [SMEM] * 2 + [VMEM] * n, kept, "route")(
        here, joining, *parts
    )
    parts = all_swapped(parts, steps, "blk")
    halves = []
    for ours in (lambda k: k < sites, lambda k: k >= sites):
        some = [(k, part) for k, part in zip(steps, parts) if ours(k)]
        share = bind(share_kernel, [k for k, _ in some], sites)
        kept = scratch(sites, 2, slots, rows, m)
        late = [] if halves else [part for k, part in zip(steps, parts) if k in FIRST]
        specs = [SMEM] + [VMEM] * sites + [pl.BlockSpec(memory_space=pl.ANY)] * len(late)
        shares = small_call(share, [shape(2, slots, rows, m)] * sites, specs, kept, "share")(
            here, *[part for _, part in some], *late
        )
        halves += all_swapped(shares, range(sites), "site")
    pieces = [shape(1, slots, m, m), shape(2, 1, slots, m, m)]
    join = bind(join_kernel, steps, sites)
    new_corner, new_b = small_call(join, pieces, [SMEM] + [VMEM] * n, [], "join")(here, *parts)
    summed = jax.ShapeDtypeStruct((2, slots, m // sites, m), jnp.float32)
    add = bind(sum_kernel, sites)
    summed = small_call(add, [summed], [SMEM] + [VMEM] * (2 * sites), [], "sum")(here, *halves)[0]
    return new_corner, new_b, summed


def transposed(pieces):
    return lax.all_to_all(pieces, "blk", 0, 0, tiled=True)


def routed_by_rows(turn, corner, bcorner, wv, joining, n, sites):
    _, slots, m, _ = corner.shape
    rows = m // n
    wv = wv.reshape(slots, 2, m, m)
    ground, re, im = jax.vmap(lambda c, b, x: blocks_of((turn[0], turn[1]), c, b, x[0], x[1]))(
        corner[0], jnp.moveaxis(bcorner[:, 0], 0, 1), wv
    )
    peak = lax.pmax(jnp.max(jnp.abs(ground)).astype(jnp.float32), "blk")
    blocks = jnp.moveaxis(jnp.stack([ground, re, im], axis=1).reshape(slots, 3, n, rows, m), 2, 0)
    pieces = transposed(blocks).reshape(n * slots, 3, rows, m)
    scaled = (pieces[joining[0]].astype(jnp.float32) / (peak + epsilon)).astype(jnp.bfloat16)
    final = transposed(scaled.reshape(n, slots, 3, rows, m))
    new = jnp.transpose(final, (2, 1, 0, 3, 4)).reshape(3, slots, m, m)
    shares = jnp.moveaxis(new[1:].reshape(2, slots, sites, m // sites, m), 2, 0)
    shares = lax.all_to_all(shares, "site", 0, 0, tiled=True)
    return new[0][None], new[1:][:, None], jnp.sum(shares.astype(jnp.float32), axis=0)


def per_device(corner, bcorner, edge, bedge, proj, joining, momentum):
    m = corner.shape[2]
    n, sites = lax.axis_size("blk"), lax.axis_size("site")
    angle = momentum[0] * lax.axis_index("site").astype(jnp.float32)
    turn = jnp.stack([jnp.cos(angle), jnp.sin(angle)])
    onward = [(i, (i + 1) % sites) for i in range(sites)]
    left_bcorner = lax.ppermute(bcorner, "site", onward)
    left_corner = lax.ppermute(corner, "site", onward)
    wv = edge_proj(edge, bedge, proj)
    routed = routed_by_tiles if m % (n * TILE) == 0 and n == 2 * sites else routed_by_rows
    return routed(turn, left_corner, left_bcorner, wv, joining, n, sites)


def solution(mesh):
    in_specs = (
        P("site", "blk", None, None),
        P(None, "site", "blk", None, None),
        P("site", "blk", None, None),
        P("site", "blk", None, None),
        P("site", "blk", None, None),
        P("site", None),
        P(),
    )
    out_specs = (
        P("site", "blk", None, None),
        P(None, "site", "blk", None, None),
        P(None, "blk", "site", None),
    )
    return jax.shard_map(
        per_device, mesh=mesh, in_specs=in_specs, out_specs=out_specs, check_vma=False
    )
```

```python
import functools

import jax
import jax.numpy as jnp
from jax import lax
from jax.experimental import pallas as pl
from jax.experimental.pallas import tpu as pltpu
from jax.sharding import PartitionSpec as P

epsilon = 1e-06
TILE = 16
FIRST = (6, 4)
AHEAD = 2
VMEM = pl.BlockSpec(memory_space=pltpu.VMEM)
ANY = pl.BlockSpec(memory_space=pl.ANY)
HBM = pl.BlockSpec(memory_space=pltpu.HBM)


def start_order(n):
    far = sorted(range(n // 2, n), key=lambda k: (k & 1, -k))
    return (0, far[0], 1, *far[1:], *range(2, n // 2))


def my_place():
    return lax.axis_index("blk"), lax.axis_index("site")


def piece_start(j, m, n, sites):
    return pl.multiple_of(lax.rem(j, sites) * (m // sites) + lax.div(j, sites) * (m // n), m // n)


def all_swapped(parts, steps, axis):
    n = len(parts)
    return [lax.ppermute(part, axis, [(i, i ^ k) for i in range(n)]) if k else part for part, k in zip(parts, steps)]


def edge_proj_kernel(edge, bedge, proj, wv_ref, edge_buf, bedge_buf, proj_buf, sems):
    slots = proj.shape[1]
    pairs = ((proj, proj_buf), (edge, edge_buf), (bedge, bedge_buf))
    copies = [
        [pltpu.make_async_copy(src.at[0, i], buf.at[i], sems.at[3 * i + a]) for a, (src, buf) in enumerate(pairs)]
        for i in range(slots)
    ]
    for group in copies[:AHEAD]:
        for copy in group:
            copy.start()
    dot = functools.partial(jnp.dot, preferred_element_type=jnp.float32)
    for i, (first, second, third) in enumerate(copies):
        for group in copies[i + AHEAD : i + AHEAD + 1]:
            for copy in group:
                copy.start()
        first.wait()
        second.wait()
        wv_ref[2 * i] = dot(edge_buf[i], proj_buf[i]).astype(wv_ref.dtype)
        third.wait()
        wv_ref[2 * i + 1] = dot(bedge_buf[i], proj_buf[i]).astype(wv_ref.dtype)


def edge_proj(edge, bedge, proj):
    _, slots, m, k = edge.shape
    return pl.pallas_call(
        edge_proj_kernel,
        out_shape=jax.ShapeDtypeStruct((2 * slots, m, m), jnp.bfloat16),
        in_specs=[HBM] * 3,
        out_specs=VMEM,
        scratch_shapes=[
            pltpu.VMEM((slots, m, k), jnp.bfloat16),
            pltpu.VMEM((slots, m, k), jnp.bfloat16),
            pltpu.VMEM((slots, k, m), jnp.bfloat16),
            pltpu.SemaphoreType.DMA((3 * slots,)),
        ],
        cost_estimate=pl.CostEstimate(
            flops=4 * slots * m * k * m, bytes_accessed=6 * slots * m * k, transcendentals=0
        ),
        compiler_params=pltpu.CompilerParams(vmem_limit_bytes=52 << 20),
        name="edge_proj",
    )(edge, bedge, proj)


def small_call(kernel, out_shape, in_specs, scratch, name):
    return pl.pallas_call(
        kernel,
        out_shape=out_shape,
        in_specs=in_specs,
        out_specs=jax.tree.map(lambda _: VMEM, out_shape),
        scratch_shapes=scratch,
        cost_estimate=pl.CostEstimate(flops=1 << 28, bytes_accessed=1 << 20, transcendentals=0),
        compiler_params=pltpu.CompilerParams(vmem_limit_bytes=24 << 20),
        name=name,
    )


def blocks_of(turn, corner, bcorner, w, v):
    cosine, sine = turn
    dot = functools.partial(jnp.dot, preferred_element_type=jnp.float32)
    ground = dot(corner, w).astype(jnp.bfloat16)
    real_term = dot(bcorner[0], w)
    imag_term = dot(bcorner[1], w)
    re = cosine * real_term - sine * imag_term + dot(corner, v)
    im = sine * real_term + cosine * imag_term
    return ground, re.astype(jnp.bfloat16), im.astype(jnp.bfloat16)


def spread_kernel(steps, sites, turn, corner, bcorner, wv, *refs):
    n = len(steps)
    out, stage = refs[:n], refs[n]
    here = my_place()
    slots, m = corner.shape[1], corner.shape[2]
    rows = m // n
    top = jnp.zeros((m, m), jnp.float32)
    for i in range(slots):
        b_here = (bcorner[0, 0, i], bcorner[1, 0, i])
        blocks = blocks_of((turn[0:1], turn[1:2]), corner[0, i], b_here, wv[2 * i], wv[2 * i + 1])
        top = jnp.maximum(top, jnp.abs(blocks[0].astype(jnp.float32)))
        for kind in range(3):
            stage[3 * i + kind] = blocks[kind]
    peak = jnp.full((TILE, m), jnp.max(top), jnp.float32).astype(jnp.bfloat16)
    for p, k in enumerate(steps):
        first = piece_start(jnp.bitwise_xor(here[0], k), m, n, sites)
        for b in range(3 * slots):
            out[p][b * rows : (b + 1) * rows] = stage[b, pl.ds(first, rows)]
        out[p][3 * slots * rows :] = peak


def route_kernel(steps, slots, joining_in, *refs):
    n = len(steps)
    pieces, out, (held, joining, sem) = refs[:n], refs[n : 2 * n], refs[2 * n :]
    copy = pltpu.make_async_copy(joining_in, joining, sem)
    copy.start()
    here = my_place()
    size = held.shape[1]
    for p, k in enumerate(steps):
        d = jnp.bitwise_xor(here[0], k)
        for i in range(slots):
            held[d * slots + i] = pieces[p][i * size : (i + 1) * size]
    top = functools.reduce(jnp.maximum, [piece[slots * size :].astype(jnp.float32) for piece in pieces])
    divisor = jnp.concatenate([top] * (size // TILE), axis=0) + epsilon
    copy.wait()
    for p, k in enumerate(steps):
        t = jnp.bitwise_xor(here[0], k)
        for i in range(slots):
            q = joining[0, t * slots + i]
            out[p][i * size : (i + 1) * size] = (held[q].astype(jnp.float32) / divisor).astype(jnp.bfloat16)


def share_kernel(steps, sites, *refs):
    pieces, out, stage = refs[:sites], refs[-1 - sites : -1], refs[-1]
    here = my_place()
    _, slots, rows, _ = out[0].shape
    for p, k in enumerate(steps):
        r = lax.rem(jnp.bitwise_xor(here[0], k), sites)
        for i in range(slots):
            for c in range(2):
                at = (3 * i + 1 + c) * rows
                stage[r, c, i] = pieces[p][at : at + rows]
    for k in range(sites):
        out[k][...] = stage[jnp.bitwise_xor(here[1], k)]


def sum_kernel(sites, *refs):
    near, far, summed = refs[:sites], refs[sites : 2 * sites], refs[2 * sites]
    here = my_place()
    _, slots, rows, _ = near[0].shape
    half = lax.div(here[0], sites)
    for shares, place in ((near, half), (far, 1 - half)):
        first = pl.multiple_of(place * rows, rows)
        for i in range(slots):
            for c in range(2):
                summed[c, i, pl.ds(first, rows)] = sum([share[c, i].astype(jnp.float32) for share in shares[1:]],
                                                       shares[0][c, i].astype(jnp.float32))


def join_kernel(steps, sites, *refs):
    n = len(steps)
    pieces, new_corner, new_b = refs[:n], refs[n], refs[n + 1]
    here = my_place()
    _, slots, m, _ = new_corner.shape
    rows = m // n
    for p, k in enumerate(steps):
        first = piece_start(jnp.bitwise_xor(here[0], k), m, n, sites)
        for i in range(slots):
            at = 3 * i * rows
            new_corner[0, i, pl.ds(first, rows)] = pieces[p][at : at + rows]
            for c in range(2):
                at = (3 * i + 1 + c) * rows
                new_b[c, 0, i, pl.ds(first, rows)] = pieces[p][at : at + rows]


def routed_by_tiles(turn, corner, bcorner, wv, joining, n, sites):
    _, slots, m, _ = corner.shape
    rows = m // n
    shape = lambda *dims: jax.ShapeDtypeStruct(dims, jnp.bfloat16)
    scratch = lambda *dims: [pltpu.VMEM(dims, jnp.bfloat16)]
    bind = functools.partial
    steps = start_order(n)
    pieces = [shape(3 * slots * rows + TILE, m)] * n
    kept = scratch(3 * slots, m, m)
    parts = small_call(bind(spread_kernel, steps, sites), pieces, [VMEM] * 4, kept, "spread")(
        turn, corner, bcorner, wv
    )
    parts = all_swapped(parts, steps, "blk")
    pieces = [shape(3 * slots * rows, m)] * n
    kept = scratch(n * slots, 3 * rows, m) + [pltpu.SMEM(joining.shape, jnp.int32), pltpu.SemaphoreType.DMA]
    parts = small_call(bind(route_kernel, steps, slots), pieces, [ANY] + [VMEM] * n, kept, "route")(
        joining, *parts
    )
    parts = all_swapped(parts, steps, "blk")
    halves = []
    for ours in (lambda k: k < sites, lambda k: k >= sites):
        some = [(k, part) for k, part in zip(steps, parts) if ours(k)]
        share = bind(share_kernel, [k for k, _ in some], sites)
        kept = scratch(sites, 2, slots, rows, m)
        late = [] if halves else [part for k, part in zip(steps, parts) if k in FIRST]
        specs = [VMEM] * sites + [ANY] * len(late)
        shares = small_call(share, [shape(2, slots, rows, m)] * sites, specs, kept, "share")(
            *[part for _, part in some], *late
        )
        halves += all_swapped(shares, range(sites), "site")
    pieces = [shape(1, slots, m, m), shape(2, 1, slots, m, m)]
    join = bind(join_kernel, steps, sites)
    new_corner, new_b = small_call(join, pieces, [VMEM] * n, [], "join")(*parts)
    summed = jax.ShapeDtypeStruct((2, slots, m // sites, m), jnp.float32)
    add = bind(sum_kernel, sites)
    summed = small_call(add, [summed], [VMEM] * (2 * sites), [], "sum")(*halves)[0]
    return new_corner, new_b, summed


def transposed(pieces):
    return lax.all_to_all(pieces, "blk", 0, 0, tiled=True)


def routed_by_rows(turn, corner, bcorner, wv, joining, n, sites):
    _, slots, m, _ = corner.shape
    rows = m // n
    wv = wv.reshape(slots, 2, m, m)
    ground, re, im = jax.vmap(lambda c, b, x: blocks_of((turn[0], turn[1]), c, b, x[0], x[1]))(
        corner[0], jnp.moveaxis(bcorner[:, 0], 0, 1), wv
    )
    peak = lax.pmax(jnp.max(jnp.abs(ground)).astype(jnp.float32), "blk")
    blocks = jnp.moveaxis(jnp.stack([ground, re, im], axis=1).reshape(slots, 3, n, rows, m), 2, 0)
    pieces = transposed(blocks).reshape(n * slots, 3, rows, m)
    scaled = (pieces[joining[0]].astype(jnp.float32) / (peak + epsilon)).astype(jnp.bfloat16)
    final = transposed(scaled.reshape(n, slots, 3, rows, m))
    new = jnp.transpose(final, (2, 1, 0, 3, 4)).reshape(3, slots, m, m)
    shares = jnp.moveaxis(new[1:].reshape(2, slots, sites, m // sites, m), 2, 0)
    shares = lax.all_to_all(shares, "site", 0, 0, tiled=True)
    return new[0][None], new[1:][:, None], jnp.sum(shares.astype(jnp.float32), axis=0)


def per_device(corner, bcorner, edge, bedge, proj, joining, momentum):
    m = corner.shape[2]
    n, sites = lax.axis_size("blk"), lax.axis_size("site")
    angle = momentum[0] * lax.axis_index("site").astype(jnp.float32)
    turn = jnp.broadcast_to(jnp.stack([jnp.cos(angle), jnp.sin(angle)])[:, None], (2, m))
    onward = [(i, (i + 1) % sites) for i in range(sites)]
    left_bcorner = lax.ppermute(bcorner, "site", onward)
    left_corner = lax.ppermute(corner, "site", onward)
    wv = edge_proj(edge, bedge, proj)
    routed = routed_by_tiles if m % (n * TILE) == 0 and n == 2 * sites else routed_by_rows
    return routed(turn, left_corner, left_bcorner, wv, joining, n, sites)


def solution(mesh):
    in_specs = (
        P("site", "blk", None, None),
        P(None, "site", "blk", None, None),
        P("site", "blk", None, None),
        P("site", "blk", None, None),
        P("site", "blk", None, None),
        P("site", None),
        P(),
    )
    out_specs = (
        P("site", "blk", None, None),
        P(None, "site", "blk", None, None),
        P(None, "blk", "site", None),
    )
    return jax.shard_map(
        per_device, mesh=mesh, in_specs=in_specs, out_specs=out_specs, check_vma=False
    )
```

```python
import functools

import jax
import jax.numpy as jnp
from jax import lax
from jax.experimental import pallas as pl
from jax.experimental.pallas import tpu as pltpu
from jax.sharding import PartitionSpec as P

epsilon = 1e-06
TILE = 16
AHEAD = 2
VMEM = pl.BlockSpec(memory_space=pltpu.VMEM)
ANY = pl.BlockSpec(memory_space=pl.ANY)
HBM = pl.BlockSpec(memory_space=pltpu.HBM)


def start_order(n):
    far = sorted(range(n // 2, n), key=lambda k: (k & 1, -k))
    return (0, far[0], 1, *far[1:], *range(2, n // 2))


def my_place():
    return lax.axis_index("blk"), lax.axis_index("site")


def piece_start(j, m, n, sites):
    return pl.multiple_of(lax.rem(j, sites) * (m // sites) + lax.div(j, sites) * (m // n), m // n)


def all_swapped(parts, steps, axis):
    n = len(parts)
    return [lax.ppermute(part, axis, [(i, i ^ k) for i in range(n)]) if k else part for part, k in zip(parts, steps)]


def edge_proj_kernel(edge, bedge, proj, wv_ref, edge_buf, bedge_buf, proj_buf, sems):
    slots = proj.shape[1]
    pairs = ((proj, proj_buf), (edge, edge_buf), (bedge, bedge_buf))
    copies = [
        [pltpu.make_async_copy(src.at[0, i], buf.at[i], sems.at[3 * i + a]) for a, (src, buf) in enumerate(pairs)]
        for i in range(slots)
    ]
    for group in copies[:AHEAD]:
        for copy in group:
            copy.start()
    dot = functools.partial(jnp.dot, preferred_element_type=jnp.float32)
    for i, (first, second, third) in enumerate(copies):
        for group in copies[i + AHEAD : i + AHEAD + 1]:
            for copy in group:
                copy.start()
        first.wait()
        second.wait()
        wv_ref[2 * i] = dot(edge_buf[i], proj_buf[i]).astype(wv_ref.dtype)
        third.wait()
        wv_ref[2 * i + 1] = dot(bedge_buf[i], proj_buf[i]).astype(wv_ref.dtype)


def edge_proj(edge, bedge, proj):
    _, slots, m, k = edge.shape
    return pl.pallas_call(
        edge_proj_kernel,
        out_shape=jax.ShapeDtypeStruct((2 * slots, m, m), jnp.bfloat16),
        in_specs=[HBM] * 3,
        out_specs=VMEM,
        scratch_shapes=[
            pltpu.VMEM((slots, m, k), jnp.bfloat16),
            pltpu.VMEM((slots, m, k), jnp.bfloat16),
            pltpu.VMEM((slots, k, m), jnp.bfloat16),
            pltpu.SemaphoreType.DMA((3 * slots,)),
        ],
        cost_estimate=pl.CostEstimate(
            flops=4 * slots * m * k * m, bytes_accessed=6 * slots * m * k, transcendentals=0
        ),
        compiler_params=pltpu.CompilerParams(vmem_limit_bytes=52 << 20),
        name="edge_proj",
    )(edge, bedge, proj)


def small_call(kernel, out_shape, in_specs, scratch, name):
    return pl.pallas_call(
        kernel,
        out_shape=out_shape,
        in_specs=in_specs,
        out_specs=jax.tree.map(lambda _: VMEM, out_shape),
        scratch_shapes=scratch,
        cost_estimate=pl.CostEstimate(flops=1 << 28, bytes_accessed=1 << 20, transcendentals=0),
        compiler_params=pltpu.CompilerParams(vmem_limit_bytes=24 << 20),
        name=name,
    )


def blocks_of(turn, corner, bcorner, w, v):
    cosine, sine = turn
    dot = functools.partial(jnp.dot, preferred_element_type=jnp.float32)
    ground = dot(corner, w).astype(jnp.bfloat16)
    real_term = dot(bcorner[0], w)
    imag_term = dot(bcorner[1], w)
    re = cosine * real_term - sine * imag_term + dot(corner, v)
    im = sine * real_term + cosine * imag_term
    return ground, re.astype(jnp.bfloat16), im.astype(jnp.bfloat16)


def spread_kernel(steps, sites, turn, corner, bcorner, wv, *refs):
    n = len(steps)
    out, stage = refs[:n], refs[n]
    here = my_place()
    slots, m = corner.shape[1], corner.shape[2]
    rows = m // n
    top = jnp.zeros((m, m), jnp.float32)
    for i in range(slots):
        b_here = (bcorner[0, 0, i], bcorner[1, 0, i])
        blocks = blocks_of((turn[0:1], turn[1:2]), corner[0, i], b_here, wv[2 * i], wv[2 * i + 1])
        top = jnp.maximum(top, jnp.abs(blocks[0].astype(jnp.float32)))
        for kind in range(3):
            stage[3 * i + kind] = blocks[kind]
    peak = jnp.full((TILE, m), jnp.max(top), jnp.float32).astype(jnp.bfloat16)
    for p, k in enumerate(steps):
        first = piece_start(jnp.bitwise_xor(here[0], k), m, n, sites)
        for b in range(3 * slots):
            out[p][b * rows : (b + 1) * rows] = stage[b, pl.ds(first, rows)]
        out[p][3 * slots * rows :] = peak


def route_kernel(steps, slots, joining_in, *refs):
    n = len(steps)
    pieces, out, (held, joining, sem) = refs[:n], refs[n : 2 * n], refs[2 * n :]
    copy = pltpu.make_async_copy(joining_in, joining, sem)
    copy.start()
    here = my_place()
    size = held.shape[1]
    top = functools.reduce(jnp.maximum, [piece[slots * size :].astype(jnp.float32) for piece in pieces])
    divisor = jnp.concatenate([top] * (size // TILE), axis=0) + epsilon
    for p, k in enumerate(steps):
        d = jnp.bitwise_xor(here[0], k)
        for i in range(slots):
            piece = pieces[p][i * size : (i + 1) * size].astype(jnp.float32)
            held[d * slots + i] = (piece / divisor).astype(jnp.bfloat16)
    copy.wait()
    for p, k in enumerate(steps):
        t = jnp.bitwise_xor(here[0], k)
        for i in range(slots):
            out[p][i * size : (i + 1) * size] = held[joining[0, t * slots + i]]


def share_kernel(steps, sites, *refs):
    pieces, (kept, away, stage) = refs[:sites], refs[-3:]
    here = my_place()
    _, _, slots, rows, _ = kept.shape
    for p, k in enumerate(steps):
        r = lax.rem(jnp.bitwise_xor(here[0], k), sites)
        for i in range(slots):
            for c in range(2):
                at = (3 * i + 1 + c) * rows
                stage[r, c, i] = pieces[p][at : at + rows]
    for k in range(sites):
        out = away if k % 2 else kept
        out[k // 2] = stage[jnp.bitwise_xor(here[1], k)]


def sum_kernel(sites, *refs):
    halves, summed = (refs[:3], refs[3:6]), refs[6]
    here = my_place()
    _, _, slots, rows, _ = refs[0].shape
    half = lax.div(here[0], sites)
    for (kept, came, last), part in zip(halves, (half, 1 - half)):
        first = pl.multiple_of(part * rows, rows)
        for i in range(slots):
            for c in range(2):
                total = kept[0, c, i].astype(jnp.float32) + came[0, c, i].astype(jnp.float32)
                summed[c, i, pl.ds(first, rows)] = total + last[c, i].astype(jnp.float32)


def join_kernel(steps, sites, *refs):
    n = len(steps)
    pieces, new_corner, new_b = refs[:n], refs[n], refs[n + 1]
    here = my_place()
    _, slots, m, _ = new_corner.shape
    rows = m // n
    for p, k in enumerate(steps):
        first = piece_start(jnp.bitwise_xor(here[0], k), m, n, sites)
        for i in range(slots):
            at = 3 * i * rows
            new_corner[0, i, pl.ds(first, rows)] = pieces[p][at : at + rows]
            for c in range(2):
                at = (3 * i + 1 + c) * rows
                new_b[c, 0, i, pl.ds(first, rows)] = pieces[p][at : at + rows]


def routed_by_tiles(turn, corner, bcorner, wv, joining, n, sites):
    _, slots, m, _ = corner.shape
    rows = m // n
    shape = lambda *dims: jax.ShapeDtypeStruct(dims, jnp.bfloat16)
    scratch = lambda *dims: [pltpu.VMEM(dims, jnp.bfloat16)]
    bind = functools.partial
    steps = start_order(n)
    pieces = [shape(3 * slots * rows + TILE, m)] * n
    kept = scratch(3 * slots, m, m)
    parts = small_call(bind(spread_kernel, steps, sites), pieces, [VMEM] * 4, kept, "spread")(
        turn, corner, bcorner, wv
    )
    parts = all_swapped(parts, steps, "blk")
    pieces = [shape(3 * slots * rows, m)] * n
    kept = scratch(n * slots, 3 * rows, m) + [pltpu.SMEM(joining.shape, jnp.int32), pltpu.SemaphoreType.DMA]
    parts = small_call(bind(route_kernel, steps, slots), pieces, [ANY] + [VMEM] * n, kept, "route")(
        joining, *parts
    )
    parts = all_swapped(parts, steps, "blk")
    halves = []
    for ours in (lambda k: k < sites, lambda k: k >= sites):
        some = [(k, part) for k, part in zip(steps, parts) if ours(k)]
        share = bind(share_kernel, [k for k, _ in some], sites)
        kept = scratch(sites, 2, slots, rows, m)
        shares = small_call(share, [shape(2, 2, slots, rows, m)] * 2, [VMEM] * sites, kept, "share")(
            *[part for _, part in some]
        )
        came = lax.ppermute(shares[1], "site", [(i, i ^ 1) for i in range(sites)])
        partial = shares[0][1].astype(jnp.float32) + came[1].astype(jnp.float32)
        last = lax.ppermute(partial.astype(jnp.bfloat16), "site", [(i, i ^ 2) for i in range(sites)])
        halves += [shares[0], came, last]
    pieces = [shape(1, slots, m, m), shape(2, 1, slots, m, m)]
    join = bind(join_kernel, steps, sites)
    new_corner, new_b = small_call(join, pieces, [VMEM] * n, [], "join")(*parts)
    summed = jax.ShapeDtypeStruct((2, slots, m // sites, m), jnp.float32)
    add = bind(sum_kernel, sites)
    summed = small_call(add, [summed], [VMEM] * 6, [], "sum")(*halves)[0]
    return new_corner, new_b, summed


def transposed(pieces):
    return lax.all_to_all(pieces, "blk", 0, 0, tiled=True)


def routed_by_rows(turn, corner, bcorner, wv, joining, n, sites):
    _, slots, m, _ = corner.shape
    rows = m // n
    wv = wv.reshape(slots, 2, m, m)
    ground, re, im = jax.vmap(lambda c, b, x: blocks_of((turn[0], turn[1]), c, b, x[0], x[1]))(
        corner[0], jnp.moveaxis(bcorner[:, 0], 0, 1), wv
    )
    peak = lax.pmax(jnp.max(jnp.abs(ground)).astype(jnp.float32), "blk")
    blocks = jnp.moveaxis(jnp.stack([ground, re, im], axis=1).reshape(slots, 3, n, rows, m), 2, 0)
    pieces = transposed(blocks).reshape(n * slots, 3, rows, m)
    scaled = (pieces[joining[0]].astype(jnp.float32) / (peak + epsilon)).astype(jnp.bfloat16)
    final = transposed(scaled.reshape(n, slots, 3, rows, m))
    new = jnp.transpose(final, (2, 1, 0, 3, 4)).reshape(3, slots, m, m)
    shares = jnp.moveaxis(new[1:].reshape(2, slots, sites, m // sites, m), 2, 0)
    shares = lax.all_to_all(shares, "site", 0, 0, tiled=True)
    return new[0][None], new[1:][:, None], jnp.sum(shares.astype(jnp.float32), axis=0)


def per_device(corner, bcorner, edge, bedge, proj, joining, momentum):
    m = corner.shape[2]
    n, sites = lax.axis_size("blk"), lax.axis_size("site")
    angle = momentum[0] * lax.axis_index("site").astype(jnp.float32)
    turn = jnp.broadcast_to(jnp.stack([jnp.cos(angle), jnp.sin(angle)])[:, None], (2, m))
    onward = [(i, (i + 1) % sites) for i in range(sites)]
    left_bcorner = lax.ppermute(bcorner, "site", [(i, i ^ 1) for i in range(sites)])
    left_bcorner, corner = lax.optimization_barrier((left_bcorner, corner))
    left_bcorner = lax.ppermute(left_bcorner, "site", [(i, i if i % 2 else (i + 2) % sites) for i in range(sites)])
    left_corner = lax.ppermute(corner, "site", onward)
    wv = edge_proj(edge, bedge, proj)
    routed = routed_by_tiles if m % (n * TILE) == 0 and (n, sites) == (8, 4) else routed_by_rows
    return routed(turn, left_corner, left_bcorner, wv, joining, n, sites)


def solution(mesh):
    in_specs = (
        P("site", "blk", None, None),
        P(None, "site", "blk", None, None),
        P("site", "blk", None, None),
        P("site", "blk", None, None),
        P("site", "blk", None, None),
        P("site", None),
        P(),
    )
    out_specs = (
        P("site", "blk", None, None),
        P(None, "site", "blk", None, None),
        P(None, "blk", "site", None),
    )
    return jax.shard_map(
        per_device, mesh=mesh, in_specs=in_specs, out_specs=out_specs, check_vma=False
    )
```

```python
import functools

import jax
import jax.numpy as jnp
from jax import lax
from jax.experimental import pallas as pl
from jax.experimental.pallas import tpu as pltpu
from jax.sharding import PartitionSpec as P

epsilon = 1e-06
TILE = 16
FIRST = (6, 4, 7)
AHEAD = 2
VMEM = pl.BlockSpec(memory_space=pltpu.VMEM)
ANY = pl.BlockSpec(memory_space=pl.ANY)
HBM = pl.BlockSpec(memory_space=pltpu.HBM)


def start_order(n):
    far = sorted(range(n // 2, n), key=lambda k: (k & 1, -k))
    return (0, far[0], 1, *far[1:], *range(2, n // 2))


def my_place():
    return lax.axis_index("blk"), lax.axis_index("site")


def piece_start(j, m, n, sites):
    return pl.multiple_of(lax.rem(j, sites) * (m // sites) + lax.div(j, sites) * (m // n), m // n)


def all_swapped(parts, steps, axis):
    n = len(parts)
    return [lax.ppermute(part, axis, [(i, i ^ k) for i in range(n)]) if k else part for part, k in zip(parts, steps)]


def edge_proj_kernel(edge, bedge, proj, wv_ref, edge_buf, bedge_buf, proj_buf, sems):
    slots = proj.shape[1]
    pairs = ((proj, proj_buf), (edge, edge_buf), (bedge, bedge_buf))
    copies = [
        [pltpu.make_async_copy(src.at[0, i], buf.at[i], sems.at[3 * i + a]) for a, (src, buf) in enumerate(pairs)]
        for i in range(slots)
    ]
    for group in copies[:AHEAD]:
        for copy in group:
            copy.start()
    dot = functools.partial(jnp.dot, preferred_element_type=jnp.float32)
    for i, (first, second, third) in enumerate(copies):
        for group in copies[i + AHEAD : i + AHEAD + 1]:
            for copy in group:
                copy.start()
        first.wait()
        second.wait()
        wv_ref[2 * i] = dot(edge_buf[i], proj_buf[i]).astype(wv_ref.dtype)
        third.wait()
        wv_ref[2 * i + 1] = dot(bedge_buf[i], proj_buf[i]).astype(wv_ref.dtype)


def edge_proj(edge, bedge, proj):
    _, slots, m, k = edge.shape
    return pl.pallas_call(
        edge_proj_kernel,
        out_shape=jax.ShapeDtypeStruct((2 * slots, m, m), jnp.bfloat16),
        in_specs=[HBM] * 3,
        out_specs=VMEM,
        scratch_shapes=[
            pltpu.VMEM((slots, m, k), jnp.bfloat16),
            pltpu.VMEM((slots, m, k), jnp.bfloat16),
            pltpu.VMEM((slots, k, m), jnp.bfloat16),
            pltpu.SemaphoreType.DMA((3 * slots,)),
        ],
        cost_estimate=pl.CostEstimate(
            flops=4 * slots * m * k * m, bytes_accessed=6 * slots * m * k, transcendentals=0
        ),
        compiler_params=pltpu.CompilerParams(vmem_limit_bytes=52 << 20),
        name="edge_proj",
    )(edge, bedge, proj)


def small_call(kernel, out_shape, in_specs, scratch, name):
    return pl.pallas_call(
        kernel,
        out_shape=out_shape,
        in_specs=in_specs,
        out_specs=jax.tree.map(lambda _: VMEM, out_shape),
        scratch_shapes=scratch,
        cost_estimate=pl.CostEstimate(flops=1 << 28, bytes_accessed=1 << 20, transcendentals=0),
        compiler_params=pltpu.CompilerParams(vmem_limit_bytes=24 << 20),
        name=name,
    )


def blocks_of(turn, corner, bcorner, w, v):
    cosine, sine = turn
    dot = functools.partial(jnp.dot, preferred_element_type=jnp.float32)
    ground = dot(corner, w).astype(jnp.bfloat16)
    real_term = dot(bcorner[0], w)
    imag_term = dot(bcorner[1], w)
    re = cosine * real_term - sine * imag_term + dot(corner, v)
    im = sine * real_term + cosine * imag_term
    return ground, re.astype(jnp.bfloat16), im.astype(jnp.bfloat16)


def spread_kernel(steps, sites, turn, corner, bcorner, wv, *refs):
    n = len(steps)
    out, stage = refs[:n], refs[n]
    here = my_place()
    slots, m = corner.shape[1], corner.shape[2]
    rows = m // n
    top = jnp.zeros((m, m), jnp.float32)
    for i in range(slots):
        b_here = (bcorner[0, 0, i], bcorner[1, 0, i])
        blocks = blocks_of((turn[0:1], turn[1:2]), corner[0, i], b_here, wv[2 * i], wv[2 * i + 1])
        top = jnp.maximum(top, jnp.abs(blocks[0].astype(jnp.float32)))
        for kind in range(3):
            stage[3 * i + kind] = blocks[kind]
    peak = jnp.full((TILE, m), jnp.max(top), jnp.float32).astype(jnp.bfloat16)
    for p, k in enumerate(steps):
        first = piece_start(jnp.bitwise_xor(here[0], k), m, n, sites)
        for b in range(3 * slots):
            out[p][b * rows : (b + 1) * rows] = stage[b, pl.ds(first, rows)]
        out[p][3 * slots * rows :] = peak


def route_kernel(steps, slots, joining_in, *refs):
    n = len(steps)
    pieces, out, (held, joining, sem) = refs[:n], refs[n : 2 * n], refs[2 * n :]
    copy = pltpu.make_async_copy(joining_in, joining, sem)
    copy.start()
    here = my_place()
    size = held.shape[1]
    top = functools.reduce(jnp.maximum, [piece[slots * size :].astype(jnp.float32) for piece in pieces])
    divisor = jnp.concatenate([top] * (size // TILE), axis=0) + epsilon
    for p, k in enumerate(steps):
        d = jnp.bitwise_xor(here[0], k)
        for i in range(slots):
            piece = pieces[p][i * size : (i + 1) * size].astype(jnp.float32)
            held[d * slots + i] = (piece / divisor).astype(jnp.bfloat16)
    copy.wait()
    for p, k in enumerate(steps):
        t = jnp.bitwise_xor(here[0], k)
        for i in range(slots):
            out[p][i * size : (i + 1) * size] = held[joining[0, t * slots + i]]


def share_kernel(steps, sites, *refs):
    pieces, out, stage = refs[:sites], refs[-1 - sites : -1], refs[-1]
    here = my_place()
    _, slots, rows, _ = out[0].shape
    for p, k in enumerate(steps):
        r = lax.rem(jnp.bitwise_xor(here[0], k), sites)
        for i in range(slots):
            for c in range(2):
                at = (3 * i + 1 + c) * rows
                stage[r, c, i] = pieces[p][at : at + rows]
    for k in range(sites):
        out[k][...] = stage[jnp.bitwise_xor(here[1], k)]


def sum_kernel(sites, *refs):
    near, far, summed = refs[:sites], refs[sites : 2 * sites], refs[2 * sites]
    here = my_place()
    _, slots, rows, _ = near[0].shape
    half = lax.div(here[0], sites)
    for shares, place in ((near, half), (far, 1 - half)):
        first = pl.multiple_of(place * rows, rows)
        for i in range(slots):
            for c in range(2):
                summed[c, i, pl.ds(first, rows)] = sum([share[c, i].astype(jnp.float32) for share in shares[1:]],
                                                       shares[0][c, i].astype(jnp.float32))


def join_kernel(steps, sites, *refs):
    n = len(steps)
    pieces, new_corner, new_b = refs[:n], refs[n], refs[n + 1]
    here = my_place()
    _, slots, m, _ = new_corner.shape
    rows = m // n
    for p, k in enumerate(steps):
        first = piece_start(jnp.bitwise_xor(here[0], k), m, n, sites)
        for i in range(slots):
            at = 3 * i * rows
            new_corner[0, i, pl.ds(first, rows)] = pieces[p][at : at + rows]
            for c in range(2):
                at = (3 * i + 1 + c) * rows
                new_b[c, 0, i, pl.ds(first, rows)] = pieces[p][at : at + rows]


def routed_by_tiles(turn, corner, bcorner, wv, joining, n, sites):
    _, slots, m, _ = corner.shape
    rows = m // n
    shape = lambda *dims: jax.ShapeDtypeStruct(dims, jnp.bfloat16)
    scratch = lambda *dims: [pltpu.VMEM(dims, jnp.bfloat16)]
    bind = functools.partial
    steps = start_order(n)
    pieces = [shape(3 * slots * rows + TILE, m)] * n
    kept = scratch(3 * slots, m, m)
    parts = small_call(bind(spread_kernel, steps, sites), pieces, [VMEM] * 4, kept, "spread")(
        turn, corner, bcorner, wv
    )
    parts = all_swapped(parts, steps, "blk")
    pieces = [shape(3 * slots * rows, m)] * n
    kept = scratch(n * slots, 3 * rows, m) + [pltpu.SMEM(joining.shape, jnp.int32), pltpu.SemaphoreType.DMA]
    parts = small_call(bind(route_kernel, steps, slots), pieces, [ANY] + [VMEM] * n, kept, "route")(
        joining, *parts
    )
    parts = all_swapped(parts, steps, "blk")
    halves = []
    for ours in (lambda k: k < sites, lambda k: k >= sites):
        some = [(k, part) for k, part in zip(steps, parts) if ours(k)]
        share = bind(share_kernel, [k for k, _ in some], sites)
        kept = scratch(sites, 2, slots, rows, m)
        late = [] if halves else [part for k, part in zip(steps, parts) if k in FIRST]
        specs = [VMEM] * sites + [ANY] * len(late)
        shares = small_call(share, [shape(2, slots, rows, m)] * sites, specs, kept, "share")(
            *[part for _, part in some], *late
        )
        halves += all_swapped(shares, range(sites), "site")
    pieces = [shape(1, slots, m, m), shape(2, 1, slots, m, m)]
    join = bind(join_kernel, steps, sites)
    new_corner, new_b = small_call(join, pieces, [VMEM] * n, [], "join")(*parts)
    summed = jax.ShapeDtypeStruct((2, slots, m // sites, m), jnp.float32)
    add = bind(sum_kernel, sites)
    summed = small_call(add, [summed], [VMEM] * (2 * sites), [], "sum")(*halves)[0]
    return new_corner, new_b, summed


def transposed(pieces):
    return lax.all_to_all(pieces, "blk", 0, 0, tiled=True)


def routed_by_rows(turn, corner, bcorner, wv, joining, n, sites):
    _, slots, m, _ = corner.shape
    rows = m // n
    wv = wv.reshape(slots, 2, m, m)
    ground, re, im = jax.vmap(lambda c, b, x: blocks_of((turn[0], turn[1]), c, b, x[0], x[1]))(
        corner[0], jnp.moveaxis(bcorner[:, 0], 0, 1), wv
    )
    peak = lax.pmax(jnp.max(jnp.abs(ground)).astype(jnp.float32), "blk")
    blocks = jnp.moveaxis(jnp.stack([ground, re, im], axis=1).reshape(slots, 3, n, rows, m), 2, 0)
    pieces = transposed(blocks).reshape(n * slots, 3, rows, m)
    scaled = (pieces[joining[0]].astype(jnp.float32) / (peak + epsilon)).astype(jnp.bfloat16)
    final = transposed(scaled.reshape(n, slots, 3, rows, m))
    new = jnp.transpose(final, (2, 1, 0, 3, 4)).reshape(3, slots, m, m)
    shares = jnp.moveaxis(new[1:].reshape(2, slots, sites, m // sites, m), 2, 0)
    shares = lax.all_to_all(shares, "site", 0, 0, tiled=True)
    return new[0][None], new[1:][:, None], jnp.sum(shares.astype(jnp.float32), axis=0)


def per_device(corner, bcorner, edge, bedge, proj, joining, momentum):
    m = corner.shape[2]
    n, sites = lax.axis_size("blk"), lax.axis_size("site")
    angle = momentum[0] * lax.axis_index("site").astype(jnp.float32)
    turn = jnp.broadcast_to(jnp.stack([jnp.cos(angle), jnp.sin(angle)])[:, None], (2, m))
    onward = [(i, (i + 1) % sites) for i in range(sites)]
    left_bcorner = lax.ppermute(bcorner, "site", onward)
    left_corner = lax.ppermute(corner, "site", onward)
    wv = edge_proj(edge, bedge, proj)
    routed = routed_by_tiles if m % (n * TILE) == 0 and n == 2 * sites else routed_by_rows
    return routed(turn, left_corner, left_bcorner, wv, joining, n, sites)


def solution(mesh):
    in_specs = (
        P("site", "blk", None, None),
        P(None, "site", "blk", None, None),
        P("site", "blk", None, None),
        P("site", "blk", None, None),
        P("site", "blk", None, None),
        P("site", None),
        P(),
    )
    out_specs = (
        P("site", "blk", None, None),
        P(None, "site", "blk", None, None),
        P(None, "blk", "site", None),
    )
    return jax.shard_map(
        per_device, mesh=mesh, in_specs=in_specs, out_specs=out_specs, check_vma=False
    )
```

```python
import functools

import jax
import jax.numpy as jnp
from jax import lax
from jax.experimental import pallas as pl
from jax.experimental.pallas import tpu as pltpu
from jax.sharding import PartitionSpec as P

epsilon = 1e-06
TILE = 16
SITE_STEPS = (0, 2, 3, 1)
FIRST = (6, 4, 7)
AHEAD = 2
VMEM = pl.BlockSpec(memory_space=pltpu.VMEM)
ANY = pl.BlockSpec(memory_space=pl.ANY)
HBM = pl.BlockSpec(memory_space=pltpu.HBM)


def start_order(n):
    far = sorted(range(n // 2, n), key=lambda k: (k & 1, -k))
    return (0, far[0], 1, *far[1:], *range(2, n // 2))


def my_place():
    return lax.axis_index("blk"), lax.axis_index("site")


def piece_start(j, m, n, sites):
    return pl.multiple_of(lax.rem(j, sites) * (m // sites) + lax.div(j, sites) * (m // n), m // n)


def all_swapped(parts, steps, axis):
    n = len(parts)
    return [lax.ppermute(part, axis, [(i, i ^ k) for i in range(n)]) if k else part for part, k in zip(parts, steps)]


def edge_proj_kernel(edge, bedge, proj, wv_ref, edge_buf, bedge_buf, proj_buf, sems):
    slots = proj.shape[1]
    pairs = ((proj, proj_buf), (edge, edge_buf), (bedge, bedge_buf))
    copies = [
        [pltpu.make_async_copy(src.at[0, i], buf.at[i], sems.at[3 * i + a]) for a, (src, buf) in enumerate(pairs)]
        for i in range(slots)
    ]
    for group in copies[:AHEAD]:
        for copy in group:
            copy.start()
    dot = functools.partial(jnp.dot, preferred_element_type=jnp.float32)
    for i, (first, second, third) in enumerate(copies):
        for group in copies[i + AHEAD : i + AHEAD + 1]:
            for copy in group:
                copy.start()
        first.wait()
        second.wait()
        wv_ref[2 * i] = dot(edge_buf[i], proj_buf[i]).astype(wv_ref.dtype)
        third.wait()
        wv_ref[2 * i + 1] = dot(bedge_buf[i], proj_buf[i]).astype(wv_ref.dtype)


def edge_proj(edge, bedge, proj):
    _, slots, m, k = edge.shape
    return pl.pallas_call(
        edge_proj_kernel,
        out_shape=jax.ShapeDtypeStruct((2 * slots, m, m), jnp.bfloat16),
        in_specs=[HBM] * 3,
        out_specs=VMEM,
        scratch_shapes=[
            pltpu.VMEM((slots, m, k), jnp.bfloat16),
            pltpu.VMEM((slots, m, k), jnp.bfloat16),
            pltpu.VMEM((slots, k, m), jnp.bfloat16),
            pltpu.SemaphoreType.DMA((3 * slots,)),
        ],
        cost_estimate=pl.CostEstimate(
            flops=4 * slots * m * k * m, bytes_accessed=6 * slots * m * k, transcendentals=0
        ),
        compiler_params=pltpu.CompilerParams(vmem_limit_bytes=52 << 20),
        name="edge_proj",
    )(edge, bedge, proj)


def small_call(kernel, out_shape, in_specs, scratch, name):
    return pl.pallas_call(
        kernel,
        out_shape=out_shape,
        in_specs=in_specs,
        out_specs=jax.tree.map(lambda _: VMEM, out_shape),
        scratch_shapes=scratch,
        cost_estimate=pl.CostEstimate(flops=1 << 28, bytes_accessed=1 << 20, transcendentals=0),
        compiler_params=pltpu.CompilerParams(vmem_limit_bytes=24 << 20),
        name=name,
    )


def blocks_of(turn, corner, bcorner, w, v):
    cosine, sine = turn
    dot = functools.partial(jnp.dot, preferred_element_type=jnp.float32)
    ground = dot(corner, w).astype(jnp.bfloat16)
    real_term = dot(bcorner[0], w)
    imag_term = dot(bcorner[1], w)
    re = cosine * real_term - sine * imag_term + dot(corner, v)
    im = sine * real_term + cosine * imag_term
    return ground, re.astype(jnp.bfloat16), im.astype(jnp.bfloat16)


def spread_kernel(steps, sites, turn, corner, bcorner, wv, *refs):
    n = len(steps)
    out, stage = refs[:n], refs[n]
    here = my_place()
    slots, m = corner.shape[1], corner.shape[2]
    rows = m // n
    top = jnp.zeros((m, m), jnp.float32)
    for i in range(slots):
        b_here = (bcorner[0, 0, i], bcorner[1, 0, i])
        blocks = blocks_of((turn[0:1], turn[1:2]), corner[0, i], b_here, wv[2 * i], wv[2 * i + 1])
        top = jnp.maximum(top, jnp.abs(blocks[0].astype(jnp.float32)))
        for kind in range(3):
            stage[3 * i + kind] = blocks[kind]
    peak = jnp.full((TILE, m), jnp.max(top), jnp.float32).astype(jnp.bfloat16)
    for p, k in enumerate(steps):
        first = piece_start(jnp.bitwise_xor(here[0], k), m, n, sites)
        for b in range(3 * slots):
            out[p][b * rows : (b + 1) * rows] = stage[b, pl.ds(first, rows)]
        out[p][3 * slots * rows :] = peak


def route_kernel(steps, slots, joining_in, *refs):
    n = len(steps)
    pieces, out, (held, joining, sem) = refs[:n], refs[n : 2 * n], refs[2 * n :]
    copy = pltpu.make_async_copy(joining_in, joining, sem)
    copy.start()
    here = my_place()
    size = held.shape[1]
    top = functools.reduce(jnp.maximum, [piece[slots * size :].astype(jnp.float32) for piece in pieces])
    divisor = jnp.concatenate([top] * (size // TILE), axis=0) + epsilon
    for p, k in enumerate(steps):
        d = jnp.bitwise_xor(here[0], k)
        for i in range(slots):
            piece = pieces[p][i * size : (i + 1) * size].astype(jnp.float32)
            held[d * slots + i] = (piece / divisor).astype(jnp.bfloat16)
    copy.wait()
    for p, k in enumerate(steps):
        t = jnp.bitwise_xor(here[0], k)
        for i in range(slots):
            out[p][i * size : (i + 1) * size] = held[joining[0, t * slots + i]]


def share_kernel(steps, sites, *refs):
    pieces, out, stage = refs[:sites], refs[-1 - sites : -1], refs[-1]
    here = my_place()
    _, slots, rows, _ = out[0].shape
    for p, k in enumerate(steps):
        r = lax.rem(jnp.bitwise_xor(here[0], k), sites)
        for i in range(slots):
            for c in range(2):
                at = (3 * i + 1 + c) * rows
                stage[r, c, i] = pieces[p][at : at + rows]
    for p, k in enumerate(SITE_STEPS):
        out[p][...] = stage[jnp.bitwise_xor(here[1], k)]


def sum_kernel(sites, *refs):
    near, far, summed = refs[:sites], refs[sites : 2 * sites], refs[2 * sites]
    here = my_place()
    _, slots, rows, _ = near[0].shape
    half = lax.div(here[0], sites)
    for shares, place in ((near, half), (far, 1 - half)):
        first = pl.multiple_of(place * rows, rows)
        for i in range(slots):
            for c in range(2):
                summed[c, i, pl.ds(first, rows)] = sum([share[c, i].astype(jnp.float32) for share in shares[1:]],
                                                       shares[0][c, i].astype(jnp.float32))


def join_kernel(steps, sites, *refs):
    n = len(steps)
    pieces, new_corner, new_b = refs[:n], refs[n], refs[n + 1]
    here = my_place()
    _, slots, m, _ = new_corner.shape
    rows = m // n
    for p, k in enumerate(steps):
        first = piece_start(jnp.bitwise_xor(here[0], k), m, n, sites)
        for i in range(slots):
            at = 3 * i * rows
            new_corner[0, i, pl.ds(first, rows)] = pieces[p][at : at + rows]
            for c in range(2):
                at = (3 * i + 1 + c) * rows
                new_b[c, 0, i, pl.ds(first, rows)] = pieces[p][at : at + rows]


def routed_by_tiles(turn, corner, bcorner, wv, joining, n, sites):
    _, slots, m, _ = corner.shape
    rows = m // n
    shape = lambda *dims: jax.ShapeDtypeStruct(dims, jnp.bfloat16)
    scratch = lambda *dims: [pltpu.VMEM(dims, jnp.bfloat16)]
    bind = functools.partial
    steps = start_order(n)
    pieces = [shape(3 * slots * rows + TILE, m)] * n
    kept = scratch(3 * slots, m, m)
    parts = small_call(bind(spread_kernel, steps, sites), pieces, [VMEM] * 4, kept, "spread")(
        turn, corner, bcorner, wv
    )
    parts = all_swapped(parts, steps, "blk")
    pieces = [shape(3 * slots * rows, m)] * n
    kept = scratch(n * slots, 3 * rows, m) + [pltpu.SMEM(joining.shape, jnp.int32), pltpu.SemaphoreType.DMA]
    parts = small_call(bind(route_kernel, steps, slots), pieces, [ANY] + [VMEM] * n, kept, "route")(
        joining, *parts
    )
    parts = all_swapped(parts, steps, "blk")
    halves = []
    for ours in (lambda k: k < sites, lambda k: k >= sites):
        some = [(k, part) for k, part in zip(steps, parts) if ours(k)]
        share = bind(share_kernel, [k for k, _ in some], sites)
        kept = scratch(sites, 2, slots, rows, m)
        late = [] if halves else [part for k, part in zip(steps, parts) if k in FIRST]
        specs = [VMEM] * sites + [ANY] * len(late)
        shares = small_call(share, [shape(2, slots, rows, m)] * sites, specs, kept, "share")(
            *[part for _, part in some], *late
        )
        halves += all_swapped(shares, SITE_STEPS, "site")
    pieces = [shape(1, slots, m, m), shape(2, 1, slots, m, m)]
    join = bind(join_kernel, steps, sites)
    new_corner, new_b = small_call(join, pieces, [VMEM] * n, [], "join")(*parts)
    summed = jax.ShapeDtypeStruct((2, slots, m // sites, m), jnp.float32)
    add = bind(sum_kernel, sites)
    summed = small_call(add, [summed], [VMEM] * (2 * sites), [], "sum")(*halves)[0]
    return new_corner, new_b, summed


def transposed(pieces):
    return lax.all_to_all(pieces, "blk", 0, 0, tiled=True)


def routed_by_rows(turn, corner, bcorner, wv, joining, n, sites):
    _, slots, m, _ = corner.shape
    rows = m // n
    wv = wv.reshape(slots, 2, m, m)
    ground, re, im = jax.vmap(lambda c, b, x: blocks_of((turn[0], turn[1]), c, b, x[0], x[1]))(
        corner[0], jnp.moveaxis(bcorner[:, 0], 0, 1), wv
    )
    peak = lax.pmax(jnp.max(jnp.abs(ground)).astype(jnp.float32), "blk")
    blocks = jnp.moveaxis(jnp.stack([ground, re, im], axis=1).reshape(slots, 3, n, rows, m), 2, 0)
    pieces = transposed(blocks).reshape(n * slots, 3, rows, m)
    scaled = (pieces[joining[0]].astype(jnp.float32) / (peak + epsilon)).astype(jnp.bfloat16)
    final = transposed(scaled.reshape(n, slots, 3, rows, m))
    new = jnp.transpose(final, (2, 1, 0, 3, 4)).reshape(3, slots, m, m)
    shares = jnp.moveaxis(new[1:].reshape(2, slots, sites, m // sites, m), 2, 0)
    shares = lax.all_to_all(shares, "site", 0, 0, tiled=True)
    return new[0][None], new[1:][:, None], jnp.sum(shares.astype(jnp.float32), axis=0)


def per_device(corner, bcorner, edge, bedge, proj, joining, momentum):
    m = corner.shape[2]
    n, sites = lax.axis_size("blk"), lax.axis_size("site")
    angle = momentum[0] * lax.axis_index("site").astype(jnp.float32)
    turn = jnp.broadcast_to(jnp.stack([jnp.cos(angle), jnp.sin(angle)])[:, None], (2, m))
    onward = [(i, (i + 1) % sites) for i in range(sites)]
    left_bcorner = lax.ppermute(bcorner, "site", onward)
    left_corner = lax.ppermute(corner, "site", onward)
    wv = edge_proj(edge, bedge, proj)
    routed = routed_by_tiles if m % (n * TILE) == 0 and (n, sites) == (8, len(SITE_STEPS)) else routed_by_rows
    return routed(turn, left_corner, left_bcorner, wv, joining, n, sites)


def solution(mesh):
    in_specs = (
        P("site", "blk", None, None),
        P(None, "site", "blk", None, None),
        P("site", "blk", None, None),
        P("site", "blk", None, None),
        P("site", "blk", None, None),
        P("site", None),
        P(),
    )
    out_specs = (
        P("site", "blk", None, None),
        P(None, "site", "blk", None, None),
        P(None, "blk", "site", None),
    )
    return jax.shard_map(
        per_device, mesh=mesh, in_specs=in_specs, out_specs=out_specs, check_vma=False
    )
```

```python
import functools

import jax
import jax.numpy as jnp
from jax import lax
from jax.experimental import pallas as pl
from jax.experimental.pallas import tpu as pltpu
from jax.sharding import PartitionSpec as P

epsilon = 1e-06
TILE = 16
SITE_STEPS = (0, 2, 3, 1)
FIRST = (6, 4, 7)
AHEAD = 2
VMEM = pl.BlockSpec(memory_space=pltpu.VMEM)
ANY = pl.BlockSpec(memory_space=pl.ANY)
HBM = pl.BlockSpec(memory_space=pltpu.HBM)


def start_order(n):
    far = sorted(range(n // 2, n), key=lambda k: (k & 1, -k))
    return (0, far[0], 1, *far[1:], *range(2, n // 2))


def my_place():
    return lax.axis_index("blk"), lax.axis_index("site")


def piece_start(j, m, n, sites):
    return pl.multiple_of(lax.rem(j, sites) * (m // sites) + lax.div(j, sites) * (m // n), m // n)


def all_swapped(parts, steps, axis):
    n = len(parts)
    return [lax.ppermute(part, axis, [(i, i ^ k) for i in range(n)]) if k else part for part, k in zip(parts, steps)]


def edge_proj_kernel(edge, bedge, proj, wv_ref, edge_buf, bedge_buf, proj_buf, sems):
    slots = proj.shape[1]
    pairs = ((proj, proj_buf), (edge, edge_buf), (bedge, bedge_buf))
    copies = [
        [pltpu.make_async_copy(src.at[0, i], buf.at[i], sems.at[3 * i + a]) for a, (src, buf) in enumerate(pairs)]
        for i in range(slots)
    ]
    for group in copies[:AHEAD]:
        for copy in group:
            copy.start()
    dot = functools.partial(jnp.dot, preferred_element_type=jnp.float32)
    for i, (first, second, third) in enumerate(copies):
        for group in copies[i + AHEAD : i + AHEAD + 1]:
            for copy in group:
                copy.start()
        first.wait()
        second.wait()
        wv_ref[2 * i] = dot(edge_buf[i], proj_buf[i]).astype(wv_ref.dtype)
        third.wait()
        wv_ref[2 * i + 1] = dot(bedge_buf[i], proj_buf[i]).astype(wv_ref.dtype)


def edge_proj(edge, bedge, proj):
    _, slots, m, k = edge.shape
    return pl.pallas_call(
        edge_proj_kernel,
        out_shape=jax.ShapeDtypeStruct((2 * slots, m, m), jnp.bfloat16),
        in_specs=[HBM] * 3,
        out_specs=VMEM,
        scratch_shapes=[
            pltpu.VMEM((slots, m, k), jnp.bfloat16),
            pltpu.VMEM((slots, m, k), jnp.bfloat16),
            pltpu.VMEM((slots, k, m), jnp.bfloat16),
            pltpu.SemaphoreType.DMA((3 * slots,)),
        ],
        cost_estimate=pl.CostEstimate(
            flops=4 * slots * m * k * m, bytes_accessed=6 * slots * m * k, transcendentals=0
        ),
        compiler_params=pltpu.CompilerParams(vmem_limit_bytes=52 << 20),
        name="edge_proj",
    )(edge, bedge, proj)


def small_call(kernel, out_shape, in_specs, scratch, name):
    return pl.pallas_call(
        kernel,
        out_shape=out_shape,
        in_specs=in_specs,
        out_specs=jax.tree.map(lambda _: VMEM, out_shape),
        scratch_shapes=scratch,
        cost_estimate=pl.CostEstimate(flops=1 << 28, bytes_accessed=1 << 20, transcendentals=0),
        compiler_params=pltpu.CompilerParams(vmem_limit_bytes=24 << 20),
        name=name,
    )


def blocks_of(turn, corner, bcorner, w, v):
    cosine, sine = turn
    dot = functools.partial(jnp.dot, preferred_element_type=jnp.float32)
    ground = dot(corner, w).astype(jnp.bfloat16)
    real_term = dot(bcorner[0], w)
    imag_term = dot(bcorner[1], w)
    re = cosine * real_term - sine * imag_term + dot(corner, v)
    im = sine * real_term + cosine * imag_term
    return ground, re.astype(jnp.bfloat16), im.astype(jnp.bfloat16)


def spread_kernel(steps, sites, turn, corner, bcorner, wv, *refs):
    n = len(steps)
    out, stage = refs[:n], refs[n]
    here = my_place()
    slots, m = corner.shape[1], corner.shape[2]
    rows = m // n
    top = jnp.zeros((m, m), jnp.float32)
    for i in range(slots):
        b_here = (bcorner[0, 0, i], bcorner[1, 0, i])
        blocks = blocks_of((turn[0:1], turn[1:2]), corner[0, i], b_here, wv[2 * i], wv[2 * i + 1])
        top = jnp.maximum(top, jnp.abs(blocks[0].astype(jnp.float32)))
        for kind in range(3):
            stage[3 * i + kind] = blocks[kind]
    peak = jnp.full((TILE, m), jnp.max(top), jnp.float32).astype(jnp.bfloat16)
    for p, k in enumerate(steps):
        first = piece_start(jnp.bitwise_xor(here[0], k), m, n, sites)
        for b in range(3 * slots):
            out[p][b * rows : (b + 1) * rows] = stage[b, pl.ds(first, rows)]
        out[p][3 * slots * rows :] = peak


def route_kernel(steps, slots, joining, *refs):
    n = len(steps)
    pieces, out, held = refs[:n], refs[n : 2 * n], refs[2 * n]
    here = my_place()
    bits = (n * slots - 1).bit_length()
    row = joining[...]
    lane = lax.broadcasted_iota(jnp.int32, row.shape, 1)

    def sources(first):
        at = lane - first
        inside = jnp.logical_and(at >= 0, at < 3)
        packed = jnp.sum(jnp.where(inside, lax.shift_left(row, bits * jnp.where(inside, at, 0)), 0))
        return [jnp.bitwise_and(lax.shift_right_logical(packed, bits * i), (1 << bits) - 1) for i in range(3)]

    owners = [jnp.bitwise_xor(here[0], k) for k in steps]
    wanted = [[q for i in range(0, slots, 3) for q in sources(t * slots + i)] for t in owners]
    size = held.shape[1]
    top = functools.reduce(jnp.maximum, [piece[slots * size :].astype(jnp.float32) for piece in pieces])
    divisor = jnp.concatenate([top] * (size // TILE), axis=0) + epsilon
    for p, k in enumerate(steps):
        d = jnp.bitwise_xor(here[0], k)
        for i in range(slots):
            piece = pieces[p][i * size : (i + 1) * size].astype(jnp.float32)
            held[d * slots + i] = (piece / divisor).astype(jnp.bfloat16)
    for p in range(n):
        for i in range(slots):
            out[p][i * size : (i + 1) * size] = held[wanted[p][i]]


def share_kernel(steps, sites, *refs):
    pieces, out, stage = refs[:sites], refs[-1 - sites : -1], refs[-1]
    here = my_place()
    _, slots, rows, _ = out[0].shape
    for p, k in enumerate(steps):
        r = lax.rem(jnp.bitwise_xor(here[0], k), sites)
        for i in range(slots):
            for c in range(2):
                at = (3 * i + 1 + c) * rows
                stage[r, c, i] = pieces[p][at : at + rows]
    for p, k in enumerate(SITE_STEPS):
        out[p][...] = stage[jnp.bitwise_xor(here[1], k)]


def sum_kernel(sites, *refs):
    near, far, summed = refs[:sites], refs[sites : 2 * sites], refs[2 * sites]
    here = my_place()
    _, slots, rows, _ = near[0].shape
    half = lax.div(here[0], sites)
    for shares, place in ((near, half), (far, 1 - half)):
        first = pl.multiple_of(place * rows, rows)
        for i in range(slots):
            for c in range(2):
                summed[c, i, pl.ds(first, rows)] = sum([share[c, i].astype(jnp.float32) for share in shares[1:]],
                                                       shares[0][c, i].astype(jnp.float32))


def join_kernel(steps, sites, *refs):
    n = len(steps)
    pieces, new_corner, new_b = refs[:n], refs[n], refs[n + 1]
    here = my_place()
    _, slots, m, _ = new_corner.shape
    rows = m // n
    for p, k in enumerate(steps):
        first = piece_start(jnp.bitwise_xor(here[0], k), m, n, sites)
        for i in range(slots):
            at = 3 * i * rows
            new_corner[0, i, pl.ds(first, rows)] = pieces[p][at : at + rows]
            for c in range(2):
                at = (3 * i + 1 + c) * rows
                new_b[c, 0, i, pl.ds(first, rows)] = pieces[p][at : at + rows]


def routed_by_tiles(turn, corner, bcorner, wv, joining, n, sites):
    _, slots, m, _ = corner.shape
    rows = m // n
    shape = lambda *dims: jax.ShapeDtypeStruct(dims, jnp.bfloat16)
    scratch = lambda *dims: [pltpu.VMEM(dims, jnp.bfloat16)]
    bind = functools.partial
    steps = start_order(n)
    pieces = [shape(3 * slots * rows + TILE, m)] * n
    kept = scratch(3 * slots, m, m)
    parts = small_call(bind(spread_kernel, steps, sites), pieces, [VMEM] * 4, kept, "spread")(
        turn, corner, bcorner, wv
    )
    parts = all_swapped(parts, steps, "blk")
    pieces = [shape(3 * slots * rows, m)] * n
    kept = scratch(n * slots, 3 * rows, m)
    parts = small_call(bind(route_kernel, steps, slots), pieces, [VMEM] * (n + 1), kept, "route")(
        joining, *parts
    )
    parts = all_swapped(parts, steps, "blk")
    halves = []
    for ours in (lambda k: k < sites, lambda k: k >= sites):
        some = [(k, part) for k, part in zip(steps, parts) if ours(k)]
        share = bind(share_kernel, [k for k, _ in some], sites)
        kept = scratch(sites, 2, slots, rows, m)
        late = [] if halves else [part for k, part in zip(steps, parts) if k in FIRST]
        specs = [VMEM] * sites + [ANY] * len(late)
        shares = small_call(share, [shape(2, slots, rows, m)] * sites, specs, kept, "share")(
            *[part for _, part in some], *late
        )
        halves += all_swapped(shares, SITE_STEPS, "site")
    pieces = [shape(1, slots, m, m), shape(2, 1, slots, m, m)]
    join = bind(join_kernel, steps, sites)
    new_corner, new_b = small_call(join, pieces, [VMEM] * n, [], "join")(*parts)
    summed = jax.ShapeDtypeStruct((2, slots, m // sites, m), jnp.float32)
    add = bind(sum_kernel, sites)
    summed = small_call(add, [summed], [VMEM] * (2 * sites), [], "sum")(*halves)[0]
    return new_corner, new_b, summed


def transposed(pieces):
    return lax.all_to_all(pieces, "blk", 0, 0, tiled=True)


def routed_by_rows(turn, corner, bcorner, wv, joining, n, sites):
    _, slots, m, _ = corner.shape
    rows = m // n
    wv = wv.reshape(slots, 2, m, m)
    ground, re, im = jax.vmap(lambda c, b, x: blocks_of((turn[0], turn[1]), c, b, x[0], x[1]))(
        corner[0], jnp.moveaxis(bcorner[:, 0], 0, 1), wv
    )
    peak = lax.pmax(jnp.max(jnp.abs(ground)).astype(jnp.float32), "blk")
    blocks = jnp.moveaxis(jnp.stack([ground, re, im], axis=1).reshape(slots, 3, n, rows, m), 2, 0)
    pieces = transposed(blocks).reshape(n * slots, 3, rows, m)
    scaled = (pieces[joining[0]].astype(jnp.float32) / (peak + epsilon)).astype(jnp.bfloat16)
    final = transposed(scaled.reshape(n, slots, 3, rows, m))
    new = jnp.transpose(final, (2, 1, 0, 3, 4)).reshape(3, slots, m, m)
    shares = jnp.moveaxis(new[1:].reshape(2, slots, sites, m // sites, m), 2, 0)
    shares = lax.all_to_all(shares, "site", 0, 0, tiled=True)
    return new[0][None], new[1:][:, None], jnp.sum(shares.astype(jnp.float32), axis=0)


def per_device(corner, bcorner, edge, bedge, proj, joining, momentum):
    m = corner.shape[2]
    n, sites = lax.axis_size("blk"), lax.axis_size("site")
    angle = momentum[0] * lax.axis_index("site").astype(jnp.float32)
    turn = jnp.broadcast_to(jnp.stack([jnp.cos(angle), jnp.sin(angle)])[:, None], (2, m))
    onward = [(i, (i + 1) % sites) for i in range(sites)]
    left_bcorner = lax.ppermute(bcorner, "site", onward)
    left_corner = lax.ppermute(corner, "site", onward)
    wv = edge_proj(edge, bedge, proj)
    routed = routed_by_tiles if m % (n * TILE) == 0 and (n, sites) == (8, len(SITE_STEPS)) else routed_by_rows
    return routed(turn, left_corner, left_bcorner, wv, joining, n, sites)


def solution(mesh):
    in_specs = (
        P("site", "blk", None, None),
        P(None, "site", "blk", None, None),
        P("site", "blk", None, None),
        P("site", "blk", None, None),
        P("site", "blk", None, None),
        P("site", None),
        P(),
    )
    out_specs = (
        P("site", "blk", None, None),
        P(None, "site", "blk", None, None),
        P(None, "blk", "site", None),
    )
    return jax.shard_map(
        per_device, mesh=mesh, in_specs=in_specs, out_specs=out_specs, check_vma=False
    )
```

```python
import functools

import jax
import jax.numpy as jnp
from jax import lax
from jax.experimental import pallas as pl
from jax.experimental.pallas import tpu as pltpu
from jax.sharding import PartitionSpec as P

epsilon = 1e-06
TILE = 16
SITE_STEPS = (0, 2, 3, 1)
FIRST = (6, 4, 7)
AHEAD = 2
VMEM = pl.BlockSpec(memory_space=pltpu.VMEM)
ANY = pl.BlockSpec(memory_space=pl.ANY)
HBM = pl.BlockSpec(memory_space=pltpu.HBM)


def start_order(n):
    far = sorted(range(n // 2, n), key=lambda k: (k & 1, -k))
    return (0, *far[:2], 1, *far[2:], *range(2, n // 2))


def my_place():
    return lax.axis_index("blk"), lax.axis_index("site")


def piece_start(j, m, n, sites):
    return pl.multiple_of(lax.rem(j, sites) * (m // sites) + lax.div(j, sites) * (m // n), m // n)


def all_swapped(parts, steps, axis):
    n = len(parts)
    return [lax.ppermute(part, axis, [(i, i ^ k) for i in range(n)]) if k else part for part, k in zip(parts, steps)]


def edge_proj_kernel(edge, bedge, proj, wv_ref, edge_buf, bedge_buf, proj_buf, sems):
    slots = proj.shape[1]
    pairs = ((proj, proj_buf), (edge, edge_buf), (bedge, bedge_buf))
    copies = [
        [pltpu.make_async_copy(src.at[0, i], buf.at[i], sems.at[3 * i + a]) for a, (src, buf) in enumerate(pairs)]
        for i in range(slots)
    ]
    for group in copies[:AHEAD]:
        for copy in group:
            copy.start()
    dot = functools.partial(jnp.dot, preferred_element_type=jnp.float32)
    for i, (first, second, third) in enumerate(copies):
        for group in copies[i + AHEAD : i + AHEAD + 1]:
            for copy in group:
                copy.start()
        first.wait()
        second.wait()
        wv_ref[2 * i] = dot(edge_buf[i], proj_buf[i]).astype(wv_ref.dtype)
        third.wait()
        wv_ref[2 * i + 1] = dot(bedge_buf[i], proj_buf[i]).astype(wv_ref.dtype)


def edge_proj(edge, bedge, proj):
    _, slots, m, k = edge.shape
    return pl.pallas_call(
        edge_proj_kernel,
        out_shape=jax.ShapeDtypeStruct((2 * slots, m, m), jnp.bfloat16),
        in_specs=[HBM] * 3,
        out_specs=VMEM,
        scratch_shapes=[
            pltpu.VMEM((slots, m, k), jnp.bfloat16),
            pltpu.VMEM((slots, m, k), jnp.bfloat16),
            pltpu.VMEM((slots, k, m), jnp.bfloat16),
            pltpu.SemaphoreType.DMA((3 * slots,)),
        ],
        cost_estimate=pl.CostEstimate(
            flops=4 * slots * m * k * m, bytes_accessed=6 * slots * m * k, transcendentals=0
        ),
        compiler_params=pltpu.CompilerParams(vmem_limit_bytes=52 << 20),
        name="edge_proj",
    )(edge, bedge, proj)


def small_call(kernel, out_shape, in_specs, scratch, name):
    return pl.pallas_call(
        kernel,
        out_shape=out_shape,
        in_specs=in_specs,
        out_specs=jax.tree.map(lambda _: VMEM, out_shape),
        scratch_shapes=scratch,
        cost_estimate=pl.CostEstimate(flops=1 << 28, bytes_accessed=1 << 20, transcendentals=0),
        compiler_params=pltpu.CompilerParams(vmem_limit_bytes=24 << 20),
        name=name,
    )


def blocks_of(turn, corner, bcorner, w, v):
    cosine, sine = turn
    dot = functools.partial(jnp.dot, preferred_element_type=jnp.float32)
    ground = dot(corner, w).astype(jnp.bfloat16)
    real_term = dot(bcorner[0], w)
    imag_term = dot(bcorner[1], w)
    re = cosine * real_term - sine * imag_term + dot(corner, v)
    im = sine * real_term + cosine * imag_term
    return ground, re.astype(jnp.bfloat16), im.astype(jnp.bfloat16)


def spread_kernel(steps, sites, turn, corner, bcorner, wv, *refs):
    n = len(steps)
    out, stage = refs[:n], refs[n]
    here = my_place()
    slots, m = corner.shape[1], corner.shape[2]
    rows = m // n
    top = jnp.zeros((m, m), jnp.float32)
    for i in range(slots):
        b_here = (bcorner[0, 0, i], bcorner[1, 0, i])
        blocks = blocks_of((turn[0:1], turn[1:2]), corner[0, i], b_here, wv[2 * i], wv[2 * i + 1])
        top = jnp.maximum(top, jnp.abs(blocks[0].astype(jnp.float32)))
        for kind in range(3):
            stage[3 * i + kind] = blocks[kind]
    peak = jnp.full((TILE, m), jnp.max(top), jnp.float32).astype(jnp.bfloat16)
    for p, k in enumerate(steps):
        first = piece_start(jnp.bitwise_xor(here[0], k), m, n, sites)
        for b in range(3 * slots):
            out[p][b * rows : (b + 1) * rows] = stage[b, pl.ds(first, rows)]
        out[p][3 * slots * rows :] = peak


def route_kernel(steps, slots, joining, *refs):
    n = len(steps)
    pieces, out, held = refs[:n], refs[n : 2 * n], refs[2 * n]
    here = my_place()
    bits = (n * slots - 1).bit_length()
    row = joining[...]
    lane = lax.broadcasted_iota(jnp.int32, row.shape, 1)

    def sources(first):
        at = lane - first
        inside = jnp.logical_and(at >= 0, at < 3)
        packed = jnp.sum(jnp.where(inside, lax.shift_left(row, bits * jnp.where(inside, at, 0)), 0))
        return [jnp.bitwise_and(lax.shift_right_logical(packed, bits * i), (1 << bits) - 1) for i in range(3)]

    owners = [jnp.bitwise_xor(here[0], k) for k in steps]
    wanted = [[q for i in range(0, slots, 3) for q in sources(t * slots + i)] for t in owners]
    size = held.shape[1]
    top = functools.reduce(jnp.maximum, [piece[slots * size :].astype(jnp.float32) for piece in pieces])
    divisor = jnp.concatenate([top] * (size // TILE), axis=0) + epsilon
    for p, k in enumerate(steps):
        d = jnp.bitwise_xor(here[0], k)
        for i in range(slots):
            piece = pieces[p][i * size : (i + 1) * size].astype(jnp.float32)
            held[d * slots + i] = (piece / divisor).astype(jnp.bfloat16)
    for p in range(n):
        for i in range(slots):
            out[p][i * size : (i + 1) * size] = held[wanted[p][i]]


def share_kernel(steps, sites, *refs):
    pieces, out, stage = refs[:sites], refs[-1 - sites : -1], refs[-1]
    here = my_place()
    _, slots, rows, _ = out[0].shape
    for p, k in enumerate(steps):
        r = lax.rem(jnp.bitwise_xor(here[0], k), sites)
        for i in range(slots):
            for c in range(2):
                at = (3 * i + 1 + c) * rows
                stage[r, c, i] = pieces[p][at : at + rows]
    for p, k in enumerate(SITE_STEPS):
        out[p][...] = stage[jnp.bitwise_xor(here[1], k)]


def sum_kernel(sites, *refs):
    near, far, summed = refs[:sites], refs[sites : 2 * sites], refs[2 * sites]
    here = my_place()
    _, slots, rows, _ = near[0].shape
    half = lax.div(here[0], sites)
    for shares, place in ((near, half), (far, 1 - half)):
        first = pl.multiple_of(place * rows, rows)
        for i in range(slots):
            for c in range(2):
                summed[c, i, pl.ds(first, rows)] = sum([share[c, i].astype(jnp.float32) for share in shares[1:]],
                                                       shares[0][c, i].astype(jnp.float32))


def join_kernel(steps, sites, *refs):
    n = len(steps)
    pieces, new_corner, new_b = refs[:n], refs[n], refs[n + 1]
    here = my_place()
    _, slots, m, _ = new_corner.shape
    rows = m // n
    for p, k in enumerate(steps):
        first = piece_start(jnp.bitwise_xor(here[0], k), m, n, sites)
        for i in range(slots):
            at = 3 * i * rows
            new_corner[0, i, pl.ds(first, rows)] = pieces[p][at : at + rows]
            for c in range(2):
                at = (3 * i + 1 + c) * rows
                new_b[c, 0, i, pl.ds(first, rows)] = pieces[p][at : at + rows]


def routed_by_tiles(turn, corner, bcorner, wv, joining, n, sites):
    _, slots, m, _ = corner.shape
    rows = m // n
    shape = lambda *dims: jax.ShapeDtypeStruct(dims, jnp.bfloat16)
    scratch = lambda *dims: [pltpu.VMEM(dims, jnp.bfloat16)]
    bind = functools.partial
    steps = start_order(n)
    pieces = [shape(3 * slots * rows + TILE, m)] * n
    kept = scratch(3 * slots, m, m)
    parts = small_call(bind(spread_kernel, steps, sites), pieces, [VMEM] * 4, kept, "spread")(
        turn, corner, bcorner, wv
    )
    parts = all_swapped(parts, steps, "blk")
    pieces = [shape(3 * slots * rows, m)] * n
    kept = scratch(n * slots, 3 * rows, m)
    parts = small_call(bind(route_kernel, steps, slots), pieces, [VMEM] * (n + 1), kept, "route")(
        joining, *parts
    )
    parts = all_swapped(parts, steps, "blk")
    halves = []
    for ours in (lambda k: k < sites, lambda k: k >= sites):
        some = [(k, part) for k, part in zip(steps, parts) if ours(k)]
        share = bind(share_kernel, [k for k, _ in some], sites)
        kept = scratch(sites, 2, slots, rows, m)
        late = [] if halves else [part for k, part in zip(steps, parts) if k in FIRST]
        specs = [VMEM] * sites + [ANY] * len(late)
        shares = small_call(share, [shape(2, slots, rows, m)] * sites, specs, kept, "share")(
            *[part for _, part in some], *late
        )
        halves += all_swapped(shares, SITE_STEPS, "site")
    pieces = [shape(1, slots, m, m), shape(2, 1, slots, m, m)]
    join = bind(join_kernel, steps, sites)
    new_corner, new_b = small_call(join, pieces, [VMEM] * n, [], "join")(*parts)
    summed = jax.ShapeDtypeStruct((2, slots, m // sites, m), jnp.float32)
    add = bind(sum_kernel, sites)
    summed = small_call(add, [summed], [VMEM] * (2 * sites), [], "sum")(*halves)[0]
    return new_corner, new_b, summed


def transposed(pieces):
    return lax.all_to_all(pieces, "blk", 0, 0, tiled=True)


def routed_by_rows(turn, corner, bcorner, wv, joining, n, sites):
    _, slots, m, _ = corner.shape
    rows = m // n
    wv = wv.reshape(slots, 2, m, m)
    ground, re, im = jax.vmap(lambda c, b, x: blocks_of((turn[0], turn[1]), c, b, x[0], x[1]))(
        corner[0], jnp.moveaxis(bcorner[:, 0], 0, 1), wv
    )
    peak = lax.pmax(jnp.max(jnp.abs(ground)).astype(jnp.float32), "blk")
    blocks = jnp.moveaxis(jnp.stack([ground, re, im], axis=1).reshape(slots, 3, n, rows, m), 2, 0)
    pieces = transposed(blocks).reshape(n * slots, 3, rows, m)
    scaled = (pieces[joining[0]].astype(jnp.float32) / (peak + epsilon)).astype(jnp.bfloat16)
    final = transposed(scaled.reshape(n, slots, 3, rows, m))
    new = jnp.transpose(final, (2, 1, 0, 3, 4)).reshape(3, slots, m, m)
    shares = jnp.moveaxis(new[1:].reshape(2, slots, sites, m // sites, m), 2, 0)
    shares = lax.all_to_all(shares, "site", 0, 0, tiled=True)
    return new[0][None], new[1:][:, None], jnp.sum(shares.astype(jnp.float32), axis=0)


def per_device(corner, bcorner, edge, bedge, proj, joining, momentum):
    m = corner.shape[2]
    n, sites = lax.axis_size("blk"), lax.axis_size("site")
    angle = momentum[0] * lax.axis_index("site").astype(jnp.float32)
    turn = jnp.broadcast_to(jnp.stack([jnp.cos(angle), jnp.sin(angle)])[:, None], (2, m))
    onward = [(i, (i + 1) % sites) for i in range(sites)]
    left_bcorner = lax.ppermute(bcorner, "site", onward)
    left_corner = lax.ppermute(corner, "site", onward)
    wv = edge_proj(edge, bedge, proj)
    routed = routed_by_tiles if m % (n * TILE) == 0 and (n, sites) == (8, len(SITE_STEPS)) else routed_by_rows
    return routed(turn, left_corner, left_bcorner, wv, joining, n, sites)


def solution(mesh):
    in_specs = (
        P("site", "blk", None, None),
        P(None, "site", "blk", None, None),
        P("site", "blk", None, None),
        P("site", "blk", None, None),
        P("site", "blk", None, None),
        P("site", None),
        P(),
    )
    out_specs = (
        P("site", "blk", None, None),
        P(None, "site", "blk", None, None),
        P(None, "blk", "site", None),
    )
    return jax.shard_map(
        per_device, mesh=mesh, in_specs=in_specs, out_specs=out_specs, check_vma=False
    )
```
